32 devices in a mesh: seq: 2 (over x), fsdp: 16 (over z, y, core).
Axes of the slice: x: 2, y: 2, z: 4, core: 2. Of those that a mesh axis runs over, the one named last changes fastest.
Arguments:
- tokens: bfloat16 [16, 1024, 1536], P('fsdp', 'seq'), may hold values from -6 to 6
- lengths: int32 [16], P('fsdp'), may hold values from 513 to 1024, as said below
- routes: int32 [16, 1024, 8], P('fsdp', 'seq'), may hold values from 0 to 15, all different within a row; in each aligned block of 512 rows (0 to 511, 512 to 1023, ..., all dimensions but the last counted through in order) at most 320 rows name the same one
- route_gates: float32 [16, 1024, 8], P('fsdp', 'seq'), may hold values from 0.25 to 0.75
- cotangent: bfloat16 [16, 1024, 1536], P('fsdp', 'seq'), may hold values from -6 to 6
- norm_first: bfloat16 [1536], P('fsdp'), may hold values from 0.5 to 1.5
- attention_in: bfloat16 [1536, 2560], P('fsdp'), may hold values from -0.15625 to 0.15625
- attention_out: bfloat16 [1536, 1536], P('fsdp'), may hold values from -1.25 to 1.25
- norm_second: bfloat16 [1536], P('fsdp'), may hold values from 0.5 to 1.5
- expert_gate: bfloat16 [1536, 16, 512], P('fsdp'), may hold values from -0.15625 to 0.15625
- expert_lift: bfloat16 [1536, 16, 512], P('fsdp'), may hold values from -0.15625 to 0.15625
- expert_down: bfloat16 [1536, 16, 512], P('fsdp'), may hold values from -0.25 to 0.25
Outputs:
- block_output: bfloat16 [16, 1024, 1536], P('fsdp', 'seq')
- grad_tokens: float32 [16, 1024, 1536], P('fsdp', 'seq')
- grad_gates: float32 [16, 1024, 8], P('fsdp', 'seq')
- grad_norm_first: float32 [1536], P('fsdp')
- grad_attention_in: float32 [1536, 2560], P('fsdp')
- grad_attention_out: float32 [1536, 1536], P('fsdp')
- grad_norm_second: float32 [1536], P('fsdp')
- grad_expert_gate: float32 [1536, 16, 512], P('fsdp')
- grad_expert_lift: float32 [1536, 16, 512], P('fsdp')
- grad_expert_down: float32 [1536, 16, 512], P('fsdp')
The draws below stay inside these ranges and needn't reach their ends.
Inputs may be any that keep to these rules, and one draw needn't show every extreme that they name: `lengths`: each slot's sequence covers more than its first 512 positions; some slot is full. `routes`: each position names 8 different experts; among the 512 positions of one device no expert is named more than 320 times.
All inputs are finite; a program needn't handle non-finite values.
Results may differ from the reference program's by a relative error of at most 0.013.
Values may be sent and summed in bfloat16 or wider, within the bound.
No kernel may reach another device: no remote copies, remote signals or barrier semaphores. Data moves between devices by JAX's collectives and lax.ppermute only.
A program may use at most 448 MiB of HBM per device.

```python
import math
import jax
import jax.numpy as jnp
import numpy as np
from jax import lax

D = 1536
HEADS = 24
KV_HEADS = 8
HEAD_DIM = 64
FF = 512
EXPERTS = 16
TOP = 8
SLOT = 1024
TOK_DEV = 512
SLOTS = 16
QKV = 2560
CAP = 320


def draw_lengths(key, part):
    base_lengths = jax.random.randint(key, (SLOTS,), SLOT - TOK_DEV + 1, SLOT + 1)
    full_slot = jax.random.randint(jax.random.fold_in(key, 7), (), 0, SLOTS)
    return jnp.where(jnp.arange(SLOTS) == full_slot, SLOT, base_lengths).astype(jnp.int32)


def block_scale(stream_key, extent, shards, smallest, high):
    def one(axis_at, blocks):
        draws = jax.random.uniform(jax.random.fold_in(jax.random.fold_in(stream_key, 6), axis_at), (blocks,), jnp.float32, smallest / len(shards), high / len(shards))
        return jnp.repeat(jnp.exp(draws), extent[axis_at] // blocks).reshape((-1,) + (1,) * (len(extent) - axis_at - 1))

    level = one(*shards[0])
    for cut in shards[1:]:
        level = level * one(*cut)
    return level


def routed_block(own_key, own, number, rows, amount, top, bound, lean):
    sequence = jax.random.permutation(own_key, amount)
    heavy_load, ordinary = portions_of(amount, rows * top, bound, lean, True), portions_of(amount, rows * top, bound, lean, False)
    places = jnp.arange(amount)

    def named(sizes, offset_by):
        used = int((sizes > 0).sum())
        fixed = max(1, used // 4)
        shifted = fixed + (places - fixed + offset_by * (used - fixed)) % max(1, amount - fixed)
        return jnp.zeros((amount,), jnp.int32).at[sequence[jnp.where(places < fixed, places, shifted)]].set(jnp.asarray(sizes, jnp.int32))

    sizes = jnp.where(number % 4 == 0, named(heavy_load, number // 4), named(ordinary, number - number // 4 - 1))
    mixed = jax.random.permutation(jax.random.fold_in(own, 3), amount)
    donor, sink = mixed[0:amount // 2 * 2:2], mixed[1:amount // 2 * 2:2]
    margin = jnp.minimum(sizes[donor] - 1, bound - sizes[sink]) // 2
    margin = jnp.where((donor == sequence[0]) | (sink == sequence[0]) | (sizes[sink] == 0), 0, jnp.maximum(margin, 0))
    shifted = jax.random.randint(jax.random.fold_in(own, 4), (amount // 2,), 0, 1 << 20) % (margin + 1)
    sizes = sizes.at[donor].add(-shifted).at[sink].add(shifted)
    items = jnp.searchsorted(jnp.cumsum(sizes), jnp.arange(rows * top), side="right").astype(jnp.int32)
    listing = items.reshape(top, rows).T
    listing = listing[jax.random.permutation(jax.random.fold_in(own, 1), rows)]
    offset_by = jax.random.randint(jax.random.fold_in(own, 2), (rows, 1), 0, top)
    return jnp.take_along_axis(listing, (jnp.arange(top)[None, :] + offset_by) % top, axis=1)


def portions_of(count, total, limit, lean, full):
    portions = [(1 << 20) // math.isqrt(rank ** lean) + 1 for rank in range(1, count + 1)]
    largest = limit if full else min(limit, max(-(-total // count), total * portions[0] // sum(portions)))
    least = 1 if total - largest >= count - 1 else 0
    given, surplus = [largest] + [least] * (count - 1), total - largest - least * (count - 1)
    while surplus > 0:
        candidates = [i for i in range(1, count) if given[i] < largest] or [i for i in range(1, count) if given[i] < limit]
        mass, budget = sum([portions[i] for i in candidates]), surplus
        for i in candidates:
            addition = min(limit - given[i], max(1, budget * portions[i] // mass), surplus)
            given[i] = given[i] + addition
            surplus = surplus - addition
    return np.array(given)


def gaussian(own_key, shape, deviation, limit, cuts=(), kind=jnp.bfloat16):
    values = jax.random.normal(own_key, shape, jnp.float32) * deviation
    if len(cuts) > 0:
        values = block_scale(own_key, shape, cuts, -0.22, 0.18) * values
    return jnp.clip(values, min=-limit, max=limit).astype(kind)


def setup_inputs(seed: int = 0) -> dict:
    key_list = jax.random.split(jax.random.key(seed), 13)
    tokens = gaussian(key_list[0], (SLOTS, SLOT, D), 1.0, 6.0, ((0, 16), (1, 2)))
    lengths = draw_lengths(jax.random.fold_in(key_list[12], 71), 0)
    routes_keys = jax.random.split(jax.random.fold_in(key_list[2], 1), SLOTS * SLOT // TOK_DEV)
    routes_turns = jax.random.permutation(jax.random.fold_in(key_list[2], 3), SLOTS * SLOT // TOK_DEV)
    routes = jax.vmap(lambda own, number: routed_block(jax.random.fold_in(key_list[2], 2), own, number, TOK_DEV, EXPERTS, TOP, CAP, 1))(routes_keys, routes_turns).reshape((SLOTS, SLOT, TOP))
    route_gates = jnp.clip(0.25 + 0.5 * jax.random.uniform(key_list[3], (SLOTS, SLOT, TOP), jnp.float32) ** block_scale(key_list[3], (SLOTS, SLOT, TOP), ((0, 16), (1, 2)), -0.2, 0.2), 0.25, 0.75)
    cotangent = gaussian(key_list[4], (SLOTS, SLOT, D), 1.0, 6.0, ((0, 16), (1, 2)))
    norm_first = jnp.clip(1.0 + 0.1 * jax.random.normal(key_list[5], (D,), jnp.float32), 0.5, 1.5).astype(jnp.bfloat16)
    attention_in = gaussian(key_list[6], (D, QKV), D ** -0.5, 0.15625, ((0, 16),))
    attention_out = gaussian(key_list[7], (D, D), (max(4, 16 * D // SLOT)) ** -0.5, 1.25, ((0, 16),))
    norm_second = jnp.clip(1.0 + 0.1 * jax.random.normal(key_list[8], (D,), jnp.float32), 0.5, 1.5).astype(jnp.bfloat16)
    expert_gate = gaussian(key_list[9], (D, EXPERTS, FF), D ** -0.5, 0.15625, ((0, 16),))
    expert_lift = gaussian(key_list[10], (D, EXPERTS, FF), D ** -0.5, 0.15625, ((0, 16),))
    expert_down = gaussian(key_list[11], (D, EXPERTS, FF), FF ** -0.5, 0.25, ((0, 16),))
    return dict(tokens=tokens, lengths=lengths, routes=routes, route_gates=route_gates, cotangent=cotangent, norm_first=norm_first, attention_in=attention_in, attention_out=attention_out, norm_second=norm_second, expert_gate=expert_gate, expert_lift=expert_lift, expert_down=expert_down)


EPS = 1e-06

@jax.custom_vjp
def low(v):
    return lax.optimization_barrier(v.astype(jnp.bfloat16)).astype(jnp.float32)

@jax.custom_vjp
def low_back(v):
    return v

def low_keep(v):
    return (low(v), None)

def low_pass(kept, grad):
    return (grad,)

def back_keep(v):
    return (v, None)

def back_low(kept, grad):
    return (low(grad),)
low.defvjp(low_keep, low_pass)
low_back.defvjp(back_keep, back_low)

def highest(form, left, right):
    return jnp.einsum(form, left, right, precision=lax.Precision.HIGHEST, preferred_element_type=jnp.float32)

def rms_scale(values, gain_vector):
    inverse = lax.rsqrt(lax.optimization_barrier(jnp.mean(values * values, axis=-1, keepdims=True)) + EPS)
    return values * inverse * gain_vector

def slot_layer(params, slot_tokens, length, slot_routes, slot_gates):
    norm_one, project_in, project_out, norm_two, gate_weight, lift_weight, down_weight = params
    length_all = slot_tokens.shape[0]
    group_size = HEADS // KV_HEADS
    query_width = HEADS * HEAD_DIM
    key_width = KV_HEADS * HEAD_DIM
    normed_one = low(rms_scale(slot_tokens, norm_one))
    projected = highest('td,dq->tq', normed_one, project_in)
    queries = low_back(low(projected[:, :query_width])).reshape(length_all, KV_HEADS, group_size, HEAD_DIM)
    keys = low_back(low(projected[:, query_width:query_width + key_width])).reshape(length_all, KV_HEADS, HEAD_DIM)
    values = low_back(low(projected[:, query_width + key_width:])).reshape(length_all, KV_HEADS, HEAD_DIM)
    scores = low_back(highest('qgrd,kgd->grqk', queries, keys) * HEAD_DIM ** (-0.5))
    positions = jnp.arange(length_all, dtype=jnp.int32)
    allowed = (positions[None, :] <= positions[:, None]) & (positions[None, :] < length)
    scores = jnp.where(allowed, scores, -jnp.inf)
    row_peak = lax.optimization_barrier(jnp.max(scores, axis=-1, keepdims=True))
    lifted = jnp.exp(scores - row_peak)
    shares = low(lifted / lax.optimization_barrier(jnp.sum(lifted, axis=-1, keepdims=True)))
    attended = highest('grqk,kgd->qgrd', shares, values).reshape(length_all, query_width)
    attended = low_back(low(attended))
    branch = low_back(highest('tq,qd->td', attended, project_out))
    middle = slot_tokens + branch
    normed_two = low(rms_scale(middle, norm_two))
    valid = (positions < length).astype(jnp.float32)
    chosen = (slot_routes[:, :, None] == jnp.arange(EXPERTS, dtype=jnp.int32)[None, None, :]).astype(jnp.float32)
    combine = highest('tk,tke->te', slot_gates, chosen) * valid[:, None]
    gate_act = low_back(highest('td,def->tef', normed_two, gate_weight))
    lift_act = low_back(highest('td,def->tef', normed_two, lift_weight))
    hidden = low(jax.nn.silu(gate_act) * lift_act)
    expert_result = low_back(highest('tef,def->ted', hidden, down_weight))
    return middle + highest('te,ted->td', combine, expert_result)

def reference(tokens, lengths, routes, route_gates, cotangent, norm_first, attention_in, attention_out, norm_second, expert_gate, expert_lift, expert_down):
    params = tuple((weight.astype(jnp.float32) for weight in (norm_first, attention_in, attention_out, norm_second, expert_gate, expert_lift, expert_down)))
    slot_step = jax.checkpoint(slot_layer)

    def forward(inputs, gate_values, weights):

        def scan_step(scan_carry, slot_item):
            slot_tokens, length, slot_routes, slot_gates = slot_item
            return (scan_carry, slot_step(weights, slot_tokens, length, slot_routes, slot_gates))
        _, outputs = lax.scan(scan_step, jnp.zeros((), jnp.float32), (inputs, lengths, routes, gate_values))
        return outputs
    outputs, pullback = jax.vjp(forward, tokens.astype(jnp.float32), route_gates, params)
    grad_tokens, grad_gates, grad_params = pullback(cotangent.astype(jnp.float32))
    return (outputs.astype(jnp.bfloat16), grad_tokens, grad_gates, grad_params[0], grad_params[1], grad_params[2], grad_params[3], grad_params[4], grad_params[5], grad_params[6])
```

```python
import functools

import jax
import jax.numpy as jnp
from jax import lax
from jax.experimental import pallas as pl
from jax.experimental.pallas import tpu as pltpu
from jax.sharding import PartitionSpec as P

HEADS = 24
KV_HEADS = 8
HEAD_DIM = 64
EXPERTS = 16
GROUP = HEADS // KV_HEADS
EPS = 1e-06
BF = jnp.bfloat16
F32 = jnp.float32
ROWS = ("outer", "inner")
VMEM_LIMIT = 60 * 1024 * 1024


def norm_rows(values, gain_vector):
    inverse = lax.rsqrt(jnp.mean(values * values, axis=-1, keepdims=True) + EPS)
    normed = values * inverse
    return (normed, inverse, (normed * gain_vector).astype(BF))


def norm_back(upstream, normed, inverse, gain_vector):
    scaled = upstream * gain_vector
    spread = jnp.mean(scaled * normed, axis=-1, keepdims=True)
    return (inverse * (scaled - normed * spread), jnp.sum(upstream * normed, axis=0))


def swap(x, axis, bit):
    return lax.ppermute(x, axis, [(i, i ^ bit) for i in range(lax.axis_size(axis))])


def core_swap(x):
    return swap(x, "inner", 1)


def side_swap(x):
    return swap(x, "inner", 2)


def seq_swap(x):
    return swap(x, "seq", 1)


def layer_gather(block):
    half = block.shape[0] // 2
    across = seq_swap(block)
    beside = side_swap(block)
    sibling = core_swap(block)
    far_top = seq_swap(beside[:half])
    far_low = side_swap(across[half:])
    far = jnp.concatenate([far_top, far_low], axis=0)
    return [
        (block, sibling),
        (across, core_swap(across)),
        (beside, core_swap(beside)),
        (far, core_swap(far)),
    ]


def layer_scatter(own, across, beside, far):
    def plus(a, b):
        return (a.astype(F32) + b.astype(F32)).astype(BF)

    far_sum = plus(far[0], core_swap(far[1]))
    across_sum = plus(across[0], core_swap(across[1]))
    beside_sum = plus(beside[0], core_swap(beside[1]))
    half = far_sum.shape[0] // 2
    top = seq_swap(far_sum[:half])
    low = side_swap(far_sum[half:])
    beside_in = side_swap(jnp.concatenate([plus(beside_sum[:half], top), beside_sum[half:]]))
    across_in = seq_swap(jnp.concatenate([across_sum[:half], plus(across_sum[half:], low)]))
    own_sum = own[0].astype(F32) + core_swap(own[1]).astype(F32)
    return own_sum + across_in.astype(F32) + beside_in.astype(F32)


def dot_nt(a, b):
    return lax.dot_general(a, b, (((1,), (1,)), ((), ())), preferred_element_type=F32)


def dot_nn(a, b):
    return lax.dot_general(a, b, (((1,), (0,)), ((), ())), preferred_element_type=F32)


def dot_tn(a, b):
    return lax.dot_general(a, b, (((0,), (0,)), ((), ())), preferred_element_type=F32)


def attend_kernel(place_ref, q_ref, k_ref, v_ref, kr_ref, vr_ref, mixed_ref, stat_ref, bias_ref, col_ref):
    count = q_ref.shape[0]
    half = count // 2
    seq_at = place_ref[0]
    live = place_ref[1]

    @pl.when(pl.program_id(0) == 0)
    def _():
        row = lax.broadcasted_iota(jnp.int32, (count, count), 0)
        col = lax.broadcasted_iota(jnp.int32, (count, count), 1)
        bias_ref[...] = jnp.where((col <= row) & (col < live), 0.0, -jnp.inf)
        col_ref[...] = jnp.zeros_like(col_ref)

    def run(with_past):
        for g in range(2):
            lanes = slice(g * HEAD_DIM, (g + 1) * HEAD_DIM)
            key = k_ref[:, lanes]
            value = v_ref[:, lanes]
            if with_past:
                key_past = kr_ref[:, lanes]
                value_past = vr_ref[:, lanes]
            for r in range(GROUP):
                h = g * GROUP + r
                for part in range(2):
                    rows = slice(part * half, (part + 1) * half)
                    span = (part + 1) * half
                    query = q_ref[rows, h * HEAD_DIM : (h + 1) * HEAD_DIM] * BF(HEAD_DIM**-0.5)
                    scores = dot_nt(query, key[:span]) + bias_ref[rows, :span]
                    peak = jnp.max(scores, axis=-1, keepdims=True)
                    if with_past:
                        past = dot_nt(query, key_past)
                        peak = jnp.maximum(peak, jnp.max(past, axis=-1, keepdims=True))
                    lifted = jnp.exp(scores - peak)
                    total = jnp.sum(lifted, axis=-1, keepdims=True)
                    mixed = dot_nn(lifted.astype(BF), value[:span])
                    if with_past:
                        lifted_past = jnp.exp(past - peak)
                        total = total + jnp.sum(lifted_past, axis=-1, keepdims=True)
                        mixed = mixed + dot_nn(lifted_past.astype(BF), value_past)
                    mixed_ref[rows, h * HEAD_DIM : (h + 1) * HEAD_DIM] = (mixed / total).astype(BF)
                    col_ref[rows, h : h + 1] = peak + jnp.log(total)

    @pl.when(seq_at == 0)
    def _():
        run(False)

    @pl.when(seq_at != 0)
    def _():
        run(True)

    stat_ref[...] = col_ref[...].T[:8, :]


def attend(place, projected, past):
    count = projected.shape[0]
    steps = KV_HEADS // 2
    wide = 2 * GROUP * HEAD_DIM
    first_key = HEADS * HEAD_DIM // 128
    first_value = first_key + KV_HEADS * HEAD_DIM // 128
    return pl.pallas_call(
        attend_kernel,
        grid_spec=pltpu.PrefetchScalarGridSpec(
            num_scalar_prefetch=1,
            grid=(steps,),
            in_specs=[
                pl.BlockSpec((count, wide), lambda j, place: (0, j)),
                pl.BlockSpec((count, 128), lambda j, place: (0, first_key + j)),
                pl.BlockSpec((count, 128), lambda j, place: (0, first_value + j)),
                pl.BlockSpec((count, 128), lambda j, place: (0, j)),
                pl.BlockSpec((count, 128), lambda j, place: (0, steps + j)),
            ],
            out_specs=[
                pl.BlockSpec((count, wide), lambda j, place: (0, j)),
                pl.BlockSpec((None, 8, count), lambda j, place: (j, 0, 0)),
            ],
            scratch_shapes=[pltpu.VMEM((count, count), F32), pltpu.VMEM((count, 128), F32)],
        ),
        out_shape=[
            jax.ShapeDtypeStruct((count, HEADS * HEAD_DIM), BF),
            jax.ShapeDtypeStruct((steps, 8, count), F32),
        ],
        compiler_params=pltpu.CompilerParams(vmem_limit_bytes=VMEM_LIMIT),
        cost_estimate=pl.CostEstimate(flops=30_000_000_000, bytes_accessed=5_000_000, transcendentals=0),
        name="attend",
    )(place, projected, projected, projected, past, past)


def attend_back_kernel(
    place_ref, q_ref, k_ref, v_ref, kr_ref, vr_ref, mixed_ref, grad_ref, stat_ref,
    dq_ref, dk_ref, dv_ref, dkr_ref, dvr_ref, bias_ref,
):
    count = q_ref.shape[0]
    half = count // 2
    seq_at = place_ref[0]
    live = place_ref[1]
    scale = HEAD_DIM**-0.5

    @pl.when(pl.program_id(0) == 0)
    def _():
        key_at = lax.broadcasted_iota(jnp.int32, (count, count), 0)
        query_at = lax.broadcasted_iota(jnp.int32, (count, count), 1)
        bias_ref[...] = jnp.where((key_at <= query_at) & (key_at < live), 0.0, -jnp.inf)

    def run(with_past):
        for g in range(2):
            lanes = slice(g * HEAD_DIM, (g + 1) * HEAD_DIM)
            key = k_ref[:, lanes]
            value = v_ref[:, lanes]
            sums = [[jnp.zeros((half, HEAD_DIM), F32) for _ in range(2)] for _ in range(2)]
            if with_past:
                key_past = kr_ref[:, lanes]
                value_past = vr_ref[:, lanes]
                past_sums = [jnp.zeros((count, HEAD_DIM), F32) for _ in range(2)]
            for r in range(GROUP):
                h = g * GROUP + r
                cols = slice(h * HEAD_DIM, (h + 1) * HEAD_DIM)
                query = q_ref[:, cols] * BF(scale)
                grad = grad_ref[:, cols]
                product = grad.astype(F32) * mixed_ref[:, cols].astype(F32)
                delta = lax.dot_general(
                    jnp.ones((8, HEAD_DIM), F32), product, (((1,), (1,)), ((), ())),
                    precision=lax.Precision.HIGHEST, preferred_element_type=F32,
                )[:1]
                stat = stat_ref[h : h + 1, :]

                def piece(keys, values, queries, grads, stats, deltas, bias):
                    scores = dot_nt(keys, queries)
                    if bias is not None:
                        scores = scores + bias
                    chances = jnp.exp(scores - stats)
                    chance_grad = dot_nt(values, grads)
                    score_grad = (chances * (chance_grad - deltas)).astype(BF)
                    return chances.astype(BF), score_grad

                p0, s0 = piece(key[:half], value[:half], query, grad, stat, delta, bias_ref[:half, :])
                p1, s1 = piece(
                    key[half:], value[half:], query[half:], grad[half:], stat[:, half:], delta[:, half:],
                    bias_ref[half:, half:],
                )
                dq = dot_tn(s0, key[:half])
                dq_late = dot_tn(s1, key[half:])
                sums[0][0] += dot_nn(s0, query)
                sums[0][1] += dot_nn(s1, query[half:])
                sums[1][0] += dot_nn(p0, grad)
                sums[1][1] += dot_nn(p1, grad[half:])
                if with_past:
                    pp, sp = piece(key_past, value_past, query, grad, stat, delta, None)
                    dq = dq + dot_tn(sp, key_past)
                    past_sums[0] += dot_nn(sp, query)
                    past_sums[1] += dot_nn(pp, grad)
                dq_ref[:half, cols] = (dq[:half] * scale).astype(BF)
                dq_ref[half:, cols] = ((dq[half:] + dq_late) * scale).astype(BF)
            for where, out in ((0, dk_ref), (1, dv_ref)):
                out[:half, lanes] = sums[where][0].astype(BF)
                out[half:, lanes] = sums[where][1].astype(BF)
            if with_past:
                dkr_ref[:, lanes] = past_sums[0].astype(BF)
                dvr_ref[:, lanes] = past_sums[1].astype(BF)

    @pl.when(seq_at == 0)
    def _():
        run(False)
        dkr_ref[...] = jnp.zeros_like(dkr_ref)
        dvr_ref[...] = jnp.zeros_like(dvr_ref)

    @pl.when(seq_at != 0)
    def _():
        run(True)


def attend_back(place, projected, past, mixed, mixed_grad, stats):
    count = projected.shape[0]
    steps = KV_HEADS // 2
    wide = 2 * GROUP * HEAD_DIM
    first_key = HEADS * HEAD_DIM // 128
    first_value = first_key + KV_HEADS * HEAD_DIM // 128
    narrow = jax.ShapeDtypeStruct((count, KV_HEADS * HEAD_DIM), BF)
    head_spec = pl.BlockSpec((count, wide), lambda j, place: (0, j))
    pair_spec = pl.BlockSpec((count, 128), lambda j, place: (0, j))
    return pl.pallas_call(
        attend_back_kernel,
        grid_spec=pltpu.PrefetchScalarGridSpec(
            num_scalar_prefetch=1,
            grid=(steps,),
            in_specs=[
                head_spec,
                pl.BlockSpec((count, 128), lambda j, place: (0, first_key + j)),
                pl.BlockSpec((count, 128), lambda j, place: (0, first_value + j)),
                pair_spec,
                pl.BlockSpec((count, 128), lambda j, place: (0, steps + j)),
                head_spec,
                head_spec,
                pl.BlockSpec((None, 8, count), lambda j, place: (j, 0, 0)),
            ],
            out_specs=[head_spec, pair_spec, pair_spec, pair_spec, pair_spec],
            scratch_shapes=[pltpu.VMEM((count, count), F32)],
        ),
        out_shape=[jax.ShapeDtypeStruct((count, HEADS * HEAD_DIM), BF), narrow, narrow, narrow, narrow],
        compiler_params=pltpu.CompilerParams(vmem_limit_bytes=VMEM_LIMIT),
        cost_estimate=pl.CostEstimate(flops=60_000_000_000, bytes_accessed=10_000_000, transcendentals=0),
        name="attend_back",
    )(place, projected, projected, projected, past, past, mixed, mixed_grad, stats)


def expert_kernel(
    n_ref, c_ref, w_ref, wg_ref, wl_ref, wd_ref, ch_ref, gg_ref, lg_ref, out_ref, back_ref, dot_ref
):
    ff = wg_ref.shape[1] // 2
    rows = n_ref[...]
    up = c_ref[...]
    gate = dot_nn(rows, wg_ref[...])
    lift = dot_nn(rows, wl_ref[...])
    push = dot_nn(up, wd_ref[...])
    for e in range(2):
        cols = slice(e * ff, (e + 1) * ff)
        weight = w_ref[:, e : e + 1]
        g, l, u = gate[:, cols], lift[:, cols], push[:, cols]
        sig = 1.0 / (1.0 + jnp.exp(-g))
        silu = g * sig
        hidden = silu * l
        hidden = hidden.astype(BF).astype(F32)
        dot_ref[:, e : e + 1] = jnp.sum(hidden * u, axis=-1, keepdims=True)
        grad = u * weight
        ch_ref[:, cols] = (hidden * weight).astype(BF)
        gg_ref[:, cols] = (grad * l * sig * (1.0 + g * (1.0 - sig))).astype(BF)
        lg_ref[:, cols] = (grad * silu).astype(BF)
    out_ref[...] = dot_nt(ch_ref[...], wd_ref[...]).astype(BF)
    back_ref[...] = (dot_nt(gg_ref[...], wg_ref[...]) + dot_nt(lg_ref[...], wl_ref[...])).astype(BF)


def expert_rows(rows, up, weight, gate, lift, down):
    count, width = rows.shape
    ff = gate.shape[1]
    tile = 256
    row_spec = pl.BlockSpec((tile, width), lambda i: (i, 0))
    ff_spec = pl.BlockSpec((tile, ff), lambda i: (i, 0))
    lane_spec = pl.BlockSpec((tile, 2), lambda i: (i, 0))
    weight_spec = pl.BlockSpec((width, ff), lambda i: (0, 0), pipeline_mode=pl.Buffered(1))
    mid = jax.ShapeDtypeStruct((count, ff), BF)
    wide = jax.ShapeDtypeStruct((count, width), BF)
    return pl.pallas_call(
        expert_kernel,
        grid=(count // tile,),
        in_specs=[row_spec, row_spec, lane_spec, weight_spec, weight_spec, weight_spec],
        out_specs=[ff_spec, ff_spec, ff_spec, row_spec, row_spec, lane_spec],
        out_shape=[mid, mid, mid, wide, wide, jax.ShapeDtypeStruct((count, 2), F32)],
        compiler_params=pltpu.CompilerParams(vmem_limit_bytes=VMEM_LIMIT),
        cost_estimate=pl.CostEstimate(
            flops=12 * count * width * ff, bytes_accessed=count * (8 * width + 6 * ff), transcendentals=0
        ),
        name="expert_rows",
    )(rows, up, weight, gate, lift, down)


def body(
    tokens,
    lengths,
    routes,
    route_gates,
    cotangent,
    norm_first,
    attention_in,
    attention_out,
    norm_second,
    expert_gate,
    expert_lift,
    expert_down,
):
    count = tokens.shape[1]
    width = tokens.shape[2]
    choose = routes.shape[2]
    seq_count = lax.axis_size("seq")
    inner_count = lax.axis_size("inner")
    owners = seq_count * inner_count
    per_owner = EXPERTS // owners
    ff = expert_gate.shape[2]
    query_width = HEADS * HEAD_DIM
    seq_at = lax.axis_index("seq")
    layer_at = seq_at * inner_count + lax.axis_index("inner")
    length = lengths[0]
    place = jnp.stack([seq_at.astype(jnp.int32), length - seq_at.astype(jnp.int32) * count])
    live_rows = seq_at * count + jnp.arange(count, dtype=jnp.int32) < length
    inputs = tokens[0].astype(F32)
    upstream_low = cotangent[0]
    upstream = upstream_low.astype(F32)

    shard = width // (lax.axis_size("outer") * inner_count)
    gains = jnp.concatenate(
        [norm_first[:, None], norm_second[:, None], jnp.zeros((shard, 126), BF)], axis=1
    )
    project_in = lax.all_gather(
        jnp.concatenate([attention_in, gains], axis=1), ROWS, axis=0, tiled=True
    )
    project_out = lax.all_gather(attention_out, ROWS, axis=0, tiled=True)
    qkv = attention_in.shape[1]
    first_gain = project_in[:, qkv].astype(F32)
    second_gain = project_in[:, qkv + 1].astype(F32)
    project_in = project_in[:, :qkv]

    def fetch(weight):
        mine = lax.dynamic_slice_in_dim(
            weight, seq_at * (inner_count * per_owner), inner_count * per_owner, 1
        ).reshape(shard, inner_count, per_owner * ff).transpose(1, 0, 2)
        local = lax.all_to_all(mine, "inner", split_axis=0, concat_axis=0, tiled=True)
        local = local.reshape(inner_count * shard, per_owner * ff)
        return lax.all_gather(local, "outer", axis=0, tiled=True)

    gate_two, lift_two, down_two = fetch(expert_gate), fetch(expert_lift), fetch(expert_down)

    route_rows = routes[0]
    gate_rows = route_gates[0]
    chosen = (
        route_rows.T[:, None, :] == jnp.arange(EXPERTS, dtype=jnp.int32)[None, :, None]
    ) & live_rows[None, None, :]
    combine = jnp.sum(jnp.where(chosen, gate_rows.T[:, None, :], 0.0), axis=0)
    combine = lax.all_to_all(
        combine.reshape(owners, per_owner, count), ("seq", "inner"), split_axis=0, concat_axis=0, tiled=True
    )
    combine = combine.transpose(0, 2, 1)

    def partner(at):
        return layer_at ^ at

    chips = (0, inner_count, 2, inner_count + 2)
    weights = [
        jnp.concatenate([combine[partner(chip)], combine[partner(chip + 1)]], axis=0) for chip in chips
    ]
    up_rows = [jnp.concatenate(pair, axis=0) for pair in layer_gather(upstream_low)]

    normed_one, inverse_one, lowered_one = norm_rows(inputs, first_gain)
    projected = jnp.dot(lowered_one, project_in, preferred_element_type=F32).astype(BF)
    past = lax.ppermute(projected[:, query_width:], "seq", [(0, 1)])
    mixed, stats = attend(place, projected, past)
    middle = inputs + jnp.dot(mixed, project_out, preferred_element_type=F32)
    normed_two, inverse_two, lowered_two = norm_rows(middle, second_gain)

    row_pairs = [jnp.concatenate(pair, axis=0) for pair in layer_gather(lowered_two)]
    made = [
        expert_rows(rows, up, weight, gate_two, lift_two, down_two)
        for rows, up, weight in zip(row_pairs, up_rows, weights)
    ]

    def pairs(at):
        return [(part[at][:count], part[at][count:]) for part in made]

    normed_grad_two = layer_scatter(*pairs(4))
    combined = layer_scatter(*pairs(3))
    block_output = (middle + combined).astype(BF)[None]
    dots = jnp.zeros((owners, count, per_owner), F32)
    for chip, part in zip(chips, made):
        dots = dots.at[partner(chip)].set(part[5][:count]).at[partner(chip + 1)].set(part[5][count:])
    dots = lax.all_to_all(
        dots.transpose(0, 2, 1), ("seq", "inner"), split_axis=0, concat_axis=0, tiled=True
    ).reshape(EXPERTS, count)
    grad_gates = jnp.sum(jnp.where(chosen, dots[None], 0.0), axis=1).T[None]

    all_rows = jnp.concatenate(row_pairs, axis=0)
    all_up = jnp.concatenate(up_rows, axis=0)
    mids = [jnp.concatenate([part[at] for part in made], axis=0) for at in range(3)]

    def give_back(left, right):
        total = lax.dot_general(left, right, (((0,), (0,)), ((), ())), preferred_element_type=F32).astype(BF)
        local = lax.psum_scatter(total, "outer", scatter_dimension=0, tiled=True)
        local = local.reshape(inner_count, shard, per_owner * ff)
        mine = lax.all_to_all(local, "inner", split_axis=0, concat_axis=0, tiled=True)
        mine = mine.reshape(inner_count, shard, per_owner, ff)
        other = seq_swap(mine)
        both = jnp.where(seq_at == 0, jnp.stack([mine, other]), jnp.stack([other, mine]))
        return both.transpose(2, 0, 1, 3, 4).reshape(shard, EXPERTS, ff).astype(F32)

    grad_gate = give_back(all_rows, mids[1])
    grad_lift = give_back(all_rows, mids[2])
    grad_down = give_back(all_up, mids[0])

    middle_norm_grad, second_gain_grad = norm_back(normed_grad_two, normed_two, inverse_two, second_gain)
    middle_grad = upstream + middle_norm_grad
    branch_grad = middle_grad.astype(BF)
    mixed_grad = dot_nt(branch_grad, project_out).astype(BF)
    out_weight_grad = dot_tn(mixed, branch_grad)
    query_grad, key_grad, value_grad, key_past, value_past = attend_back(
        place, projected, past, mixed, mixed_grad, stats
    )
    late = lax.ppermute(jnp.concatenate([key_past, value_past], axis=1), "seq", [(1, 0)])
    pair_grad = jnp.concatenate([key_grad, value_grad], axis=1)
    pair_grad = (pair_grad.astype(F32) + late.astype(F32)).astype(BF)
    projected_grad = jnp.concatenate([query_grad, pair_grad], axis=1)
    normed_grad_one = dot_nt(projected_grad, project_in)
    in_weight_grad = dot_tn(lowered_one, projected_grad)
    input_norm_grad, first_gain_grad = norm_back(normed_grad_one, normed_one, inverse_one, first_gain)
    grad_tokens = (middle_grad + input_norm_grad)[None]

    def home(total):
        part = lax.psum_scatter(total.astype(BF), ROWS, scatter_dimension=0, tiled=True)
        return part.astype(F32) + seq_swap(part).astype(F32)

    gain_grads = jnp.concatenate(
        [first_gain_grad[:, None], second_gain_grad[:, None], jnp.zeros((width, 126), F32)], axis=1
    )
    in_part = home(jnp.concatenate([in_weight_grad, gain_grads], axis=1))
    out_part = home(out_weight_grad)
    return (
        block_output,
        grad_tokens,
        grad_gates,
        in_part[:, qkv],
        in_part[:, :qkv],
        out_part,
        in_part[:, qkv + 1],
        grad_gate,
        grad_lift,
        grad_down,
    )


def solution(mesh):
    seq_count, fsdp_count = mesh.devices.shape
    inner_count = EXPERTS // (2 * seq_count)
    fine = jax.sharding.Mesh(
        mesh.devices.reshape(seq_count, fsdp_count // inner_count, inner_count), ("seq", "outer", "inner")
    )
    return jax.shard_map(
        body,
        mesh=fine,
        in_specs=(
            P(ROWS, "seq", None),
            P(ROWS),
            P(ROWS, "seq", None),
            P(ROWS, "seq", None),
            P(ROWS, "seq", None),
            P(ROWS),
            P(ROWS, None),
            P(ROWS, None),
            P(ROWS),
            P(ROWS, None, None),
            P(ROWS, None, None),
            P(ROWS, None, None),
        ),
        out_specs=(
            P(ROWS, "seq", None),
            P(ROWS, "seq", None),
            P(ROWS, "seq", None),
            P(ROWS),
            P(ROWS, None),
            P(ROWS, None),
            P(ROWS),
            P(ROWS, None, None),
            P(ROWS, None, None),
            P(ROWS, None, None),
        ),
        check_vma=False,
    )
```

```python
import functools

import jax
import jax.numpy as jnp
from jax import lax
from jax.experimental import pallas as pl
from jax.experimental.pallas import tpu as pltpu
from jax.sharding import PartitionSpec as P

HEADS = 24
KV_HEADS = 8
HEAD_DIM = 64
EXPERTS = 16
GROUP = HEADS // KV_HEADS
EPS = 1e-06
BF = jnp.bfloat16
F32 = jnp.float32
ROWS = ("outer", "inner")
VMEM_LIMIT = 60 * 1024 * 1024


def cost(microseconds):
    return pl.CostEstimate(flops=int(microseconds * 0.6e9), bytes_accessed=1000, transcendentals=0)


def norm_rows(values, gain_vector):
    inverse = lax.rsqrt(jnp.mean(values * values, axis=-1, keepdims=True) + EPS)
    normed = values * inverse
    return (normed, inverse, (normed * gain_vector).astype(BF))


def norm_back(upstream, normed, inverse, gain_vector):
    scaled = upstream * gain_vector
    spread = jnp.mean(scaled * normed, axis=-1, keepdims=True)
    return (inverse * (scaled - normed * spread), jnp.sum(upstream * normed, axis=0))


def swap(x, axis, bit):
    return lax.ppermute(x, axis, [(i, i ^ bit) for i in range(lax.axis_size(axis))])


def core_swap(x):
    return swap(x, "inner", 1)


def side_swap(x):
    return swap(x, "inner", 2)


def seq_swap(x):
    return swap(x, "seq", 1)


def after(x, *others):
    return lax.optimization_barrier((x, others))[0]


def low_plus(a, b):
    return (a.astype(F32) + b.astype(F32)).astype(BF)


def exchange_start(pieces):
    at = lax.axis_index("inner")
    bits = range(1, lax.axis_size("inner"))
    return [swap(lax.dynamic_index_in_dim(pieces, at ^ bit, 0, keepdims=False), "inner", bit) for bit in bits]


def exchange_end(pieces, got):
    at = lax.axis_index("inner")
    for bit, piece in enumerate(got, 1):
        pieces = lax.dynamic_update_index_in_dim(pieces, piece, at ^ bit, 0)
    return pieces


def pick(x, at, axis):
    return lax.dynamic_index_in_dim(x, at, axis, keepdims=False)


class HomeSum:
    def __init__(self, *totals):
        rows, columns = totals[0].shape[0], sum(total.shape[1] for total in totals)
        self.n = lax.axis_size("outer")
        self.seq_at = lax.axis_index("seq")
        self.outer_at = lax.axis_index("outer")
        inner_at = lax.axis_index("inner")
        sides = lax.axis_size("inner") // 2
        self.side_at, core_at = inner_at // 2, inner_at % 2
        self.half = columns // 2
        self.split = False
        part = rows // (self.n * sides * 2)

        def half_of(at):
            return jnp.concatenate(
                [pick(total.reshape(self.n, sides, 2, part, total.shape[1]), at, 2) for total in totals], axis=-1
            )

        self.held = half_of(core_at)
        self.got = core_swap(half_of(1 - core_at))

    def beside(self):
        held = low_plus(self.held, self.got)
        self.got = side_swap(pick(held, 1 - self.side_at, 1))
        self.held = pick(held, self.side_at, 1)
        return held

    def across(self):
        held = low_plus(self.held, self.got)
        self.got = seq_swap(lax.dynamic_slice_in_dim(held, (1 - self.seq_at) * self.half, self.half, 2))
        self.held = lax.dynamic_slice_in_dim(held, self.seq_at * self.half, self.half, 2)
        self.split = True
        return held

    def along(self):
        held = low_plus(self.held, self.got)
        self.held = pick(held, self.outer_at, 0)
        self.got = []
        for step in range(1, self.n):
            piece = pick(held, lax.rem(self.outer_at + step, self.n), 0)
            self.got.append(lax.ppermute(piece, "outer", [(i, (i + step) % self.n) for i in range(self.n)]))
        return held

    def final(self):
        result = self.held.astype(F32)
        for got in self.got:
            result = result + got.astype(F32)
        self.low = result.astype(BF)
        self.other = seq_swap(self.low)
        return self.low

    def result(self):
        low, other = self.low.astype(F32), self.other.astype(F32)
        if not self.split:
            return low + other
        first = self.seq_at == 0
        return jnp.concatenate([jnp.where(first, low, other), jnp.where(first, other, low)], axis=1)


class Chain:
    def __init__(self, last):
        self.last = last

    def enter(self, x):
        return after(x, self.last)

    def leave(self, y):
        self.last = y
        return y


def dot_nt(a, b):
    return lax.dot_general(a, b, (((1,), (1,)), ((), ())), preferred_element_type=F32)


def dot_nn(a, b):
    return lax.dot_general(a, b, (((1,), (0,)), ((), ())), preferred_element_type=F32)


def dot_tn(a, b):
    return lax.dot_general(a, b, (((0,), (0,)), ((), ())), preferred_element_type=F32)


def project_in_kernel(token_ref, weight_ref, tail_ref, query_ref, pair_ref, low_ref, gain_ref):
    step = pl.program_id(0)
    queries = HEADS * HEAD_DIM // weight_ref.shape[1]

    @pl.when(step == 0)
    def _():
        row = lax.broadcasted_iota(jnp.int32, (8, 128), 0)
        lane = lax.broadcasted_iota(jnp.int32, (8, 128), 1)
        gain_ref[...] = dot_nt((row == lane).astype(BF), tail_ref[...])
        x = token_ref[...].astype(F32)
        inverse = lax.rsqrt(jnp.mean(x * x, axis=-1, keepdims=True) + EPS)
        low_ref[...] = (x * inverse * gain_ref[0:1, :]).astype(BF)

    result = dot_nn(low_ref[...], weight_ref[...]).astype(BF)

    @pl.when(step < queries)
    def _():
        query_ref[...] = result

    @pl.when(step >= queries)
    def _():
        pair_ref[...] = result


def project_rows(tokens, weight, qkv):
    count, width = tokens.shape
    tile = 512
    query_width = HEADS * HEAD_DIM
    queries = query_width // tile
    return pl.pallas_call(
        project_in_kernel,
        grid=(qkv // tile,),
        in_specs=[
            pl.BlockSpec((count, width), lambda j: (0, 0)),
            pl.BlockSpec((width, tile), lambda j: (0, j)),
            pl.BlockSpec((width, 128), lambda j: (0, qkv // 128)),
        ],
        out_specs=[
            pl.BlockSpec((count, tile), lambda j: (0, jnp.minimum(j, queries - 1))),
            pl.BlockSpec((count, tile), lambda j: (0, jnp.maximum(j - queries, 0))),
            pl.BlockSpec((count, width), lambda j: (0, 0)),
            pl.BlockSpec((8, width), lambda j: (0, 0)),
        ],
        out_shape=[
            jax.ShapeDtypeStruct((count, query_width), BF),
            jax.ShapeDtypeStruct((count, qkv - query_width), BF),
            jax.ShapeDtypeStruct((count, width), BF),
            jax.ShapeDtypeStruct((8, width), F32),
        ],
        compiler_params=pltpu.CompilerParams(vmem_limit_bytes=VMEM_LIMIT),
        cost_estimate=cost(0),
        name="project_rows",
    )(tokens, weight, weight)


def merge_kernel(mixed_ref, weight_ref, token_ref, gain_ref, middle_ref, low_ref):
    product = dot_nn(mixed_ref[...], weight_ref[...])
    step = pl.program_id(0)

    @pl.when(step == 0)
    def _():
        middle_ref[...] = token_ref[...].astype(F32) + product

    @pl.when(step > 0)
    def _():
        middle_ref[...] += product

    @pl.when(step == pl.num_programs(0) - 1)
    def _():
        x = middle_ref[...]
        inverse = lax.rsqrt(jnp.mean(x * x, axis=-1, keepdims=True) + EPS)
        low_ref[...] = (x * inverse * gain_ref[1:2, :]).astype(BF)


def merge_rows(mixed, weight, tokens, gains):
    count, width = tokens.shape
    tile = 512
    whole = pl.BlockSpec((count, width), lambda j: (0, 0))
    return pl.pallas_call(
        merge_kernel,
        grid=(mixed.shape[1] // tile,),
        in_specs=[
            pl.BlockSpec((count, tile), lambda j: (0, j)),
            pl.BlockSpec((tile, width), lambda j: (j, 0)),
            whole,
            pl.BlockSpec((8, width), lambda j: (0, 0)),
        ],
        out_specs=[whole, whole],
        out_shape=[jax.ShapeDtypeStruct((count, width), F32), jax.ShapeDtypeStruct((count, width), BF)],
        compiler_params=pltpu.CompilerParams(vmem_limit_bytes=VMEM_LIMIT),
        cost_estimate=cost(0),
        name="merge_rows",
    )(mixed, weight, tokens, gains)


def attend_kernel(place_ref, q_ref, k_ref, v_ref, kr_ref, vr_ref, mixed_ref, stat_ref, bias_ref, col_ref):
    count = q_ref.shape[0]
    half = count // 2
    seq_at = place_ref[0]
    live = place_ref[1]

    @pl.when(pl.program_id(0) == 0)
    def _():
        row = lax.broadcasted_iota(jnp.int32, (count, count), 0)
        col = lax.broadcasted_iota(jnp.int32, (count, count), 1)
        bias_ref[...] = jnp.where((col <= row) & (col < live), 0.0, -jnp.inf)
        col_ref[...] = jnp.zeros_like(col_ref)

    def run(with_past):
        for g in range(2):
            lanes = slice(g * HEAD_DIM, (g + 1) * HEAD_DIM)
            key = k_ref[:, lanes]
            value = v_ref[:, lanes]
            if with_past:
                key_past = kr_ref[:, lanes]
                value_past = vr_ref[:, lanes]
            for r in range(GROUP):
                h = g * GROUP + r
                for part in range(2):
                    rows = slice(part * half, (part + 1) * half)
                    span = (part + 1) * half
                    query = q_ref[rows, h * HEAD_DIM : (h + 1) * HEAD_DIM] * BF(HEAD_DIM**-0.5)
                    scores = dot_nt(query, key[:span]) + bias_ref[rows, :span]
                    peak = jnp.max(scores, axis=-1, keepdims=True)
                    if with_past:
                        past = dot_nt(query, key_past)
                        peak = jnp.maximum(peak, jnp.max(past, axis=-1, keepdims=True))
                    lifted = jnp.exp(scores - peak)
                    total = jnp.sum(lifted, axis=-1, keepdims=True)
                    mixed = dot_nn(lifted.astype(BF), value[:span])
                    if with_past:
                        lifted_past = jnp.exp(past - peak)
                        total = total + jnp.sum(lifted_past, axis=-1, keepdims=True)
                        mixed = mixed + dot_nn(lifted_past.astype(BF), value_past)
                    mixed_ref[rows, h * HEAD_DIM : (h + 1) * HEAD_DIM] = (mixed / total).astype(BF)
                    col_ref[rows, h : h + 1] = peak + jnp.log(total)

    @pl.when(seq_at == 0)
    def _():
        run(False)

    @pl.when(seq_at != 0)
    def _():
        run(True)

    stat_ref[...] = col_ref[...].T[:8, :]


def attend(place, query, pair, past):
    count = query.shape[0]
    steps = KV_HEADS // 2
    wide = 2 * GROUP * HEAD_DIM
    return pl.pallas_call(
        attend_kernel,
        grid_spec=pltpu.PrefetchScalarGridSpec(
            num_scalar_prefetch=1,
            grid=(steps,),
            in_specs=[
                pl.BlockSpec((count, wide), lambda j, place: (0, j)),
                pl.BlockSpec((count, 128), lambda j, place: (0, j)),
                pl.BlockSpec((count, 128), lambda j, place: (0, steps + j)),
                pl.BlockSpec((count, 128), lambda j, place: (0, j)),
                pl.BlockSpec((count, 128), lambda j, place: (0, steps + j)),
            ],
            out_specs=[
                pl.BlockSpec((count, wide), lambda j, place: (0, j)),
                pl.BlockSpec((None, 8, count), lambda j, place: (j, 0, 0)),
            ],
            scratch_shapes=[pltpu.VMEM((count, count), F32), pltpu.VMEM((count, 128), F32)],
        ),
        out_shape=[
            jax.ShapeDtypeStruct((count, HEADS * HEAD_DIM), BF),
            jax.ShapeDtypeStruct((steps, 8, count), F32),
        ],
        compiler_params=pltpu.CompilerParams(vmem_limit_bytes=VMEM_LIMIT),
        cost_estimate=cost(0),
        name="attend",
    )(place, query, pair, pair, past, past)


def attend_back_kernel(
    place_ref, q_ref, k_ref, v_ref, kr_ref, vr_ref, mixed_ref, grad_ref, stat_ref,
    dq_ref, dk_ref, dv_ref, dkr_ref, dvr_ref, bias_ref,
):
    count = q_ref.shape[0]
    half = count // 2
    seq_at = place_ref[0]
    live = place_ref[1]
    scale = HEAD_DIM**-0.5

    @pl.when(pl.program_id(0) == 0)
    def _():
        key_at = lax.broadcasted_iota(jnp.int32, (count, count), 0)
        query_at = lax.broadcasted_iota(jnp.int32, (count, count), 1)
        bias_ref[...] = jnp.where((key_at <= query_at) & (key_at < live), 0.0, -jnp.inf)

    def run(with_past):
        for g in range(2):
            lanes = slice(g * HEAD_DIM, (g + 1) * HEAD_DIM)
            key = k_ref[:, lanes]
            value = v_ref[:, lanes]
            sums = [[jnp.zeros((half, HEAD_DIM), F32) for _ in range(2)] for _ in range(2)]
            if with_past:
                key_past = kr_ref[:, lanes]
                value_past = vr_ref[:, lanes]
                past_sums = [jnp.zeros((count, HEAD_DIM), F32) for _ in range(2)]
            for r in range(GROUP):
                h = g * GROUP + r
                cols = slice(h * HEAD_DIM, (h + 1) * HEAD_DIM)
                query = q_ref[:, cols] * BF(scale)
                grad = grad_ref[:, cols]
                product = grad.astype(F32) * mixed_ref[:, cols].astype(F32)
                delta = lax.dot_general(
                    jnp.ones((8, HEAD_DIM), F32), product, (((1,), (1,)), ((), ())),
                    precision=lax.Precision.HIGHEST, preferred_element_type=F32,
                )[:1]
                stat = stat_ref[h : h + 1, :]

                def piece(keys, values, queries, grads, stats, deltas, bias):
                    scores = dot_nt(keys, queries)
                    if bias is not None:
                        scores = scores + bias
                    chances = jnp.exp(scores - stats)
                    chance_grad = dot_nt(values, grads)
                    score_grad = (chances * (chance_grad - deltas)).astype(BF)
                    return chances.astype(BF), score_grad

                p0, s0 = piece(key[:half], value[:half], query, grad, stat, delta, bias_ref[:half, :])
                p1, s1 = piece(
                    key[half:], value[half:], query[half:], grad[half:], stat[:, half:], delta[:, half:],
                    bias_ref[half:, half:],
                )
                dq = dot_tn(s0, key[:half])
                dq_late = dot_tn(s1, key[half:])
                sums[0][0] += dot_nn(s0, query)
                sums[0][1] += dot_nn(s1, query[half:])
                sums[1][0] += dot_nn(p0, grad)
                sums[1][1] += dot_nn(p1, grad[half:])
                if with_past:
                    pp, sp = piece(key_past, value_past, query, grad, stat, delta, None)
                    dq = dq + dot_tn(sp, key_past)
                    past_sums[0] += dot_nn(sp, query)
                    past_sums[1] += dot_nn(pp, grad)
                dq_ref[:half, cols] = (dq[:half] * scale).astype(BF)
                dq_ref[half:, cols] = ((dq[half:] + dq_late) * scale).astype(BF)
            for where, out in ((0, dk_ref), (1, dv_ref)):
                out[:half, lanes] = sums[where][0].astype(BF)
                out[half:, lanes] = sums[where][1].astype(BF)
            if with_past:
                dkr_ref[:, lanes] = past_sums[0].astype(BF)
                dvr_ref[:, lanes] = past_sums[1].astype(BF)

    @pl.when(seq_at == 0)
    def _():
        run(False)
        dkr_ref[...] = jnp.zeros_like(dkr_ref)
        dvr_ref[...] = jnp.zeros_like(dvr_ref)

    @pl.when(seq_at != 0)
    def _():
        run(True)


def attend_back(place, query, pair, past, mixed, mixed_grad, stats, first, steps, us):
    count = query.shape[0]
    pairs = KV_HEADS // 2
    wide = 2 * GROUP * HEAD_DIM
    narrow = jax.ShapeDtypeStruct((count, steps * 128), BF)
    head_spec = pl.BlockSpec((count, wide), lambda j, place: (0, first + j))
    pair_spec = pl.BlockSpec((count, 128), lambda j, place: (0, j))
    return pl.pallas_call(
        attend_back_kernel,
        grid_spec=pltpu.PrefetchScalarGridSpec(
            num_scalar_prefetch=1,
            grid=(steps,),
            in_specs=[
                head_spec,
                pl.BlockSpec((count, 128), lambda j, place: (0, first + j)),
                pl.BlockSpec((count, 128), lambda j, place: (0, pairs + first + j)),
                pl.BlockSpec((count, 128), lambda j, place: (0, first + j)),
                pl.BlockSpec((count, 128), lambda j, place: (0, pairs + first + j)),
                head_spec,
                head_spec,
                pl.BlockSpec((None, 8, count), lambda j, place: (first + j, 0, 0)),
            ],
            out_specs=[pl.BlockSpec((count, wide), lambda j, place: (0, j))] + [pair_spec] * 4,
            scratch_shapes=[pltpu.VMEM((count, count), F32)],
        ),
        out_shape=[jax.ShapeDtypeStruct((count, steps * wide), BF), narrow, narrow, narrow, narrow],
        compiler_params=pltpu.CompilerParams(vmem_limit_bytes=VMEM_LIMIT),
        cost_estimate=cost(us),
        name="attend_back",
    )(place, query, pair, pair, past, past, mixed, mixed_grad, stats)


def pack_kernel(seq_ref, gate_ref, lift_ref, down_ref, *out_refs):
    owners, _, columns = out_refs[0].shape
    ff = columns // 3
    for seq in range(2):

        @pl.when(seq_ref[0] == seq)
        def _():
            for kind, ref in enumerate((gate_ref, lift_ref, down_ref)):
                for owner in range(owners):
                    for e in range(2):
                        out_refs[e][owner, :, kind * ff : (kind + 1) * ff] = ref[:, (seq * owners + owner) * 2 + e, :]


def pack_experts(seq, gate, lift, down, owners):
    rows, experts, ff = gate.shape
    tile = 32 if rows % 32 == 0 else rows
    in_spec = pl.BlockSpec((tile, experts, ff), lambda i, seq: (i, 0, 0))
    out_spec = pl.BlockSpec((owners, tile, 3 * ff), lambda i, seq: (0, i, 0))
    out = jax.ShapeDtypeStruct((owners, rows, 3 * ff), BF)
    return pl.pallas_call(
        pack_kernel,
        grid_spec=pltpu.PrefetchScalarGridSpec(
            num_scalar_prefetch=1, grid=(rows // tile,), in_specs=[in_spec] * 3, out_specs=[out_spec] * 2
        ),
        out_shape=[out, out],
        compiler_params=pltpu.CompilerParams(vmem_limit_bytes=VMEM_LIMIT),
        cost_estimate=cost(6),
        name="pack_experts",
    )(seq, gate, lift, down)


def unpack_kernel(seq_ref, *refs):
    out_ref = refs[-1]
    owners = refs[0].shape[0]
    for seq in range(2):

        @pl.when(seq_ref[0] == seq)
        def _():
            for e in range(2):
                for at, ref in ((seq, refs[2 * e]), (1 - seq, refs[2 * e + 1])):
                    for owner in range(owners):
                        out_ref[:, (at * owners + owner) * 2 + e, :] = ref[owner].astype(F32)


def unpack_experts(seq, parts, column, ff):
    owners, rows, _ = parts[0].shape
    in_spec = pl.BlockSpec((owners, rows, ff), lambda i, seq: (0, 0, column))
    return pl.pallas_call(
        unpack_kernel,
        grid_spec=pltpu.PrefetchScalarGridSpec(
            num_scalar_prefetch=1,
            grid=(1,),
            in_specs=[in_spec] * 4,
            out_specs=pl.BlockSpec((rows, EXPERTS, ff), lambda i, seq: (0, 0, 0)),
        ),
        out_shape=jax.ShapeDtypeStruct((rows, EXPERTS, ff), F32),
        compiler_params=pltpu.CompilerParams(vmem_limit_bytes=VMEM_LIMIT),
        cost_estimate=cost(4),
        name="unpack_experts",
    )(seq, *parts)


def expert_kernel(e, has_earlier, n, place_ref, *refs):
    na_ref, nb_ref, ca_ref, cb_ref = refs[:4]
    earlier_refs = refs[4:8] if has_earlier else (None,) * 4
    begin = 8 if has_earlier else 4
    block_refs = refs[begin : begin + n]
    (ch_ref, gl_ref, outa_ref, outb_ref, backa_ref, backb_ref) = refs[-8:-2]
    wt_ref, sems = refs[-2:]
    part = block_refs[0].shape[0]
    width = na_ref.shape[1]
    ff = wt_ref.shape[1] // 3
    step_at = pl.program_id(0)
    fresh = step_at == 0
    first = step_at < 2
    mine = 2 * place_ref[0] + e
    at = place_ref[1]

    def piece(step, kind):
        slot = lax.rem(at + n - step, n) if n > 1 else 0
        rows = pl.ds(pl.multiple_of(slot * part, part), part) if n > 1 else slice(None)
        cols = slice(kind * ff, (kind + 1) * ff)
        return pltpu.make_async_copy(block_refs[step].at[:, cols], wt_ref.at[rows, cols], sems.at[kind * n + step])

    @pl.when(fresh)
    def _():
        for kind in range(3):
            for step in range(n):
                piece(step, kind).start()

    def run(n_ref, c_ref, earlier_out, earlier_back, out_ref, back_ref, is_first):
        def arrived(kind):
            if is_first:

                @pl.when(fresh)
                def _():
                    for step in range(n):
                        piece(step, kind).wait()

        packed = c_ref[:, width:].astype(F32)
        lane = lax.broadcasted_iota(jnp.int32, packed.shape, 1)
        arrived(0)
        g = dot_nn(n_ref[...], wt_ref[:, :ff])
        arrived(1)
        l = dot_nn(n_ref[...], wt_ref[:, ff : 2 * ff])
        arrived(2)
        u = dot_nn(c_ref[:, :width], wt_ref[:, 2 * ff :])
        own_lane = (lane == mine) | (lane == EXPERTS + mine)
        weight = jnp.sum(jnp.where(own_lane, packed, 0.0), axis=-1, keepdims=True)
        sig = 1.0 / (1.0 + jnp.exp(-g))
        silu = g * sig
        hidden = silu * l
        dot = jnp.sum(hidden * u, axis=-1, keepdims=True)
        dot_high = dot.astype(BF).astype(F32)
        dots = jnp.where(lane == mine, dot_high, 0.0)
        dots = jnp.where(lane == EXPERTS + mine, dot - dot_high, dots)
        grad = u * weight
        ch_ref[...] = (hidden * weight).astype(BF)
        gl_ref[:, :ff] = (grad * l * (sig + silu * (1.0 - sig))).astype(BF)
        gl_ref[:, ff:] = (grad * silu).astype(BF)
        back = dot_nt(gl_ref[...], wt_ref[:, : 2 * ff])
        out = dot_nt(ch_ref[...], wt_ref[:, 2 * ff :])
        if has_earlier:
            out = out + earlier_out[:, :width].astype(F32)
            dots = dots + earlier_out[:, width:].astype(F32)
            back = back + earlier_back[...].astype(F32)
        back_ref[...] = back.astype(BF)
        out_ref[:, :width] = out.astype(BF)
        out_ref[:, width:] = dots.astype(BF)

    @pl.when(first)
    def _():
        run(na_ref, ca_ref, earlier_refs[0], earlier_refs[2], outa_ref, backa_ref, True)

    @pl.when(jnp.logical_not(first))
    def _():
        run(nb_ref, cb_ref, earlier_refs[1], earlier_refs[3], outb_ref, backb_ref, False)


def expert_rows(place, e, rows, up, blocks, chunk, chunks, held, earlier, us):
    count, width = rows[0].shape
    ff = blocks[0].shape[1] // 3
    tile = count // 2
    more = width + 128

    def early(i, place):
        return (jnp.minimum(i, 1), 0)

    def late(i, place):
        return (jnp.maximum(i - 2, 0), 0)

    def at_rows(i, place):
        return (4 * chunk + i, 0)

    any_spec = pl.BlockSpec(memory_space=pl.ANY)
    wide_specs = [pl.BlockSpec((tile, width), early), pl.BlockSpec((tile, width), late)]
    more_specs = [pl.BlockSpec((tile, more), early), pl.BlockSpec((tile, more), late)]
    total = 2 * count * chunks
    one = jax.ShapeDtypeStruct((count, width), BF)
    one_more = jax.ShapeDtypeStruct((count, more), BF)
    held, earlier = list(held), list(earlier)
    begin = 5 + len(earlier) + len(blocks)
    return pl.pallas_call(
        functools.partial(expert_kernel, e, len(earlier) > 0, len(blocks)),
        grid_spec=pltpu.PrefetchScalarGridSpec(
            num_scalar_prefetch=1,
            grid=(4,),
            in_specs=wide_specs
            + more_specs
            + (more_specs + wide_specs if earlier else [])
            + [any_spec] * (len(blocks) + len(held)),
            out_specs=[pl.BlockSpec((tile, ff), at_rows), pl.BlockSpec((tile, 2 * ff), at_rows)]
            + more_specs
            + wide_specs,
            scratch_shapes=[pltpu.VMEM((width, 3 * ff), BF), pltpu.SemaphoreType.DMA((3 * len(blocks),))],
        ),
        out_shape=[jax.ShapeDtypeStruct((total, ff), BF), jax.ShapeDtypeStruct((total, 2 * ff), BF)]
        + [one_more] * 2
        + [one] * 2,
        input_output_aliases={begin + at: at for at in range(len(held))},
        compiler_params=pltpu.CompilerParams(vmem_limit_bytes=VMEM_LIMIT),
        cost_estimate=cost(us),
        name="expert_rows",
    )(place, *rows, *up, *earlier, *blocks, *held)


def expert_grad_kernel(*refs):
    right_ref, out_ref, sum_ref, held_ref, sems = refs[-5:]
    sources = refs[:-5]
    width = held_ref.shape[2]
    step = pl.program_id(0)

    def fetch(at):
        return pltpu.make_async_copy(sources[at].at[:, :width], held_ref.at[at % 2], sems.at[at % 2])

    @pl.when(step == 0)
    def _():
        fetch(0).start()

    for at in range(len(sources)):

        @pl.when(step == at)
        def _():
            if at + 1 < len(sources):
                fetch(at + 1).start()
            fetch(at).wait()
            product = dot_tn(held_ref[at % 2], right_ref[...])
            if at == 0:
                sum_ref[...] = product
            elif at + 1 < len(sources):
                sum_ref[...] += product
            else:
                out_ref[...] = (sum_ref[...] + product).astype(BF)


def expert_grad(lefts, right, width, us):
    count = lefts[0].shape[0]
    columns = right.shape[1]
    return pl.pallas_call(
        expert_grad_kernel,
        grid=(len(lefts),),
        in_specs=[pl.BlockSpec(memory_space=pl.ANY)] * len(lefts) + [pl.BlockSpec((count, columns), lambda i: (i, 0))],
        out_specs=pl.BlockSpec((width, columns), lambda i: (0, 0)),
        out_shape=jax.ShapeDtypeStruct((width, columns), BF),
        scratch_shapes=[
            pltpu.VMEM((width, columns), F32),
            pltpu.VMEM((2, count, width), BF),
            pltpu.SemaphoreType.DMA((2,)),
        ],
        compiler_params=pltpu.CompilerParams(vmem_limit_bytes=VMEM_LIMIT),
        cost_estimate=cost(us),
        name="expert_grad",
    )(*lefts, right)


def body(
    tokens,
    lengths,
    routes,
    route_gates,
    cotangent,
    norm_first,
    attention_in,
    attention_out,
    norm_second,
    expert_gate,
    expert_lift,
    expert_down,
):
    count = tokens.shape[1]
    width = tokens.shape[2]
    choose = routes.shape[2]
    seq_count = lax.axis_size("seq")
    inner_count = lax.axis_size("inner")
    owners = seq_count * inner_count
    per_owner = EXPERTS // owners
    ff = expert_gate.shape[2]
    query_width = HEADS * HEAD_DIM
    seq_at = lax.axis_index("seq")
    layer_at = seq_at * inner_count + lax.axis_index("inner")
    length = lengths[0]
    place = jnp.stack([seq_at.astype(jnp.int32), length - seq_at.astype(jnp.int32) * count])
    live_rows = seq_at * count + jnp.arange(count, dtype=jnp.int32) < length
    inputs = tokens[0].astype(F32)
    upstream_low = cotangent[0]
    upstream = upstream_low.astype(F32)

    outer_count = lax.axis_size("outer")
    outer_at = lax.axis_index("outer")
    shard = width // (outer_count * inner_count)
    qkv = attention_in.shape[1]
    gains = jnp.concatenate([norm_first[:, None], norm_second[:, None], jnp.zeros((shard, 126), BF)], axis=1)
    project_in = lax.all_gather(jnp.concatenate([attention_in, gains], axis=1), ROWS, axis=0, tiled=True)
    project_out = lax.all_gather(attention_out, ROWS, axis=0, tiled=True)

    seq_place = seq_at.astype(jnp.int32)[None]
    expert_place = jnp.stack([layer_at.astype(jnp.int32), outer_at.astype(jnp.int32)])
    packed = pack_experts(seq_place, expert_gate, expert_lift, expert_down, inner_count)
    got = [exchange_start(part) for part in packed]
    packed = [exchange_end(*pair).reshape(inner_count * shard, 3 * ff) for pair in zip(packed, got)]
    if outer_count == 4:
        blocks_a = [packed[0]] + [
            lax.ppermute(packed[0], "outer", [(i, (i + step) % outer_count) for i in range(outer_count)])
            for step in range(1, outer_count)
        ]
    else:
        blocks_a = [lax.all_gather(packed[0], "outer", axis=0, tiled=True)]
    blocks = (blocks_a, [lax.all_gather(after(packed[1], project_out[:8, :128]), "outer", axis=0, tiled=True)])

    chosen = (
        routes[0][:, :, None] == jnp.arange(EXPERTS, dtype=jnp.int32)[None, None, :]
    ) & live_rows[:, None, None]
    combine = jnp.sum(jnp.where(chosen, route_gates[0][:, :, None], 0.0), axis=1)
    combine_high = combine.astype(BF)
    combine_low = (combine - combine_high.astype(F32)).astype(BF)
    up_block = jnp.concatenate(
        [upstream_low, combine_high, combine_low, jnp.zeros((count, 128 - 2 * EXPERTS), BF)], axis=1
    )
    half = count // 2
    up_block = after(up_block, packed)
    up_across, up_beside, up_sibling = seq_swap(up_block), side_swap(up_block), core_swap(up_block)

    query, pair, lowered_one, gains = project_rows(tokens[0], project_in, qkv)
    past = lax.ppermute(pair, "seq", [(0, 1)])
    past, up_across, up_beside = lax.optimization_barrier((past, up_across, up_beside))
    up_far_top, up_far_low = seq_swap(up_beside[:half]), side_swap(up_across[half:])
    mixed, stats = attend(place, query, pair, past)
    mixed, up_far_top, up_far_low = lax.optimization_barrier((mixed, up_far_top, up_far_low))
    up_pair_across = (up_across, core_swap(up_across))
    up_pair_beside = (up_beside, core_swap(up_beside))
    middle, lowered_two = merge_rows(mixed, project_out, tokens[0], gains)

    across, beside, sibling = seq_swap(lowered_two), side_swap(lowered_two), core_swap(lowered_two)

    def experts(e, at, rows, up, held, earlier=(), us=1):
        return expert_rows(expert_place, e, rows, up, blocks[e], at, 4, held, earlier, us)

    def upper(block, more):
        return jnp.concatenate([low_plus(block[:half], more), block[half:]])

    def lower(block, more):
        return jnp.concatenate([block[:half], low_plus(block[half:], more)])

    row_own, up_own = (lowered_two, sibling), (up_block, up_sibling)
    made_own = experts(0, 0, row_own, up_own, ())
    across, beside, held = lax.optimization_barrier((across, beside, made_own[:2]))
    far_top, far_low = seq_swap(beside[:half]), side_swap(across[half:])
    row_across = (across, core_swap(across))
    row_beside = (beside, core_swap(beside))
    made_across = experts(0, 1, row_across, up_pair_across, held)
    up_far = jnp.concatenate([up_far_top, up_far_low], axis=0)
    up_pair_far = (up_far, core_swap(up_far))
    made_beside = experts(0, 2, row_beside, up_pair_beside, made_across[:2])
    far_top, far_low, held = lax.optimization_barrier((far_top, far_low, made_beside[:2]))
    far = jnp.concatenate([far_top, far_low], axis=0)
    row_far = (far, core_swap(far))
    made_far = experts(0, 3, row_far, up_pair_far, held)
    hidden_a, grads_a = made_far[:2]

    row_all = (*row_own, *row_across, *row_beside, *row_far)
    up_all = (*up_own, *up_pair_across, *up_pair_beside, *up_pair_far)

    def home(total):
        return lax.psum_scatter(total, "outer", scatter_dimension=0, tiled=True)

    def slots(*locals_):
        local = jnp.concatenate(locals_, axis=1) if len(locals_) > 1 else locals_[0]
        return local.reshape(inner_count, shard, local.shape[1])

    total_a = expert_grad(row_all, grads_a, width, 1)
    home_a = home(total_a)
    hidden_a = after(hidden_a, total_a)
    down_a = expert_grad(up_all, hidden_a, width, 1)
    home_down_a = home(down_a)
    far_parts = after(made_far[2:], down_a)

    made_far = experts(1, 3, row_far, up_pair_far, (), far_parts)
    far_got, far_out_got = core_swap(made_far[5]), core_swap(made_far[3])
    made_across = experts(1, 1, row_across, up_pair_across, made_far[:2], made_across[2:])
    across_got, across_out_got = core_swap(made_across[5]), core_swap(made_across[3])
    far_got, held = lax.optimization_barrier((far_got, made_across[:2]))
    far_sum, held = lax.optimization_barrier((low_plus(made_far[4], far_got), held))
    back_low, back_top = side_swap(far_sum[half:]), seq_swap(far_sum[:half])
    made_beside = experts(1, 2, row_beside, up_pair_beside, held, made_beside[2:], 15)
    beside_got, beside_out_got = core_swap(made_beside[5]), core_swap(made_beside[3])
    across_got, back_low, back_top, held = lax.optimization_barrier(
        (across_got, back_low, back_top, made_beside[:2])
    )
    across_sum, held = lax.optimization_barrier((lower(low_plus(made_across[4], across_got), back_low), held))
    across_in = seq_swap(across_sum)
    made_own = experts(1, 0, row_own, up_own, held, made_own[2:], 15)
    hidden_b, grads_b = made_own[:2]
    own_got, own_out_got = core_swap(made_own[5]), core_swap(made_own[3])
    beside_got, far_out_got, grads_b = lax.optimization_barrier((beside_got, far_out_got, grads_b))
    beside_sum, grads_b = lax.optimization_barrier((upper(low_plus(made_beside[4], beside_got), back_top), grads_b))
    beside_in = side_swap(beside_sum)
    far_out = low_plus(made_far[2], far_out_got)
    out_low, out_top = side_swap(far_out[half:]), seq_swap(far_out[:half])

    total_b = expert_grad(row_all, grads_b, width, 1)
    home_b = home(total_b)
    across_in, hidden_b = lax.optimization_barrier((across_in, after(hidden_b, total_b)))
    down_b = expert_grad(up_all, hidden_b, width, 1)
    home_down_b = home(down_b)
    beside_in, own_got, out_top, out_low, across_out_got, beside_out_got, own_out_got, _ = lax.optimization_barrier(
        (beside_in, own_got, out_top, out_low, across_out_got, beside_out_got, own_out_got, down_b)
    )
    out_across = lower(low_plus(made_across[2], across_out_got), out_low)
    out_beside = upper(low_plus(made_beside[2], beside_out_got), out_top)
    normed_grad_two = (
        made_own[4].astype(F32) + own_got.astype(F32) + across_in.astype(F32) + beside_in.astype(F32)
    )

    normed_two, inverse_two, _ = norm_rows(middle, gains[1])
    middle_norm_grad, second_gain_grad = norm_back(normed_grad_two, normed_two, inverse_two, gains[1])
    middle_grad = upstream + middle_norm_grad
    branch_grad = middle_grad.astype(BF)
    mixed_grad = dot_nt(branch_grad, project_out).astype(BF)
    out_across, out_beside, mixed_grad = lax.optimization_barrier((out_across, out_beside, mixed_grad))
    out_across_in, out_beside_in = seq_swap(out_across), side_swap(out_beside)
    chain = Chain(mixed_grad)
    pairs = KV_HEADS // 2
    first_pairs = pairs // 2

    def back(first, steps):
        return attend_back(chain.enter(place), query, pair, past, mixed, mixed_grad, stats, first, steps, 24)

    query_a, key_a, value_a, key_past_a, value_past_a = chain.leave(back(0, first_pairs))
    late_a = lax.ppermute(jnp.concatenate([key_past_a, value_past_a], axis=1), "seq", [(1, 0)])
    out_weight_grad = chain.leave(dot_tn(chain.enter(mixed), branch_grad).astype(BF))
    out_across_in, out_beside_in = chain.enter((out_across_in, out_beside_in))
    combined = (
        made_own[2].astype(F32) + own_out_got.astype(F32) + out_across_in.astype(F32) + out_beside_in.astype(F32)
    )
    block_output = chain.leave((middle + combined[:, :width]).astype(BF))[None]
    dots = combined[:, width : width + EXPERTS] + combined[:, width + EXPERTS : width + 2 * EXPERTS]
    query_weight_a = chain.leave(dot_tn(chain.enter(lowered_one), query_a).astype(BF))
    early_home = HomeSum(out_weight_grad, query_weight_a)
    grad_gates = chain.leave(jnp.sum(jnp.where(chosen, chain.enter(dots)[:, None, :], 0.0), axis=-1))[None]
    early_home.got = chain.enter(early_home.got)
    late_a = chain.enter(late_a)
    chain.leave((early_home.beside(), late_a))
    a_slots = slots(chain.enter(home_a), chain.enter(home_down_a))
    a_got = exchange_start(a_slots)
    query_b, key_b, value_b, key_past_b, value_past_b = chain.leave(back(first_pairs, pairs - first_pairs))
    late_b = lax.ppermute(jnp.concatenate([key_past_b, value_past_b], axis=1), "seq", [(1, 0)])
    query_weight_b = chain.leave(dot_tn(chain.enter(lowered_one), query_b).astype(BF))
    a_mine = chain.leave(exchange_end(a_slots, chain.enter(a_got)))
    late_b = chain.enter(late_b)
    split_a, split_b = key_past_a.shape[1], key_past_b.shape[1]
    pair_own = jnp.concatenate([key_a, key_b, value_a, value_b], axis=1)
    pair_late = jnp.concatenate(
        [late_a[:, :split_a], late_b[:, :split_b], late_a[:, split_a:], late_b[:, split_b:]], axis=1
    )
    pair_grad = low_plus(pair_own, pair_late)
    pair_weight = chain.leave(dot_tn(lowered_one, pair_grad).astype(BF))
    final_total = chain.leave(jnp.concatenate([query_weight_b, pair_weight], axis=1))
    final_part = lax.psum_scatter(final_total, ROWS, scatter_dimension=0, tiled=True)
    early_home.got = chain.enter(early_home.got)
    chain.leave(early_home.across())
    projected_grad = jnp.concatenate([query_a, query_b, pair_grad], axis=1)
    normed_grad_one = chain.leave(dot_nt(chain.enter(projected_grad), project_in[:, :qkv]))
    normed_one, inverse_one, _ = norm_rows(inputs, gains[0])
    input_norm_grad, first_gain_grad = norm_back(chain.enter(normed_grad_one), normed_one, inverse_one, gains[0])
    grad_tokens = chain.leave(middle_grad + input_norm_grad)[None]
    gain_grads = jnp.stack([first_gain_grad, second_gain_grad])
    gain_grads = gain_grads + seq_swap(gain_grads)
    b_slots = slots(chain.enter(home_b), chain.enter(home_down_b))
    b_got = exchange_start(b_slots)
    gain_grads = chain.enter(gain_grads)
    gain_grads = chain.leave(gain_grads + core_swap(gain_grads))
    early_home.got = chain.enter(early_home.got)
    chain.leave(early_home.along())
    b_mine = chain.leave(exchange_end(b_slots, chain.enter(b_got)))
    a_other, b_other = seq_swap(a_mine), seq_swap(b_mine)

    gain_grads = chain.leave(gain_grads + side_swap(gain_grads))
    gain_grads = gain_grads.reshape(2, outer_count, inner_count * shard)
    gain_sum = pick(gain_grads, outer_at, 1)
    for step in range(1, outer_count):
        piece = pick(gain_grads, lax.rem(outer_at + step, outer_count), 1)
        gain_sum = gain_sum + lax.ppermute(
            piece, "outer", [(i, (i + step) % outer_count) for i in range(outer_count)]
        )
    gain_sum = pick(gain_sum.reshape(2, inner_count, shard), lax.axis_index("inner"), 1)
    early_home.got = chain.enter(early_home.got)
    chain.leave(early_home.final())
    early_home.other = chain.enter(early_home.other)
    early = early_home.result()
    grad_out = chain.leave(early[:, : mixed.shape[1]])
    parts = chain.enter((a_mine, a_other, b_mine, b_other))
    grad_gate, grad_lift, grad_down = [unpack_experts(seq_place, parts, kind, ff) for kind in range(3)]
    final_part = after(final_part, grad_gate, grad_lift, grad_down)
    final_sum = final_part.astype(F32) + seq_swap(final_part).astype(F32)
    grad_in = jnp.concatenate([early[:, mixed.shape[1] :], final_sum], axis=1)
    return (
        block_output,
        grad_tokens,
        grad_gates,
        gain_sum[0],
        grad_in,
        grad_out,
        gain_sum[1],
        grad_gate,
        grad_lift,
        grad_down,
    )


def solution(mesh):
    seq_count, fsdp_count = mesh.devices.shape
    inner_count = EXPERTS // (2 * seq_count)
    fine = jax.sharding.Mesh(
        mesh.devices.reshape(seq_count, fsdp_count // inner_count, inner_count), ("seq", "outer", "inner")
    )
    return jax.shard_map(
        body,
        mesh=fine,
        in_specs=(
            P(ROWS, "seq", None),
            P(ROWS),
            P(ROWS, "seq", None),
            P(ROWS, "seq", None),
            P(ROWS, "seq", None),
            P(ROWS),
            P(ROWS, None),
            P(ROWS, None),
            P(ROWS),
            P(ROWS, None, None),
            P(ROWS, None, None),
            P(ROWS, None, None),
        ),
        out_specs=(
            P(ROWS, "seq", None),
            P(ROWS, "seq", None),
            P(ROWS, "seq", None),
            P(ROWS),
            P(ROWS, None),
            P(ROWS, None),
            P(ROWS),
            P(ROWS, None, None),
            P(ROWS, None, None),
            P(ROWS, None, None),
        ),
        check_vma=False,
    )
```

```python
import functools

import jax
import jax.numpy as jnp
from jax import lax
from jax.experimental import pallas as pl
from jax.experimental.pallas import tpu as pltpu
from jax.sharding import PartitionSpec as P

HEADS = 24
KV_HEADS = 8
HEAD_DIM = 64
EXPERTS = 16
GROUP = HEADS // KV_HEADS
EPS = 1e-06
BF = jnp.bfloat16
F32 = jnp.float32
ROWS = ("outer", "inner")
VMEM_LIMIT = 60 * 1024 * 1024


def cost(microseconds):
    return pl.CostEstimate(flops=int(microseconds * 0.6e9), bytes_accessed=1000, transcendentals=0)


def norm_rows(values, gain_vector):
    inverse = lax.rsqrt(jnp.mean(values * values, axis=-1, keepdims=True) + EPS)
    normed = values * inverse
    return (normed, inverse, (normed * gain_vector).astype(BF))


def norm_back(upstream, normed, inverse, gain_vector):
    scaled = upstream * gain_vector
    spread = jnp.mean(scaled * normed, axis=-1, keepdims=True)
    return (inverse * (scaled - normed * spread), jnp.sum(upstream * normed, axis=0))


def swap(x, axis, bit):
    return lax.ppermute(x, axis, [(i, i ^ bit) for i in range(lax.axis_size(axis))])


def core_swap(x):
    return swap(x, "inner", 1)


def side_swap(x):
    return swap(x, "inner", 2)


def seq_swap(x):
    return swap(x, "seq", 1)


def after(x, *others):
    return lax.optimization_barrier((x, others))[0]


def low_plus(a, b):
    return (a.astype(F32) + b.astype(F32)).astype(BF)


def exchange_start(pieces):
    at = lax.axis_index("inner")
    bits = range(1, lax.axis_size("inner"))
    return [swap(lax.dynamic_index_in_dim(pieces, at ^ bit, 0, keepdims=False), "inner", bit) for bit in bits]


def exchange_end(pieces, got):
    at = lax.axis_index("inner")
    for bit, piece in enumerate(got, 1):
        pieces = lax.dynamic_update_index_in_dim(pieces, piece, at ^ bit, 0)
    return pieces


def pick(x, at, axis):
    return lax.dynamic_index_in_dim(x, at, axis, keepdims=False)


class HomeSum:
    def __init__(self, *totals):
        rows, columns = totals[0].shape[0], sum(total.shape[1] for total in totals)
        self.n = lax.axis_size("outer")
        self.seq_at = lax.axis_index("seq")
        self.outer_at = lax.axis_index("outer")
        inner_at = lax.axis_index("inner")
        sides = lax.axis_size("inner") // 2
        self.side_at, core_at = inner_at // 2, inner_at % 2
        self.half = columns // 2
        self.split = False
        part = rows // (self.n * sides * 2)

        def half_of(at):
            return jnp.concatenate(
                [pick(total.reshape(self.n, sides, 2, part, total.shape[1]), at, 2) for total in totals], axis=-1
            )

        self.held = half_of(core_at)
        self.got = core_swap(half_of(1 - core_at))

    def beside(self):
        held = low_plus(self.held, self.got)
        self.got = side_swap(pick(held, 1 - self.side_at, 1))
        self.held = pick(held, self.side_at, 1)
        return held

    def across(self):
        held = low_plus(self.held, self.got)
        self.got = seq_swap(lax.dynamic_slice_in_dim(held, (1 - self.seq_at) * self.half, self.half, 2))
        self.held = lax.dynamic_slice_in_dim(held, self.seq_at * self.half, self.half, 2)
        self.split = True
        return held

    def along(self):
        held = low_plus(self.held, self.got)
        self.held = pick(held, self.outer_at, 0)
        self.got = []
        for step in range(1, self.n):
            piece = pick(held, lax.rem(self.outer_at + step, self.n), 0)
            self.got.append(lax.ppermute(piece, "outer", [(i, (i + step) % self.n) for i in range(self.n)]))
        return held

    def final(self):
        result = self.held.astype(F32)
        for got in self.got:
            result = result + got.astype(F32)
        self.low = result.astype(BF)
        self.other = seq_swap(self.low)
        return self.low

    def result(self):
        low, other = self.low.astype(F32), self.other.astype(F32)
        if not self.split:
            return low + other
        first = self.seq_at == 0
        return jnp.concatenate([jnp.where(first, low, other), jnp.where(first, other, low)], axis=1)


class Chain:
    def __init__(self, last):
        self.last = last

    def enter(self, x):
        return after(x, self.last)

    def leave(self, y):
        self.last = y
        return y


def dot_nt(a, b):
    return lax.dot_general(a, b, (((1,), (1,)), ((), ())), preferred_element_type=F32)


def dot_nn(a, b):
    return lax.dot_general(a, b, (((1,), (0,)), ((), ())), preferred_element_type=F32)


def dot_tn(a, b):
    return lax.dot_general(a, b, (((0,), (0,)), ((), ())), preferred_element_type=F32)


def project_in_kernel(token_ref, weight_ref, tail_ref, query_ref, paira_ref, pairb_ref, low_ref, gain_ref):
    step = pl.program_id(0)
    queries = HEADS * HEAD_DIM // weight_ref.shape[1]

    @pl.when(step == 0)
    def _():
        row = lax.broadcasted_iota(jnp.int32, (8, 128), 0)
        lane = lax.broadcasted_iota(jnp.int32, (8, 128), 1)
        gain_ref[...] = dot_nt((row == lane).astype(BF), tail_ref[...])
        x = token_ref[...].astype(F32)
        inverse = lax.rsqrt(jnp.mean(x * x, axis=-1, keepdims=True) + EPS)
        low_ref[...] = (x * inverse * gain_ref[0:1, :]).astype(BF)

    result = dot_nn(low_ref[...], weight_ref[...]).astype(BF)

    @pl.when(step < queries)
    def _():
        query_ref[...] = result

    half = result.shape[1] // 2
    for part in range(2):

        @pl.when(step == queries + part)
        def _():
            cols = slice(part * half, (part + 1) * half)
            paira_ref[:, cols] = result[:, :half]
            pairb_ref[:, cols] = result[:, half:]


def project_rows(tokens, weight, qkv, before):
    count, width = tokens.shape
    tile = 512
    query_width = HEADS * HEAD_DIM
    queries = query_width // tile
    return pl.pallas_call(
        project_in_kernel,
        grid=(qkv // tile,),
        in_specs=[
            pl.BlockSpec((count, width), lambda j: (0, 0)),
            pl.BlockSpec((width, tile), lambda j: (0, before // tile + j)),
            pl.BlockSpec((width, 128), lambda j: (0, (before + qkv) // 128)),
        ],
        out_specs=[
            pl.BlockSpec((count, tile), lambda j: (0, jnp.minimum(j, queries - 1))),
            pl.BlockSpec((count, tile), lambda j: (0, 0)),
            pl.BlockSpec((count, tile), lambda j: (0, 0)),
            pl.BlockSpec((count, width), lambda j: (0, 0)),
            pl.BlockSpec((8, width), lambda j: (0, 0)),
        ],
        out_shape=[
            jax.ShapeDtypeStruct((count, query_width), BF),
            jax.ShapeDtypeStruct((count, tile), BF),
            jax.ShapeDtypeStruct((count, tile), BF),
            jax.ShapeDtypeStruct((count, width), BF),
            jax.ShapeDtypeStruct((8, width), F32),
        ],
        compiler_params=pltpu.CompilerParams(vmem_limit_bytes=VMEM_LIMIT),
        cost_estimate=cost(0),
        name="project_rows",
    )(tokens, weight, weight)


def merge_kernel(mixed_ref, weight_ref, token_ref, gain_ref, middle_ref, low_ref):
    product = dot_nn(mixed_ref[...], weight_ref[...])
    step = pl.program_id(0)

    @pl.when(step == 0)
    def _():
        middle_ref[...] = token_ref[...].astype(F32) + product

    @pl.when(step > 0)
    def _():
        middle_ref[...] += product

    @pl.when(step == pl.num_programs(0) - 1)
    def _():
        x = middle_ref[...]
        inverse = lax.rsqrt(jnp.mean(x * x, axis=-1, keepdims=True) + EPS)
        low_ref[...] = (x * inverse * gain_ref[1:2, :]).astype(BF)


def merge_rows(mixed, weight, tokens, gains):
    count, width = tokens.shape
    tile = 512
    whole = pl.BlockSpec((count, width), lambda j: (0, 0))
    return pl.pallas_call(
        merge_kernel,
        grid=(mixed.shape[1] // tile,),
        in_specs=[
            pl.BlockSpec((count, tile), lambda j: (0, j)),
            pl.BlockSpec((tile, width), lambda j: (j, 0)),
            whole,
            pl.BlockSpec((8, width), lambda j: (0, 0)),
        ],
        out_specs=[whole, whole],
        out_shape=[jax.ShapeDtypeStruct((count, width), F32), jax.ShapeDtypeStruct((count, width), BF)],
        compiler_params=pltpu.CompilerParams(vmem_limit_bytes=VMEM_LIMIT),
        cost_estimate=cost(0),
        name="merge_rows",
    )(mixed, weight, tokens, gains)


def middle_back_kernel(
    own_ref, got_ref, across_ref, beside_ref, middle_ref, up_ref, gain_ref, weight_ref,
    grad_ref, low_ref, mixed_ref, sum_ref,
):
    @pl.when(pl.program_id(0) == 0)
    def _():
        above = own_ref[...].astype(F32) + got_ref[...].astype(F32)
        above = above + across_ref[...].astype(F32) + beside_ref[...].astype(F32)
        x = middle_ref[...]
        inverse = lax.rsqrt(jnp.mean(x * x, axis=-1, keepdims=True) + EPS)
        normed = x * inverse
        scaled = above * gain_ref[1:2, :]
        spread = jnp.mean(scaled * normed, axis=-1, keepdims=True)
        grad = up_ref[...].astype(F32) + inverse * (scaled - normed * spread)
        grad_ref[...] = grad
        low_ref[...] = grad.astype(BF)
        sum_ref[...] = jnp.broadcast_to(jnp.sum(above * normed, axis=0, keepdims=True), sum_ref.shape)

    mixed_ref[...] = dot_nt(low_ref[...], weight_ref[...]).astype(BF)


def middle_back(own, got, across, beside, middle, up, gains, weight, columns):
    count, width = own.shape
    tile = 512
    whole = pl.BlockSpec((count, width), lambda j: (0, 0))
    row = pl.BlockSpec((8, width), lambda j: (0, 0))
    return pl.pallas_call(
        middle_back_kernel,
        grid=(columns // tile,),
        in_specs=[whole] * 6 + [row, pl.BlockSpec((tile, width), lambda j: (j, 0))],
        out_specs=[whole, whole, pl.BlockSpec((count, tile), lambda j: (0, j)), row],
        out_shape=[
            jax.ShapeDtypeStruct((count, width), F32),
            jax.ShapeDtypeStruct((count, width), BF),
            jax.ShapeDtypeStruct((count, columns), BF),
            jax.ShapeDtypeStruct((8, width), F32),
        ],
        compiler_params=pltpu.CompilerParams(vmem_limit_bytes=VMEM_LIMIT),
        cost_estimate=cost(1),
        name="middle_back",
    )(own, got, across, beside, middle, up, gains, weight)


def attend_kernel(place_ref, q_ref, k_ref, v_ref, kr_ref, vr_ref, *refs):
    mixed_ref, stat_ref, bias_ref, col_ref = refs[-4:]
    count = q_ref.shape[0]
    half = count // 2
    seq_at = place_ref[0]
    live = place_ref[1]

    @pl.when(pl.program_id(0) == 0)
    def _():
        row = lax.broadcasted_iota(jnp.int32, (count, count), 0)
        col = lax.broadcasted_iota(jnp.int32, (count, count), 1)
        bias_ref[...] = jnp.where((col <= row) & (col < live), 0.0, -jnp.inf)
        col_ref[...] = jnp.zeros_like(col_ref)

    def run(with_past):
        for g in range(2):
            lanes = slice(g * HEAD_DIM, (g + 1) * HEAD_DIM)
            key = k_ref[:, lanes]
            value = v_ref[:, lanes]
            if with_past:
                key_past = kr_ref[:, lanes]
                value_past = vr_ref[:, lanes]
            for r in range(GROUP):
                h = g * GROUP + r
                for part in range(2):
                    rows = slice(part * half, (part + 1) * half)
                    span = (part + 1) * half
                    query = q_ref[rows, h * HEAD_DIM : (h + 1) * HEAD_DIM] * BF(HEAD_DIM**-0.5)
                    scores = dot_nt(query, key[:span]) + bias_ref[rows, :span]
                    peak = jnp.max(scores, axis=-1, keepdims=True)
                    if with_past:
                        past = dot_nt(query, key_past)
                        peak = jnp.maximum(peak, jnp.max(past, axis=-1, keepdims=True))
                    lifted = jnp.exp(scores - peak)
                    total = jnp.sum(lifted, axis=-1, keepdims=True)
                    mixed = dot_nn(lifted.astype(BF), value[:span])
                    if with_past:
                        lifted_past = jnp.exp(past - peak)
                        total = total + jnp.sum(lifted_past, axis=-1, keepdims=True)
                        mixed = mixed + dot_nn(lifted_past.astype(BF), value_past)
                    mixed_ref[rows, h * HEAD_DIM : (h + 1) * HEAD_DIM] = (mixed / total).astype(BF)
                    col_ref[rows, h : h + 1] = peak + jnp.log(total)

    @pl.when(seq_at == 0)
    def _():
        run(False)

    @pl.when(seq_at != 0)
    def _():
        run(True)

    stat_ref[...] = col_ref[...].T[:8, :]


def attend(place, query, pair, past, first, held=()):
    count = query.shape[0]
    steps = pair.shape[1] // 256
    wide = 2 * GROUP * HEAD_DIM
    return pl.pallas_call(
        attend_kernel,
        grid_spec=pltpu.PrefetchScalarGridSpec(
            num_scalar_prefetch=1,
            grid=(steps,),
            in_specs=[
                pl.BlockSpec((count, wide), lambda j, place: (0, first + j)),
                pl.BlockSpec((count, 128), lambda j, place: (0, j)),
                pl.BlockSpec((count, 128), lambda j, place: (0, steps + j)),
                pl.BlockSpec((count, 128), lambda j, place: (0, j)),
                pl.BlockSpec((count, 128), lambda j, place: (0, steps + j)),
            ]
            + [pl.BlockSpec(memory_space=pl.ANY)] * len(held),
            out_specs=[
                pl.BlockSpec((count, wide), lambda j, place: (0, first + j)),
                pl.BlockSpec((None, 8, count), lambda j, place: (j, 0, 0)),
            ],
            scratch_shapes=[pltpu.VMEM((count, count), F32), pltpu.VMEM((count, 128), F32)],
        ),
        out_shape=[
            jax.ShapeDtypeStruct((count, HEADS * HEAD_DIM), BF),
            jax.ShapeDtypeStruct((steps, 8, count), F32),
        ],
        input_output_aliases={6: 0} if held else {},
        compiler_params=pltpu.CompilerParams(vmem_limit_bytes=VMEM_LIMIT),
        cost_estimate=cost(0),
        name="attend",
    )(place, query, pair, pair, past, past, *held)


def attend_back_kernel(
    place_ref, q_ref, k_ref, v_ref, kr_ref, vr_ref, mixed_ref, grad_ref, stat_ref,
    dq_ref, dk_ref, dv_ref, dkr_ref, dvr_ref, bias_ref,
):
    count = q_ref.shape[0]
    half = count // 2
    seq_at = place_ref[0]
    live = place_ref[1]
    scale = HEAD_DIM**-0.5

    @pl.when(pl.program_id(0) == 0)
    def _():
        key_at = lax.broadcasted_iota(jnp.int32, (count, count), 0)
        query_at = lax.broadcasted_iota(jnp.int32, (count, count), 1)
        bias_ref[...] = jnp.where((key_at <= query_at) & (key_at < live), 0.0, -jnp.inf)

    def run(with_past):
        for g in range(2):
            lanes = slice(g * HEAD_DIM, (g + 1) * HEAD_DIM)
            key = k_ref[:, lanes]
            value = v_ref[:, lanes]
            sums = [[jnp.zeros((half, HEAD_DIM), F32) for _ in range(2)] for _ in range(2)]
            if with_past:
                key_past = kr_ref[:, lanes]
                value_past = vr_ref[:, lanes]
                past_sums = [jnp.zeros((count, HEAD_DIM), F32) for _ in range(2)]
            for r in range(GROUP):
                h = g * GROUP + r
                cols = slice(h * HEAD_DIM, (h + 1) * HEAD_DIM)
                query = q_ref[:, cols] * BF(scale)
                grad = grad_ref[:, cols]
                product = grad.astype(F32) * mixed_ref[:, cols].astype(F32)
                delta = lax.dot_general(
                    jnp.ones((8, HEAD_DIM), F32), product, (((1,), (1,)), ((), ())),
                    precision=lax.Precision.HIGHEST, preferred_element_type=F32,
                )[:1]
                stat = stat_ref[h : h + 1, :]

                def piece(keys, values, queries, grads, stats, deltas, bias):
                    scores = dot_nt(keys, queries)
                    if bias is not None:
                        scores = scores + bias
                    chances = jnp.exp(scores - stats)
                    chance_grad = dot_nt(values, grads)
                    score_grad = (chances * (chance_grad - deltas)).astype(BF)
                    return chances.astype(BF), score_grad

                p0, s0 = piece(key[:half], value[:half], query, grad, stat, delta, bias_ref[:half, :])
                p1, s1 = piece(
                    key[half:], value[half:], query[half:], grad[half:], stat[:, half:], delta[:, half:],
                    bias_ref[half:, half:],
                )
                dq = dot_tn(s0, key[:half])
                dq_late = dot_tn(s1, key[half:])
                sums[0][0] += dot_nn(s0, query)
                sums[0][1] += dot_nn(s1, query[half:])
                sums[1][0] += dot_nn(p0, grad)
                sums[1][1] += dot_nn(p1, grad[half:])
                if with_past:
                    pp, sp = piece(key_past, value_past, query, grad, stat, delta, None)
                    dq = dq + dot_tn(sp, key_past)
                    past_sums[0] += dot_nn(sp, query)
                    past_sums[1] += dot_nn(pp, grad)
                dq_ref[:half, cols] = (dq[:half] * scale).astype(BF)
                dq_ref[half:, cols] = ((dq[half:] + dq_late) * scale).astype(BF)
            for where, out in ((0, dk_ref), (1, dv_ref)):
                out[:half, lanes] = sums[where][0].astype(BF)
                out[half:, lanes] = sums[where][1].astype(BF)
            if with_past:
                dkr_ref[:, lanes] = past_sums[0].astype(BF)
                dvr_ref[:, lanes] = past_sums[1].astype(BF)

    @pl.when(seq_at == 0)
    def _():
        run(False)
        dkr_ref[...] = jnp.zeros_like(dkr_ref)
        dvr_ref[...] = jnp.zeros_like(dvr_ref)

    @pl.when(seq_at != 0)
    def _():
        run(True)


def attend_back(place, query, pair, past, mixed, mixed_grad, stats, first, steps, us):
    count = query.shape[0]
    wide = 2 * GROUP * HEAD_DIM
    narrow = jax.ShapeDtypeStruct((count, steps * 128), BF)
    head_spec = pl.BlockSpec((count, wide), lambda j, place: (0, first + j))
    pair_spec = pl.BlockSpec((count, 128), lambda j, place: (0, j))
    return pl.pallas_call(
        attend_back_kernel,
        grid_spec=pltpu.PrefetchScalarGridSpec(
            num_scalar_prefetch=1,
            grid=(steps,),
            in_specs=[
                head_spec,
                pl.BlockSpec((count, 128), lambda j, place: (0, j)),
                pl.BlockSpec((count, 128), lambda j, place: (0, steps + j)),
                pl.BlockSpec((count, 128), lambda j, place: (0, j)),
                pl.BlockSpec((count, 128), lambda j, place: (0, steps + j)),
                head_spec,
                head_spec,
                pl.BlockSpec((None, 8, count), lambda j, place: (j, 0, 0)),
            ],
            out_specs=[pl.BlockSpec((count, wide), lambda j, place: (0, j))] + [pair_spec] * 4,
            scratch_shapes=[pltpu.VMEM((count, count), F32)],
        ),
        out_shape=[jax.ShapeDtypeStruct((count, steps * wide), BF), narrow, narrow, narrow, narrow],
        compiler_params=pltpu.CompilerParams(vmem_limit_bytes=VMEM_LIMIT),
        cost_estimate=cost(us),
        name="attend_back",
    )(place, query, pair, pair, past, past, mixed, mixed_grad, stats)


def pack_kernel(seq_ref, gate_ref, lift_ref, down_ref, *out_refs):
    owners, _, columns = out_refs[0].shape
    ff = columns // 3
    for seq in range(2):

        @pl.when(seq_ref[0] == seq)
        def _():
            for kind, ref in enumerate((gate_ref, lift_ref, down_ref)):
                for owner in range(owners):
                    for e in range(2):
                        out_refs[e][owner, :, kind * ff : (kind + 1) * ff] = ref[:, (seq * owners + owner) * 2 + e, :]


def pack_experts(seq, gate, lift, down, owners):
    rows, experts, ff = gate.shape
    tile = 32 if rows % 32 == 0 else rows
    in_spec = pl.BlockSpec((tile, experts, ff), lambda i, seq: (i, 0, 0))
    out_spec = pl.BlockSpec((owners, tile, 3 * ff), lambda i, seq: (0, i, 0))
    out = jax.ShapeDtypeStruct((owners, rows, 3 * ff), BF)
    return pl.pallas_call(
        pack_kernel,
        grid_spec=pltpu.PrefetchScalarGridSpec(
            num_scalar_prefetch=1, grid=(rows // tile,), in_specs=[in_spec] * 3, out_specs=[out_spec] * 2
        ),
        out_shape=[out, out],
        compiler_params=pltpu.CompilerParams(vmem_limit_bytes=VMEM_LIMIT),
        cost_estimate=cost(6),
        name="pack_experts",
    )(seq, gate, lift, down)


def unpack_kernel(seq_ref, *refs):
    out_ref = refs[-1]
    owners = refs[0].shape[0]
    for seq in range(2):

        @pl.when(seq_ref[0] == seq)
        def _():
            for e in range(2):
                for at, ref in ((seq, refs[2 * e]), (1 - seq, refs[2 * e + 1])):
                    for owner in range(owners):
                        out_ref[:, (at * owners + owner) * 2 + e, :] = ref[owner].astype(F32)


def unpack_experts(seq, parts, column, ff):
    owners, rows, _ = parts[0].shape
    in_spec = pl.BlockSpec((owners, rows, ff), lambda i, seq: (0, 0, column))
    return pl.pallas_call(
        unpack_kernel,
        grid_spec=pltpu.PrefetchScalarGridSpec(
            num_scalar_prefetch=1,
            grid=(1,),
            in_specs=[in_spec] * 4,
            out_specs=pl.BlockSpec((rows, EXPERTS, ff), lambda i, seq: (0, 0, 0)),
        ),
        out_shape=jax.ShapeDtypeStruct((rows, EXPERTS, ff), F32),
        compiler_params=pltpu.CompilerParams(vmem_limit_bytes=VMEM_LIMIT),
        cost_estimate=cost(4),
        name="unpack_experts",
    )(seq, *parts)


def expert_kernel(e, has_earlier, place_ref, *refs):
    na_ref, nb_ref, ca_ref, cb_ref = refs[:4]
    earlier_refs = refs[4:8] if has_earlier else (None,) * 4
    wt_ref = refs[8] if has_earlier else refs[4]
    (ch_ref, gl_ref, outa_ref, outb_ref, backa_ref, backb_ref) = refs[-6:]
    width = na_ref.shape[1]
    ff = wt_ref.shape[1] // 3
    first = pl.program_id(0) < 2
    mine = 2 * place_ref[0] + e

    def run(n_ref, c_ref, earlier_out, earlier_back, out_ref, back_ref):
        packed = c_ref[:, width:].astype(F32)
        lane = lax.broadcasted_iota(jnp.int32, packed.shape, 1)
        g = dot_nn(n_ref[...], wt_ref[:, :ff])
        l = dot_nn(n_ref[...], wt_ref[:, ff : 2 * ff])
        u = dot_nn(c_ref[:, :width], wt_ref[:, 2 * ff :])
        own_lane = (lane == mine) | (lane == EXPERTS + mine)
        weight = jnp.sum(jnp.where(own_lane, packed, 0.0), axis=-1, keepdims=True)
        sig = 1.0 / (1.0 + jnp.exp(-g))
        silu = g * sig
        hidden = silu * l
        dot = jnp.sum(hidden * u, axis=-1, keepdims=True)
        dot_high = dot.astype(BF).astype(F32)
        dots = jnp.where(lane == mine, dot_high, 0.0)
        dots = jnp.where(lane == EXPERTS + mine, dot - dot_high, dots)
        grad = u * weight
        ch_ref[...] = (hidden * weight).astype(BF)
        gl_ref[:, :ff] = (grad * l * (sig + silu * (1.0 - sig))).astype(BF)
        gl_ref[:, ff:] = (grad * silu).astype(BF)
        back = dot_nt(gl_ref[...], wt_ref[:, : 2 * ff])
        out = dot_nt(ch_ref[...], wt_ref[:, 2 * ff :])
        if has_earlier:
            out = out + earlier_out[:, :width].astype(F32)
            dots = dots + earlier_out[:, width:].astype(F32)
            back = back + earlier_back[...].astype(F32)
        back_ref[...] = back.astype(BF)
        out_ref[:, :width] = out.astype(BF)
        out_ref[:, width:] = dots.astype(BF)

    @pl.when(first)
    def _():
        run(na_ref, ca_ref, earlier_refs[0], earlier_refs[2], outa_ref, backa_ref)

    @pl.when(jnp.logical_not(first))
    def _():
        run(nb_ref, cb_ref, earlier_refs[1], earlier_refs[3], outb_ref, backb_ref)


def expert_rows(place, e, rows, up, packed, chunk, chunks, held, earlier, us):
    count, width = rows[0].shape
    ff = packed.shape[1] // 3
    tile = count // 2
    more = width + 128

    def early(i, place):
        return (jnp.minimum(i, 1), 0)

    def late(i, place):
        return (jnp.maximum(i - 2, 0), 0)

    def at_rows(i, place):
        return (4 * chunk + i, 0)

    any_spec = pl.BlockSpec(memory_space=pl.ANY)
    wide_specs = [pl.BlockSpec((tile, width), early), pl.BlockSpec((tile, width), late)]
    more_specs = [pl.BlockSpec((tile, more), early), pl.BlockSpec((tile, more), late)]
    total = 2 * count * chunks
    one = jax.ShapeDtypeStruct((count, width), BF)
    one_more = jax.ShapeDtypeStruct((count, more), BF)
    held, earlier = list(held), list(earlier)
    begin = 6 + len(earlier)
    packed_spec = pl.BlockSpec((width, 3 * ff), lambda i, place: (0, 0), pipeline_mode=pl.Buffered(1))
    return pl.pallas_call(
        functools.partial(expert_kernel, e, len(earlier) > 0),
        grid_spec=pltpu.PrefetchScalarGridSpec(
            num_scalar_prefetch=1,
            grid=(4,),
            in_specs=wide_specs
            + more_specs
            + (more_specs + wide_specs if earlier else [])
            + [packed_spec]
            + [any_spec] * len(held),
            out_specs=[pl.BlockSpec((tile, ff), at_rows), pl.BlockSpec((tile, 2 * ff), at_rows)]
            + more_specs
            + wide_specs,
        ),
        out_shape=[jax.ShapeDtypeStruct((total, ff), BF), jax.ShapeDtypeStruct((total, 2 * ff), BF)]
        + [one_more] * 2
        + [one] * 2,
        input_output_aliases={begin + at: at for at in range(len(held))},
        compiler_params=pltpu.CompilerParams(vmem_limit_bytes=VMEM_LIMIT),
        cost_estimate=cost(us),
        name="expert_rows",
    )(place, *rows, *up, *earlier, packed, *held)


def expert_grad_kernel(*refs):
    out_ref, sum_ref, held_ref, sems = refs[-4:]
    sources, right_ref = refs[:8], refs[8]
    width = held_ref.shape[2]
    step = pl.program_id(0)

    def fetch(at):
        return pltpu.make_async_copy(sources[at].at[:, :width], held_ref.at[at % 2], sems.at[at % 2])

    @pl.when(step == 0)
    def _():
        fetch(0).start()

    for at in range(len(sources)):

        @pl.when(step == at)
        def _():
            if at + 1 < len(sources):
                fetch(at + 1).start()
            fetch(at).wait()
            product = dot_tn(held_ref[at % 2], right_ref[...])
            if at == 0:
                sum_ref[...] = product
            elif at + 1 < len(sources):
                sum_ref[...] += product
            else:
                out_ref[...] = (sum_ref[...] + product).astype(BF)


def expert_grad(lefts, right, width, total, column, us, held=()):
    count = lefts[0].shape[0]
    columns = right.shape[1]
    any_spec = pl.BlockSpec(memory_space=pl.ANY)
    return pl.pallas_call(
        expert_grad_kernel,
        grid=(len(lefts),),
        in_specs=[any_spec] * len(lefts)
        + [pl.BlockSpec((count, columns), lambda i: (i, 0))]
        + [any_spec] * len(held),
        out_specs=pl.BlockSpec((width, columns), lambda i: (0, column)),
        out_shape=jax.ShapeDtypeStruct((width, total), BF),
        scratch_shapes=[
            pltpu.VMEM((width, columns), F32),
            pltpu.VMEM((2, count, width), BF),
            pltpu.SemaphoreType.DMA((2,)),
        ],
        input_output_aliases={len(lefts) + 1: 0} if held else {},
        compiler_params=pltpu.CompilerParams(vmem_limit_bytes=VMEM_LIMIT),
        cost_estimate=cost(us),
        name="expert_grad",
    )(*lefts, right, *held)


def body(
    tokens,
    lengths,
    routes,
    route_gates,
    cotangent,
    norm_first,
    attention_in,
    attention_out,
    norm_second,
    expert_gate,
    expert_lift,
    expert_down,
):
    count = tokens.shape[1]
    width = tokens.shape[2]
    choose = routes.shape[2]
    seq_count = lax.axis_size("seq")
    inner_count = lax.axis_size("inner")
    owners = seq_count * inner_count
    per_owner = EXPERTS // owners
    ff = expert_gate.shape[2]
    query_width = HEADS * HEAD_DIM
    seq_at = lax.axis_index("seq")
    layer_at = seq_at * inner_count + lax.axis_index("inner")
    length = lengths[0]
    place = jnp.stack([seq_at.astype(jnp.int32), length - seq_at.astype(jnp.int32) * count])
    live_rows = seq_at * count + jnp.arange(count, dtype=jnp.int32) < length
    inputs = tokens[0].astype(F32)
    upstream_low = cotangent[0]
    upstream = upstream_low.astype(F32)

    outer_count = lax.axis_size("outer")
    outer_at = lax.axis_index("outer")
    shard = width // (outer_count * inner_count)
    qkv = attention_in.shape[1]
    gains = jnp.concatenate([norm_first[:, None], norm_second[:, None], jnp.zeros((shard, 126), BF)], axis=1)
    projections = lax.all_gather(
        jnp.concatenate([attention_out, attention_in, gains], axis=1), ROWS, axis=0, tiled=True
    )

    seq_place = seq_at.astype(jnp.int32)[None]
    expert_place = jnp.stack([layer_at.astype(jnp.int32), outer_at.astype(jnp.int32)])
    packed = pack_experts(seq_place, expert_gate, expert_lift, expert_down, inner_count)
    got = [exchange_start(part) for part in packed]
    packed = [exchange_end(*pair).reshape(inner_count * shard, 3 * ff) for pair in zip(packed, got)]
    gathered = [lax.all_gather(packed[0], "outer", axis=0, tiled=True)]
    gathered.append(lax.all_gather(after(packed[1], gathered[0][:8, :128]), "outer", axis=0, tiled=True))

    chosen = (
        routes[0][:, :, None] == jnp.arange(EXPERTS, dtype=jnp.int32)[None, None, :]
    ) & live_rows[:, None, None]
    combine = jnp.sum(jnp.where(chosen, route_gates[0][:, :, None], 0.0), axis=1)
    combine_high = combine.astype(BF)
    combine_low = (combine - combine_high.astype(F32)).astype(BF)
    up_block = jnp.concatenate(
        [upstream_low, combine_high, combine_low, jnp.zeros((count, 128 - 2 * EXPERTS), BF)], axis=1
    )
    half = count // 2
    up_block = after(up_block, packed)
    up_across, up_beside, up_sibling = seq_swap(up_block), side_swap(up_block), core_swap(up_block)

    up_pair_across = (up_across, core_swap(up_across))
    up_pair_beside = (up_beside, core_swap(up_beside))
    query, pair_a, pair_b, lowered_one, gains = project_rows(tokens[0], projections, qkv, query_width)
    past_a = lax.ppermute(pair_a, "seq", [(0, 1)])
    late_pair, past_a = lax.optimization_barrier((pair_b, past_a))
    past_b = lax.ppermute(late_pair, "seq", [(0, 1)])
    mixed, stats_a = attend(place, query, pair_a, past_a, 0)
    mixed, stats_b = attend(place, query, pair_b, past_b, stats_a.shape[0], (mixed,))
    middle, lowered_two = merge_rows(mixed, projections, tokens[0], gains)

    across, beside, sibling = seq_swap(lowered_two), side_swap(lowered_two), core_swap(lowered_two)

    def experts(e, at, rows, up, held, earlier=(), us=1):
        return expert_rows(expert_place, e, rows, up, gathered[e], at, 4, held, earlier, us)

    def upper(block, more):
        return jnp.concatenate([low_plus(block[:half], more), block[half:]])

    def lower(block, more):
        return jnp.concatenate([block[:half], low_plus(block[half:], more)])

    row_own, up_own = (lowered_two, sibling), (up_block, up_sibling)
    made_own = experts(0, 0, row_own, up_own, ())
    across, beside, held = lax.optimization_barrier((across, beside, made_own[:2]))
    far_top, far_low = seq_swap(beside[:half]), side_swap(across[half:])
    up_beside_far, up_across_far = after((up_beside, up_across), held)
    up_far_top, up_far_low = seq_swap(up_beside_far[:half]), side_swap(up_across_far[half:])
    row_across = (across, core_swap(across))
    row_beside = (beside, core_swap(beside))
    made_across = experts(0, 1, row_across, up_pair_across, held)
    made_beside = experts(0, 2, row_beside, up_pair_beside, made_across[:2])
    far_top, far_low, up_far_top, up_far_low, held = lax.optimization_barrier(
        (far_top, far_low, up_far_top, up_far_low, made_beside[:2])
    )
    up_far = jnp.concatenate([up_far_top, up_far_low], axis=0)
    up_pair_far = (up_far, core_swap(up_far))
    far = jnp.concatenate([far_top, far_low], axis=0)
    row_far = (far, core_swap(far))
    made_far = experts(0, 3, row_far, up_pair_far, held)
    hidden_a, grads_a = made_far[:2]

    row_all = (*row_own, *row_across, *row_beside, *row_far)
    up_all = (*up_own, *up_pair_across, *up_pair_beside, *up_pair_far)

    def home(total):
        return lax.psum_scatter(total, "outer", scatter_dimension=0, tiled=True)

    def slots(local):
        return local.reshape(inner_count, shard, local.shape[1])

    total_a = expert_grad(row_all, grads_a, width, 3 * ff, 0, 1)
    total_a = expert_grad(up_all, hidden_a, width, 3 * ff, 2, 1, (total_a,))
    home_a = home(total_a)
    far_parts = after(made_far[2:], total_a)

    made_far = experts(1, 3, row_far, up_pair_far, (), far_parts)
    far_got, far_out_got = core_swap(made_far[5]), core_swap(made_far[3])
    made_across = experts(1, 1, row_across, up_pair_across, made_far[:2], made_across[2:])
    across_got, across_out_got = core_swap(made_across[5]), core_swap(made_across[3])
    far_got, far_out_got, held = lax.optimization_barrier((far_got, far_out_got, made_across[:2]))
    far_sum, far_out, held = lax.optimization_barrier(
        (low_plus(made_far[4], far_got), low_plus(made_far[2], far_out_got), held)
    )
    back_low, back_top = side_swap(far_sum[half:]), seq_swap(far_sum[:half])
    made_beside = experts(1, 2, row_beside, up_pair_beside, held, made_beside[2:], 15)
    beside_got, beside_out_got = core_swap(made_beside[5]), core_swap(made_beside[3])
    across_got, across_out_got, back_low, back_top, held = lax.optimization_barrier(
        (across_got, across_out_got, back_low, back_top, made_beside[:2])
    )
    across_sum, out_across, held = lax.optimization_barrier(
        (lower(low_plus(made_across[4], across_got), back_low), low_plus(made_across[2], across_out_got), held)
    )
    across_in = seq_swap(across_sum)
    made_own = experts(1, 0, row_own, up_own, held, made_own[2:], 15)
    hidden_b, grads_b = made_own[:2]
    own_got = core_swap(made_own[5])
    beside_got, beside_out_got, grads_b = lax.optimization_barrier((beside_got, beside_out_got, grads_b))
    beside_sum, out_beside, grads_b = lax.optimization_barrier(
        (
            upper(low_plus(made_beside[4], beside_got), back_top),
            low_plus(made_beside[2], beside_out_got),
            grads_b,
        )
    )
    beside_in = side_swap(beside_sum)
    out_low, out_top = side_swap(far_out[half:]), seq_swap(far_out[:half])

    total_b = expert_grad(row_all, grads_b, width, 3 * ff, 0, 1)
    total_b = expert_grad(up_all, hidden_b, width, 3 * ff, 2, 1, (total_b,))
    home_b = home(total_b)
    across_in, beside_in, own_got, _ = lax.optimization_barrier((across_in, beside_in, own_got, total_b))

    middle_grad, branch_grad, mixed_grad, second_gain_grad = middle_back(
        made_own[4], own_got, across_in, beside_in, middle, upstream_low, gains, projections, query_width
    )
    second_gain_grad = second_gain_grad[0]
    chain = Chain(mixed_grad)
    own_out_got = core_swap(chain.enter(made_own[3]))
    out_top, out_low = chain.enter((out_top, out_low))
    out_across, out_beside = lower(out_across, out_low), upper(out_beside, out_top)
    out_across, out_beside = chain.leave(lax.optimization_barrier((out_across, out_beside)))
    out_across_in, out_beside_in = seq_swap(out_across), side_swap(out_beside)
    def back(pair, past, stats, first):
        return attend_back(
            chain.enter(place), query, pair, past, mixed, mixed_grad, stats, first, stats.shape[0], 24
        )

    query_a, key_a, value_a, key_past_a, value_past_a = chain.leave(back(pair_a, past_a, stats_a, 0))
    late_a = lax.ppermute(jnp.concatenate([key_past_a, value_past_a], axis=1), "seq", [(1, 0)])
    out_home = HomeSum(chain.leave(dot_tn(chain.enter(mixed), branch_grad).astype(BF)))
    out_across_in, out_beside_in, own_out_got = chain.enter((out_across_in, out_beside_in, own_out_got))
    combined = (
        made_own[2].astype(F32) + own_out_got.astype(F32) + out_across_in.astype(F32) + out_beside_in.astype(F32)
    )
    block_output = chain.leave((middle + combined[:, :width]).astype(BF))[None]
    dots = combined[:, width : width + EXPERTS] + combined[:, width + EXPERTS : width + 2 * EXPERTS]
    grad_gates = chain.leave(jnp.sum(jnp.where(chosen, chain.enter(dots)[:, None, :], 0.0), axis=-1))[None]
    out_home.got = chain.enter(out_home.got)
    chain.leave(out_home.beside())
    a_slots = slots(home_a)
    a_mine = chain.leave(exchange_end(a_slots, chain.enter(exchange_start(a_slots))))
    late_a = chain.leave(chain.enter(late_a))
    a_other = seq_swap(a_mine)
    query_b, key_b, value_b, key_past_b, value_past_b = chain.leave(
        back(pair_b, past_b, stats_b, stats_a.shape[0])
    )
    late_b = lax.ppermute(jnp.concatenate([key_past_b, value_past_b], axis=1), "seq", [(1, 0)])
    a_other = chain.enter(a_other)
    out_home.got = chain.enter(out_home.got)
    chain.leave((out_home.across(), a_other))
    query_grad = jnp.concatenate([query_a, query_b], axis=1)
    query_home = HomeSum(chain.leave(dot_tn(chain.enter(lowered_one), query_grad).astype(BF)))
    query_home.got = chain.enter(query_home.got)
    chain.leave(query_home.beside())
    late_b = chain.enter(late_b)
    split_a, split_b = key_past_a.shape[1], key_past_b.shape[1]
    pair_own = jnp.concatenate([key_a, key_b, value_a, value_b], axis=1)
    pair_late = jnp.concatenate(
        [late_a[:, :split_a], late_b[:, :split_b], late_a[:, split_a:], late_b[:, split_b:]], axis=1
    )
    pair_grad = low_plus(pair_own, pair_late)
    pair_weight = chain.leave(dot_tn(lowered_one, pair_grad).astype(BF))
    pair_part = lax.psum_scatter(pair_weight, ROWS, scatter_dimension=0, tiled=True)
    projected_grad = jnp.concatenate([query_grad, pair_grad], axis=1)
    normed_grad_one = chain.leave(
        dot_nt(chain.enter(projected_grad), projections[:, query_width : query_width + qkv])
    )
    query_home.got = chain.enter(query_home.got)
    chain.leave(query_home.across())
    out_home.got = chain.enter(out_home.got)
    chain.leave(out_home.along())
    normed_one, inverse_one, _ = norm_rows(inputs, gains[0])
    input_norm_grad, first_gain_grad = norm_back(chain.enter(normed_grad_one), normed_one, inverse_one, gains[0])
    grad_tokens = chain.leave(middle_grad + input_norm_grad)[None]
    gain_grads = jnp.stack([first_gain_grad, second_gain_grad])
    gain_grads = gain_grads + core_swap(gain_grads)
    query_home.got = chain.enter(query_home.got)
    chain.leave(query_home.along())
    gain_grads = chain.leave(chain.enter(gain_grads))
    gain_grads = gain_grads + seq_swap(gain_grads)
    b_slots = slots(chain.enter(home_b))
    b_mine = chain.leave(exchange_end(b_slots, chain.enter(exchange_start(b_slots))))
    gain_grads = chain.leave(chain.enter(gain_grads))
    b_other = seq_swap(after(b_mine, gain_grads))
    gain_grads = gain_grads + side_swap(gain_grads)
    query_home.got = chain.enter(query_home.got)
    out_home.got = chain.enter(out_home.got)
    chain.leave((query_home.final(), out_home.final()))

    gain_grads = chain.leave(chain.enter(gain_grads)).reshape(2, outer_count, inner_count * shard)
    gain_sum = pick(gain_grads, outer_at, 1)
    for step in range(1, outer_count):
        piece = pick(gain_grads, lax.rem(outer_at + step, outer_count), 1)
        gain_sum = gain_sum + lax.ppermute(
            piece, "outer", [(i, (i + step) % outer_count) for i in range(outer_count)]
        )
    gain_sum = chain.leave(pick(gain_sum.reshape(2, inner_count, shard), lax.axis_index("inner"), 1))
    parts = chain.enter((a_mine, a_other, b_mine, b_other))
    grads = [unpack_experts(seq_place, parts, kind, ff) for kind in range(3)]
    grad_gate, grad_lift, grad_down = chain.leave(lax.optimization_barrier(tuple(grads)))
    out_home.other, query_home.other = chain.enter((out_home.other, query_home.other))
    grad_out = chain.leave(out_home.result())
    pair_part = chain.enter(pair_part)
    pair_sum = pair_part.astype(F32) + seq_swap(pair_part).astype(F32)
    grad_in = jnp.concatenate([query_home.result(), pair_sum], axis=1)
    return (
        block_output,
        grad_tokens,
        grad_gates,
        gain_sum[0],
        grad_in,
        grad_out,
        gain_sum[1],
        grad_gate,
        grad_lift,
        grad_down,
    )


def solution(mesh):
    seq_count, fsdp_count = mesh.devices.shape
    inner_count = EXPERTS // (2 * seq_count)
    fine = jax.sharding.Mesh(
        mesh.devices.reshape(seq_count, fsdp_count // inner_count, inner_count), ("seq", "outer", "inner")
    )
    return jax.shard_map(
        body,
        mesh=fine,
        in_specs=(
            P(ROWS, "seq", None),
            P(ROWS),
            P(ROWS, "seq", None),
            P(ROWS, "seq", None),
            P(ROWS, "seq", None),
            P(ROWS),
            P(ROWS, None),
            P(ROWS, None),
            P(ROWS),
            P(ROWS, None, None),
            P(ROWS, None, None),
            P(ROWS, None, None),
        ),
        out_specs=(
            P(ROWS, "seq", None),
            P(ROWS, "seq", None),
            P(ROWS, "seq", None),
            P(ROWS),
            P(ROWS, None),
            P(ROWS, None),
            P(ROWS),
            P(ROWS, None, None),
            P(ROWS, None, None),
            P(ROWS, None, None),
        ),
        check_vma=False,
    )
```

```python
import functools

import jax
import jax.numpy as jnp
from jax import lax
from jax.experimental import pallas as pl
from jax.experimental.pallas import tpu as pltpu
from jax.sharding import PartitionSpec as P

HEADS = 24
KV_HEADS = 8
HEAD_DIM = 64
EXPERTS = 16
GROUP = HEADS // KV_HEADS
EPS = 1e-06
BF = jnp.bfloat16
F32 = jnp.float32
ROWS = ("outer", "inner")
VMEM_LIMIT = 60 * 1024 * 1024


def cost(microseconds):
    return pl.CostEstimate(flops=int(microseconds * 0.6e9), bytes_accessed=1000, transcendentals=0)


def norm_rows(values, gain_vector):
    inverse = lax.rsqrt(jnp.mean(values * values, axis=-1, keepdims=True) + EPS)
    normed = values * inverse
    return (normed, inverse, (normed * gain_vector).astype(BF))


def norm_back(upstream, normed, inverse, gain_vector):
    scaled = upstream * gain_vector
    spread = jnp.mean(scaled * normed, axis=-1, keepdims=True)
    return (inverse * (scaled - normed * spread), jnp.sum(upstream * normed, axis=0))


def swap(x, axis, bit):
    return lax.ppermute(x, axis, [(i, i ^ bit) for i in range(lax.axis_size(axis))])


def core_swap(x):
    return swap(x, "inner", 1)


def side_swap(x):
    return swap(x, "inner", 2)


def seq_swap(x):
    return swap(x, "seq", 1)


def after(x, *others):
    return lax.optimization_barrier((x, others))[0]


def low_plus(a, b):
    return (a.astype(F32) + b.astype(F32)).astype(BF)


def exchange_start(pieces):
    at = lax.axis_index("inner")
    bits = range(1, lax.axis_size("inner"))
    return [swap(lax.dynamic_index_in_dim(pieces, at ^ bit, 0, keepdims=False), "inner", bit) for bit in bits]


def exchange_end(pieces, got):
    at = lax.axis_index("inner")
    for bit, piece in enumerate(got, 1):
        pieces = lax.dynamic_update_index_in_dim(pieces, piece, at ^ bit, 0)
    return pieces


def pick(x, at, axis):
    return lax.dynamic_index_in_dim(x, at, axis, keepdims=False)


class HomeSum:
    def __init__(self, *totals):
        rows, columns = totals[0].shape[0], sum(total.shape[1] for total in totals)
        self.n = lax.axis_size("outer")
        self.seq_at = lax.axis_index("seq")
        self.outer_at = lax.axis_index("outer")
        inner_at = lax.axis_index("inner")
        sides = lax.axis_size("inner") // 2
        self.side_at, core_at = inner_at // 2, inner_at % 2
        self.half = columns // 2
        self.split = False
        part = rows // (self.n * sides * 2)

        def half_of(at):
            return jnp.concatenate(
                [pick(total.reshape(self.n, sides, 2, part, total.shape[1]), at, 2) for total in totals], axis=-1
            )

        self.held = half_of(core_at)
        self.got = core_swap(half_of(1 - core_at))

    def beside(self):
        held = low_plus(self.held, self.got)
        self.got = side_swap(pick(held, 1 - self.side_at, 1))
        self.held = pick(held, self.side_at, 1)
        return held

    def across(self):
        held = low_plus(self.held, self.got)
        self.got = seq_swap(lax.dynamic_slice_in_dim(held, (1 - self.seq_at) * self.half, self.half, 2))
        self.held = lax.dynamic_slice_in_dim(held, self.seq_at * self.half, self.half, 2)
        self.split = True
        return held

    def along(self):
        held = low_plus(self.held, self.got)
        self.held = pick(held, self.outer_at, 0)
        self.got = []
        for step in range(1, self.n):
            piece = pick(held, lax.rem(self.outer_at + step, self.n), 0)
            self.got.append(lax.ppermute(piece, "outer", [(i, (i + step) % self.n) for i in range(self.n)]))
        return held

    def final(self):
        result = self.held.astype(F32)
        for got in self.got:
            result = result + got.astype(F32)
        self.low = result.astype(BF)
        self.other = seq_swap(self.low)
        return self.low

    def result(self):
        low, other = self.low.astype(F32), self.other.astype(F32)
        if not self.split:
            return low + other
        first = self.seq_at == 0
        return jnp.concatenate([jnp.where(first, low, other), jnp.where(first, other, low)], axis=1)


class Chain:
    def __init__(self, last):
        self.last = last

    def enter(self, x):
        return after(x, self.last)

    def leave(self, y):
        self.last = y
        return y


def dot_nt(a, b):
    return lax.dot_general(a, b, (((1,), (1,)), ((), ())), preferred_element_type=F32)


def dot_nn(a, b):
    return lax.dot_general(a, b, (((1,), (0,)), ((), ())), preferred_element_type=F32)


def dot_tn(a, b):
    return lax.dot_general(a, b, (((0,), (0,)), ((), ())), preferred_element_type=F32)


def project_in_kernel(token_ref, weight_ref, tail_ref, query_ref, paira_ref, pairb_ref, low_ref, gain_ref):
    step = pl.program_id(0)
    queries = HEADS * HEAD_DIM // weight_ref.shape[1]

    @pl.when(step == 0)
    def _():
        row = lax.broadcasted_iota(jnp.int32, (8, 128), 0)
        lane = lax.broadcasted_iota(jnp.int32, (8, 128), 1)
        gain_ref[...] = dot_nt((row == lane).astype(BF), tail_ref[...])
        x = token_ref[...].astype(F32)
        inverse = lax.rsqrt(jnp.mean(x * x, axis=-1, keepdims=True) + EPS)
        low_ref[...] = (x * inverse * gain_ref[0:1, :]).astype(BF)

    result = dot_nn(low_ref[...], weight_ref[...]).astype(BF)

    @pl.when(step < queries)
    def _():
        query_ref[...] = result

    half = result.shape[1] // 2
    for part in range(2):

        @pl.when(step == queries + part)
        def _():
            cols = slice(part * half, (part + 1) * half)
            paira_ref[:, cols] = result[:, :half]
            pairb_ref[:, cols] = result[:, half:]


def project_rows(tokens, weight, qkv, before):
    count, width = tokens.shape
    tile = 512
    query_width = HEADS * HEAD_DIM
    queries = query_width // tile
    return pl.pallas_call(
        project_in_kernel,
        grid=(qkv // tile,),
        in_specs=[
            pl.BlockSpec((count, width), lambda j: (0, 0)),
            pl.BlockSpec((width, tile), lambda j: (0, before // tile + j)),
            pl.BlockSpec((width, 128), lambda j: (0, (before + qkv) // 128)),
        ],
        out_specs=[
            pl.BlockSpec((count, tile), lambda j: (0, jnp.minimum(j, queries - 1))),
            pl.BlockSpec((count, tile), lambda j: (0, 0)),
            pl.BlockSpec((count, tile), lambda j: (0, 0)),
            pl.BlockSpec((count, width), lambda j: (0, 0)),
            pl.BlockSpec((8, width), lambda j: (0, 0)),
        ],
        out_shape=[
            jax.ShapeDtypeStruct((count, query_width), BF),
            jax.ShapeDtypeStruct((count, tile), BF),
            jax.ShapeDtypeStruct((count, tile), BF),
            jax.ShapeDtypeStruct((count, width), BF),
            jax.ShapeDtypeStruct((8, width), F32),
        ],
        compiler_params=pltpu.CompilerParams(vmem_limit_bytes=VMEM_LIMIT),
        cost_estimate=cost(0),
        name="project_rows",
    )(tokens, weight, weight)


def merge_kernel(mixed_ref, weight_ref, token_ref, gain_ref, middle_ref, low_ref):
    product = dot_nn(mixed_ref[...], weight_ref[...])
    step = pl.program_id(0)

    @pl.when(step == 0)
    def _():
        middle_ref[...] = token_ref[...].astype(F32) + product

    @pl.when(step > 0)
    def _():
        middle_ref[...] += product

    @pl.when(step == pl.num_programs(0) - 1)
    def _():
        x = middle_ref[...]
        inverse = lax.rsqrt(jnp.mean(x * x, axis=-1, keepdims=True) + EPS)
        low_ref[...] = (x * inverse * gain_ref[1:2, :]).astype(BF)


def merge_rows(mixed, weight, tokens, gains):
    count, width = tokens.shape
    tile = 512
    whole = pl.BlockSpec((count, width), lambda j: (0, 0))
    return pl.pallas_call(
        merge_kernel,
        grid=(mixed.shape[1] // tile,),
        in_specs=[
            pl.BlockSpec((count, tile), lambda j: (0, j)),
            pl.BlockSpec((tile, width), lambda j: (j, 0)),
            whole,
            pl.BlockSpec((8, width), lambda j: (0, 0)),
        ],
        out_specs=[whole, whole],
        out_shape=[jax.ShapeDtypeStruct((count, width), F32), jax.ShapeDtypeStruct((count, width), BF)],
        compiler_params=pltpu.CompilerParams(vmem_limit_bytes=VMEM_LIMIT),
        cost_estimate=cost(0),
        name="merge_rows",
    )(mixed, weight, tokens, gains)


def middle_back_kernel(
    own_ref, got_ref, across_ref, beside_ref, middle_ref, up_ref, gain_ref, weight_ref,
    grad_ref, low_ref, mixed_ref, sum_ref,
):
    @pl.when(pl.program_id(0) == 0)
    def _():
        above = own_ref[...].astype(F32) + got_ref[...].astype(F32)
        above = above + across_ref[...].astype(F32) + beside_ref[...].astype(F32)
        x = middle_ref[...]
        inverse = lax.rsqrt(jnp.mean(x * x, axis=-1, keepdims=True) + EPS)
        normed = x * inverse
        scaled = above * gain_ref[1:2, :]
        spread = jnp.mean(scaled * normed, axis=-1, keepdims=True)
        grad = up_ref[...].astype(F32) + inverse * (scaled - normed * spread)
        grad_ref[...] = grad
        low_ref[...] = grad.astype(BF)
        sum_ref[...] = jnp.broadcast_to(jnp.sum(above * normed, axis=0, keepdims=True), sum_ref.shape)

    mixed_ref[...] = dot_nt(low_ref[...], weight_ref[...]).astype(BF)


def middle_back(own, got, across, beside, middle, up, gains, weight, columns):
    count, width = own.shape
    tile = 512
    whole = pl.BlockSpec((count, width), lambda j: (0, 0))
    row = pl.BlockSpec((8, width), lambda j: (0, 0))
    return pl.pallas_call(
        middle_back_kernel,
        grid=(columns // tile,),
        in_specs=[whole] * 6 + [row, pl.BlockSpec((tile, width), lambda j: (j, 0))],
        out_specs=[whole, whole, pl.BlockSpec((count, tile), lambda j: (0, j)), row],
        out_shape=[
            jax.ShapeDtypeStruct((count, width), F32),
            jax.ShapeDtypeStruct((count, width), BF),
            jax.ShapeDtypeStruct((count, columns), BF),
            jax.ShapeDtypeStruct((8, width), F32),
        ],
        compiler_params=pltpu.CompilerParams(vmem_limit_bytes=VMEM_LIMIT),
        cost_estimate=cost(1),
        name="middle_back",
    )(own, got, across, beside, middle, up, gains, weight)


def attend_kernel(place_ref, q_ref, k_ref, v_ref, kr_ref, vr_ref, *refs):
    mixed_ref, stat_ref, bias_ref, col_ref = refs[-4:]
    count = q_ref.shape[0]
    half = count // 2
    seq_at = place_ref[0]
    live = place_ref[1]

    @pl.when(pl.program_id(0) == 0)
    def _():
        row = lax.broadcasted_iota(jnp.int32, (count, count), 0)
        col = lax.broadcasted_iota(jnp.int32, (count, count), 1)
        bias_ref[...] = jnp.where((col <= row) & (col < live), 0.0, -jnp.inf)
        col_ref[...] = jnp.zeros_like(col_ref)

    def run(with_past):
        for g in range(2):
            lanes = slice(g * HEAD_DIM, (g + 1) * HEAD_DIM)
            key = k_ref[:, lanes]
            value = v_ref[:, lanes]
            if with_past:
                key_past = kr_ref[:, lanes]
                value_past = vr_ref[:, lanes]
            for r in range(GROUP):
                h = g * GROUP + r
                for part in range(2):
                    rows = slice(part * half, (part + 1) * half)
                    span = (part + 1) * half
                    query = q_ref[rows, h * HEAD_DIM : (h + 1) * HEAD_DIM] * BF(HEAD_DIM**-0.5)
                    scores = dot_nt(query, key[:span]) + bias_ref[rows, :span]
                    peak = jnp.max(scores, axis=-1, keepdims=True)
                    if with_past:
                        past = dot_nt(query, key_past)
                        peak = jnp.maximum(peak, jnp.max(past, axis=-1, keepdims=True))
                    lifted = jnp.exp(scores - peak)
                    total = jnp.sum(lifted, axis=-1, keepdims=True)
                    mixed = dot_nn(lifted.astype(BF), value[:span])
                    if with_past:
                        lifted_past = jnp.exp(past - peak)
                        total = total + jnp.sum(lifted_past, axis=-1, keepdims=True)
                        mixed = mixed + dot_nn(lifted_past.astype(BF), value_past)
                    mixed_ref[rows, h * HEAD_DIM : (h + 1) * HEAD_DIM] = (mixed / total).astype(BF)
                    col_ref[rows, h : h + 1] = peak + jnp.log(total)

    @pl.when(seq_at == 0)
    def _():
        run(False)

    @pl.when(seq_at != 0)
    def _():
        run(True)

    stat_ref[...] = col_ref[...].T[:8, :]


def attend(place, query, pair, past, first, held=()):
    count = query.shape[0]
    steps = pair.shape[1] // 256
    wide = 2 * GROUP * HEAD_DIM
    return pl.pallas_call(
        attend_kernel,
        grid_spec=pltpu.PrefetchScalarGridSpec(
            num_scalar_prefetch=1,
            grid=(steps,),
            in_specs=[
                pl.BlockSpec((count, wide), lambda j, place: (0, first + j)),
                pl.BlockSpec((count, 128), lambda j, place: (0, j)),
                pl.BlockSpec((count, 128), lambda j, place: (0, steps + j)),
                pl.BlockSpec((count, 128), lambda j, place: (0, j)),
                pl.BlockSpec((count, 128), lambda j, place: (0, steps + j)),
            ]
            + [pl.BlockSpec(memory_space=pl.ANY)] * len(held),
            out_specs=[
                pl.BlockSpec((count, wide), lambda j, place: (0, first + j)),
                pl.BlockSpec((None, 8, count), lambda j, place: (j, 0, 0)),
            ],
            scratch_shapes=[pltpu.VMEM((count, count), F32), pltpu.VMEM((count, 128), F32)],
        ),
        out_shape=[
            jax.ShapeDtypeStruct((count, HEADS * HEAD_DIM), BF),
            jax.ShapeDtypeStruct((steps, 8, count), F32),
        ],
        input_output_aliases={6: 0} if held else {},
        compiler_params=pltpu.CompilerParams(vmem_limit_bytes=VMEM_LIMIT),
        cost_estimate=cost(0),
        name="attend",
    )(place, query, pair, pair, past, past, *held)


def attend_back_kernel(
    place_ref, q_ref, k_ref, v_ref, kr_ref, vr_ref, mixed_ref, grad_ref, stat_ref,
    dq_ref, dk_ref, dv_ref, dkr_ref, dvr_ref, bias_ref,
):
    count = q_ref.shape[0]
    half = count // 2
    seq_at = place_ref[0]
    live = place_ref[1]
    scale = HEAD_DIM**-0.5

    @pl.when(pl.program_id(0) == 0)
    def _():
        key_at = lax.broadcasted_iota(jnp.int32, (count, count), 0)
        query_at = lax.broadcasted_iota(jnp.int32, (count, count), 1)
        bias_ref[...] = jnp.where((key_at <= query_at) & (key_at < live), 0.0, -jnp.inf)

    def run(with_past):
        for g in range(2):
            lanes = slice(g * HEAD_DIM, (g + 1) * HEAD_DIM)
            key = k_ref[:, lanes]
            value = v_ref[:, lanes]
            sums = [[jnp.zeros((half, HEAD_DIM), F32) for _ in range(2)] for _ in range(2)]
            if with_past:
                key_past = kr_ref[:, lanes]
                value_past = vr_ref[:, lanes]
                past_sums = [jnp.zeros((count, HEAD_DIM), F32) for _ in range(2)]
            for r in range(GROUP):
                h = g * GROUP + r
                cols = slice(h * HEAD_DIM, (h + 1) * HEAD_DIM)
                query = q_ref[:, cols] * BF(scale)
                grad = grad_ref[:, cols]
                product = grad.astype(F32) * mixed_ref[:, cols].astype(F32)
                delta = lax.dot_general(
                    jnp.ones((8, HEAD_DIM), F32), product, (((1,), (1,)), ((), ())),
                    precision=lax.Precision.HIGHEST, preferred_element_type=F32,
                )[:1]
                stat = stat_ref[h : h + 1, :]

                def piece(keys, values, queries, grads, stats, deltas, bias):
                    scores = dot_nt(keys, queries)
                    if bias is not None:
                        scores = scores + bias
                    chances = jnp.exp(scores - stats)
                    chance_grad = dot_nt(values, grads)
                    score_grad = (chances * (chance_grad - deltas)).astype(BF)
                    return chances.astype(BF), score_grad

                p0, s0 = piece(key[:half], value[:half], query, grad, stat, delta, bias_ref[:half, :])
                p1, s1 = piece(
                    key[half:], value[half:], query[half:], grad[half:], stat[:, half:], delta[:, half:],
                    bias_ref[half:, half:],
                )
                dq = dot_tn(s0, key[:half])
                dq_late = dot_tn(s1, key[half:])
                sums[0][0] += dot_nn(s0, query)
                sums[0][1] += dot_nn(s1, query[half:])
                sums[1][0] += dot_nn(p0, grad)
                sums[1][1] += dot_nn(p1, grad[half:])
                if with_past:
                    pp, sp = piece(key_past, value_past, query, grad, stat, delta, None)
                    dq = dq + dot_tn(sp, key_past)
                    past_sums[0] += dot_nn(sp, query)
                    past_sums[1] += dot_nn(pp, grad)
                dq_ref[:half, cols] = (dq[:half] * scale).astype(BF)
                dq_ref[half:, cols] = ((dq[half:] + dq_late) * scale).astype(BF)
            for where, out in ((0, dk_ref), (1, dv_ref)):
                out[:half, lanes] = sums[where][0].astype(BF)
                out[half:, lanes] = sums[where][1].astype(BF)
            if with_past:
                dkr_ref[:, lanes] = past_sums[0].astype(BF)
                dvr_ref[:, lanes] = past_sums[1].astype(BF)

    @pl.when(seq_at == 0)
    def _():
        run(False)
        dkr_ref[...] = jnp.zeros_like(dkr_ref)
        dvr_ref[...] = jnp.zeros_like(dvr_ref)

    @pl.when(seq_at != 0)
    def _():
        run(True)


def attend_back(place, query, pair, past, mixed, mixed_grad, stats, first, steps, us):
    count = query.shape[0]
    wide = 2 * GROUP * HEAD_DIM
    narrow = jax.ShapeDtypeStruct((count, steps * 128), BF)
    head_spec = pl.BlockSpec((count, wide), lambda j, place: (0, first + j))
    pair_spec = pl.BlockSpec((count, 128), lambda j, place: (0, j))
    return pl.pallas_call(
        attend_back_kernel,
        grid_spec=pltpu.PrefetchScalarGridSpec(
            num_scalar_prefetch=1,
            grid=(steps,),
            in_specs=[
                head_spec,
                pl.BlockSpec((count, 128), lambda j, place: (0, j)),
                pl.BlockSpec((count, 128), lambda j, place: (0, steps + j)),
                pl.BlockSpec((count, 128), lambda j, place: (0, j)),
                pl.BlockSpec((count, 128), lambda j, place: (0, steps + j)),
                head_spec,
                head_spec,
                pl.BlockSpec((None, 8, count), lambda j, place: (j, 0, 0)),
            ],
            out_specs=[pl.BlockSpec((count, wide), lambda j, place: (0, j))] + [pair_spec] * 4,
            scratch_shapes=[pltpu.VMEM((count, count), F32)],
        ),
        out_shape=[jax.ShapeDtypeStruct((count, steps * wide), BF), narrow, narrow, narrow, narrow],
        compiler_params=pltpu.CompilerParams(vmem_limit_bytes=VMEM_LIMIT),
        cost_estimate=cost(us),
        name="attend_back",
    )(place, query, pair, pair, past, past, mixed, mixed_grad, stats)


def pair_kernel(low_ref, keya_ref, keyb_ref, valuea_ref, valueb_ref, latea_ref, lateb_ref, pair_ref, grad_ref):
    half = keya_ref.shape[1]
    for part, (a_ref, b_ref) in enumerate(((keya_ref, keyb_ref), (valuea_ref, valueb_ref))):

        @pl.when(pl.program_id(0) == part)
        def _():
            cols = slice(part * half, (part + 1) * half)
            pair_ref[:, :half] = (a_ref[...].astype(F32) + latea_ref[:, cols].astype(F32)).astype(BF)
            pair_ref[:, half:] = (b_ref[...].astype(F32) + lateb_ref[:, cols].astype(F32)).astype(BF)

    grad_ref[...] = dot_tn(low_ref[...], pair_ref[...]).astype(BF)


def pair_back(low, key_a, key_b, value_a, value_b, late_a, late_b):
    count, width = low.shape
    half = key_a.shape[1]

    def whole(x):
        return pl.BlockSpec(x.shape, lambda j: (0, 0))

    args = (low, key_a, key_b, value_a, value_b, late_a, late_b)
    return pl.pallas_call(
        pair_kernel,
        grid=(2,),
        in_specs=[whole(x) for x in args],
        out_specs=[
            pl.BlockSpec((count, 2 * half), lambda j: (0, j)),
            pl.BlockSpec((width, 2 * half), lambda j: (0, j)),
        ],
        out_shape=[
            jax.ShapeDtypeStruct((count, 4 * half), BF),
            jax.ShapeDtypeStruct((width, 4 * half), BF),
        ],
        compiler_params=pltpu.CompilerParams(vmem_limit_bytes=VMEM_LIMIT),
        cost_estimate=cost(0),
        name="pair_back",
    )(*args)


def pack_kernel(seq_ref, gate_ref, lift_ref, down_ref, *out_refs):
    owners, _, columns = out_refs[0].shape
    ff = columns // 3
    for seq in range(2):

        @pl.when(seq_ref[0] == seq)
        def _():
            for kind, ref in enumerate((gate_ref, lift_ref, down_ref)):
                for owner in range(owners):
                    for e in range(2):
                        out_refs[e][owner, :, kind * ff : (kind + 1) * ff] = ref[:, (seq * owners + owner) * 2 + e, :]


def pack_experts(seq, gate, lift, down, owners):
    rows, experts, ff = gate.shape
    tile = 32 if rows % 32 == 0 else rows
    in_spec = pl.BlockSpec((tile, experts, ff), lambda i, seq: (i, 0, 0))
    out_spec = pl.BlockSpec((owners, tile, 3 * ff), lambda i, seq: (0, i, 0))
    out = jax.ShapeDtypeStruct((owners, rows, 3 * ff), BF)
    return pl.pallas_call(
        pack_kernel,
        grid_spec=pltpu.PrefetchScalarGridSpec(
            num_scalar_prefetch=1, grid=(rows // tile,), in_specs=[in_spec] * 3, out_specs=[out_spec] * 2
        ),
        out_shape=[out, out],
        compiler_params=pltpu.CompilerParams(vmem_limit_bytes=VMEM_LIMIT),
        cost_estimate=cost(6),
        name="pack_experts",
    )(seq, gate, lift, down)


def unpack_kernel(seq_ref, *refs):
    out_ref = refs[-1]
    owners = refs[0].shape[0]
    for seq in range(2):

        @pl.when(seq_ref[0] == seq)
        def _():
            for e in range(2):
                for at, ref in ((seq, refs[2 * e]), (1 - seq, refs[2 * e + 1])):
                    for owner in range(owners):
                        out_ref[:, (at * owners + owner) * 2 + e, :] = ref[owner].astype(F32)


def unpack_experts(seq, parts, column, ff):
    owners, rows, _ = parts[0].shape
    in_spec = pl.BlockSpec((owners, rows, ff), lambda i, seq: (0, 0, column))
    return pl.pallas_call(
        unpack_kernel,
        grid_spec=pltpu.PrefetchScalarGridSpec(
            num_scalar_prefetch=1,
            grid=(1,),
            in_specs=[in_spec] * 4,
            out_specs=pl.BlockSpec((rows, EXPERTS, ff), lambda i, seq: (0, 0, 0)),
        ),
        out_shape=jax.ShapeDtypeStruct((rows, EXPERTS, ff), F32),
        compiler_params=pltpu.CompilerParams(vmem_limit_bytes=VMEM_LIMIT),
        cost_estimate=cost(4),
        name="unpack_experts",
    )(seq, *parts)


def expert_kernel(e, has_earlier, place_ref, *refs):
    na_ref, nb_ref, ca_ref, cb_ref = refs[:4]
    earlier_refs = refs[4:8] if has_earlier else (None,) * 4
    wt_ref = refs[8] if has_earlier else refs[4]
    (ch_ref, gl_ref, outa_ref, outb_ref, backa_ref, backb_ref) = refs[-6:]
    width = na_ref.shape[1]
    ff = wt_ref.shape[1] // 3
    first = pl.program_id(0) < 2
    mine = 2 * place_ref[0] + e

    def run(n_ref, c_ref, earlier_out, earlier_back, out_ref, back_ref):
        packed = c_ref[:, width:].astype(F32)
        lane = lax.broadcasted_iota(jnp.int32, packed.shape, 1)
        g = dot_nn(n_ref[...], wt_ref[:, :ff])
        l = dot_nn(n_ref[...], wt_ref[:, ff : 2 * ff])
        u = dot_nn(c_ref[:, :width], wt_ref[:, 2 * ff :])
        own_lane = (lane == mine) | (lane == EXPERTS + mine)
        weight = jnp.sum(jnp.where(own_lane, packed, 0.0), axis=-1, keepdims=True)
        sig = 1.0 / (1.0 + jnp.exp(-g))
        silu = g * sig
        hidden = silu * l
        dot = jnp.sum(hidden * u, axis=-1, keepdims=True)
        dot_high = dot.astype(BF).astype(F32)
        dots = jnp.where(lane == mine, dot_high, 0.0)
        dots = jnp.where(lane == EXPERTS + mine, dot - dot_high, dots)
        grad = u * weight
        ch_ref[...] = (hidden * weight).astype(BF)
        gl_ref[:, :ff] = (grad * l * (sig + silu * (1.0 - sig))).astype(BF)
        gl_ref[:, ff:] = (grad * silu).astype(BF)
        back = dot_nt(gl_ref[...], wt_ref[:, : 2 * ff])
        out = dot_nt(ch_ref[...], wt_ref[:, 2 * ff :])
        if has_earlier:
            out = out + earlier_out[:, :width].astype(F32)
            dots = dots + earlier_out[:, width:].astype(F32)
            back = back + earlier_back[...].astype(F32)
        back_ref[...] = back.astype(BF)
        out_ref[:, :width] = out.astype(BF)
        out_ref[:, width:] = dots.astype(BF)

    @pl.when(first)
    def _():
        run(na_ref, ca_ref, earlier_refs[0], earlier_refs[2], outa_ref, backa_ref)

    @pl.when(jnp.logical_not(first))
    def _():
        run(nb_ref, cb_ref, earlier_refs[1], earlier_refs[3], outb_ref, backb_ref)


def expert_rows(place, e, rows, up, packed, chunk, chunks, held, earlier, us):
    count, width = rows[0].shape
    ff = packed.shape[1] // 3
    tile = count // 2
    more = width + 128

    def early(i, place):
        return (jnp.minimum(i, 1), 0)

    def late(i, place):
        return (jnp.maximum(i - 2, 0), 0)

    def at_rows(i, place):
        return (4 * chunk + i, 0)

    any_spec = pl.BlockSpec(memory_space=pl.ANY)
    wide_specs = [pl.BlockSpec((tile, width), early), pl.BlockSpec((tile, width), late)]
    more_specs = [pl.BlockSpec((tile, more), early), pl.BlockSpec((tile, more), late)]
    total = 2 * count * chunks
    one = jax.ShapeDtypeStruct((count, width), BF)
    one_more = jax.ShapeDtypeStruct((count, more), BF)
    held, earlier = list(held), list(earlier)
    begin = 6 + len(earlier)
    packed_spec = pl.BlockSpec((width, 3 * ff), lambda i, place: (0, 0), pipeline_mode=pl.Buffered(1))
    return pl.pallas_call(
        functools.partial(expert_kernel, e, len(earlier) > 0),
        grid_spec=pltpu.PrefetchScalarGridSpec(
            num_scalar_prefetch=1,
            grid=(4,),
            in_specs=wide_specs
            + more_specs
            + (more_specs + wide_specs if earlier else [])
            + [packed_spec]
            + [any_spec] * len(held),
            out_specs=[pl.BlockSpec((tile, ff), at_rows), pl.BlockSpec((tile, 2 * ff), at_rows)]
            + more_specs
            + wide_specs,
        ),
        out_shape=[jax.ShapeDtypeStruct((total, ff), BF), jax.ShapeDtypeStruct((total, 2 * ff), BF)]
        + [one_more] * 2
        + [one] * 2,
        input_output_aliases={begin + at: at for at in range(len(held))},
        compiler_params=pltpu.CompilerParams(vmem_limit_bytes=VMEM_LIMIT),
        cost_estimate=cost(us),
        name="expert_rows",
    )(place, *rows, *up, *earlier, packed, *held)


def expert_grad_kernel(*refs):
    out_ref, sum_ref, held_ref, sems = refs[-4:]
    sources, right_ref = refs[:8], refs[8]
    width = held_ref.shape[2]
    step = pl.program_id(0)

    def fetch(at):
        return pltpu.make_async_copy(sources[at].at[:, :width], held_ref.at[at % 2], sems.at[at % 2])

    @pl.when(step == 0)
    def _():
        fetch(0).start()

    for at in range(len(sources)):

        @pl.when(step == at)
        def _():
            if at + 1 < len(sources):
                fetch(at + 1).start()
            fetch(at).wait()
            product = dot_tn(held_ref[at % 2], right_ref[...])
            if at == 0:
                sum_ref[...] = product
            elif at + 1 < len(sources):
                sum_ref[...] += product
            else:
                out_ref[...] = (sum_ref[...] + product).astype(BF)


def expert_grad(lefts, right, width, total, column, us, held=()):
    count = lefts[0].shape[0]
    columns = right.shape[1]
    any_spec = pl.BlockSpec(memory_space=pl.ANY)
    return pl.pallas_call(
        expert_grad_kernel,
        grid=(len(lefts),),
        in_specs=[any_spec] * len(lefts)
        + [pl.BlockSpec((count, columns), lambda i: (i, 0))]
        + [any_spec] * len(held),
        out_specs=pl.BlockSpec((width, columns), lambda i: (0, column)),
        out_shape=jax.ShapeDtypeStruct((width, total), BF),
        scratch_shapes=[
            pltpu.VMEM((width, columns), F32),
            pltpu.VMEM((2, count, width), BF),
            pltpu.SemaphoreType.DMA((2,)),
        ],
        input_output_aliases={len(lefts) + 1: 0} if held else {},
        compiler_params=pltpu.CompilerParams(vmem_limit_bytes=VMEM_LIMIT),
        cost_estimate=cost(us),
        name="expert_grad",
    )(*lefts, right, *held)


def body(
    tokens,
    lengths,
    routes,
    route_gates,
    cotangent,
    norm_first,
    attention_in,
    attention_out,
    norm_second,
    expert_gate,
    expert_lift,
    expert_down,
):
    count = tokens.shape[1]
    width = tokens.shape[2]
    choose = routes.shape[2]
    seq_count = lax.axis_size("seq")
    inner_count = lax.axis_size("inner")
    owners = seq_count * inner_count
    per_owner = EXPERTS // owners
    ff = expert_gate.shape[2]
    query_width = HEADS * HEAD_DIM
    seq_at = lax.axis_index("seq")
    layer_at = seq_at * inner_count + lax.axis_index("inner")
    length = lengths[0]
    place = jnp.stack([seq_at.astype(jnp.int32), length - seq_at.astype(jnp.int32) * count])
    live_rows = seq_at * count + jnp.arange(count, dtype=jnp.int32) < length
    inputs = tokens[0].astype(F32)
    upstream_low = cotangent[0]
    upstream = upstream_low.astype(F32)

    outer_count = lax.axis_size("outer")
    outer_at = lax.axis_index("outer")
    shard = width // (outer_count * inner_count)
    qkv = attention_in.shape[1]
    gains = jnp.concatenate([norm_first[:, None], norm_second[:, None], jnp.zeros((shard, 126), BF)], axis=1)
    project_in = lax.all_gather(jnp.concatenate([attention_in, gains], axis=1), ROWS, axis=0, tiled=True)
    project_out = lax.all_gather(attention_out, ROWS, axis=0, tiled=True)

    seq_place = seq_at.astype(jnp.int32)[None]
    expert_place = jnp.stack([layer_at.astype(jnp.int32), outer_at.astype(jnp.int32)])
    packed = pack_experts(seq_place, expert_gate, expert_lift, expert_down, inner_count)
    got = [exchange_start(part) for part in packed]
    packed = [exchange_end(*pair).reshape(inner_count * shard, 3 * ff) for pair in zip(packed, got)]
    gathered = [lax.all_gather(packed[0], "outer", axis=0, tiled=True)]
    gathered.append(lax.all_gather(after(packed[1], gathered[0][:8, :128]), "outer", axis=0, tiled=True))

    chosen = (
        routes[0][:, :, None] == jnp.arange(EXPERTS, dtype=jnp.int32)[None, None, :]
    ) & live_rows[:, None, None]
    combine = jnp.sum(jnp.where(chosen, route_gates[0][:, :, None], 0.0), axis=1)
    combine_high = combine.astype(BF)
    combine_low = (combine - combine_high.astype(F32)).astype(BF)
    up_block = jnp.concatenate(
        [upstream_low, combine_high, combine_low, jnp.zeros((count, 128 - 2 * EXPERTS), BF)], axis=1
    )
    half = count // 2
    up_block = after(up_block, packed)
    up_across, up_beside, up_sibling = seq_swap(up_block), side_swap(up_block), core_swap(up_block)

    up_pair_across = (up_across, core_swap(up_across))
    up_pair_beside = (up_beside, core_swap(up_beside))
    query, pair_a, pair_b, lowered_one, gains = project_rows(tokens[0], project_in, qkv, 0)
    past_a = lax.ppermute(pair_a, "seq", [(0, 1)])
    late_pair, past_a = lax.optimization_barrier((pair_b, past_a))
    past_b = lax.ppermute(late_pair, "seq", [(0, 1)])
    mixed, stats_a = attend(place, query, pair_a, past_a, 0)
    mixed, stats_b = attend(place, query, pair_b, past_b, stats_a.shape[0], (mixed,))
    middle, lowered_two = merge_rows(mixed, project_out, tokens[0], gains)

    across, beside, sibling = seq_swap(lowered_two), side_swap(lowered_two), core_swap(lowered_two)

    def experts(e, at, rows, up, held, earlier=(), us=1):
        return expert_rows(expert_place, e, rows, up, gathered[e], at, 4, held, earlier, us)

    def upper(block, more):
        return jnp.concatenate([low_plus(block[:half], more), block[half:]])

    def lower(block, more):
        return jnp.concatenate([block[:half], low_plus(block[half:], more)])

    lowered_two, across, beside, up_beside, up_across = lax.optimization_barrier(
        (lowered_two, across, beside, up_beside, up_across)
    )
    row_own, up_own = (lowered_two, sibling), (up_block, up_sibling)
    far_top, far_low = seq_swap(beside[:half]), side_swap(across[half:])
    up_far_top, up_far_low = seq_swap(up_beside[:half]), side_swap(up_across[half:])
    row_across = (across, core_swap(across))
    row_beside = (beside, core_swap(beside))
    made_own = experts(0, 0, row_own, up_own, ())
    made_across = experts(0, 1, row_across, up_pair_across, made_own[:2])
    made_beside = experts(0, 2, row_beside, up_pair_beside, made_across[:2])
    far_top, far_low, up_far_top, up_far_low, held = lax.optimization_barrier(
        (far_top, far_low, up_far_top, up_far_low, made_beside[:2])
    )
    up_far = jnp.concatenate([up_far_top, up_far_low], axis=0)
    up_pair_far = (up_far, core_swap(up_far))
    far = jnp.concatenate([far_top, far_low], axis=0)
    row_far = (far, core_swap(far))
    made_far = experts(0, 3, row_far, up_pair_far, held)
    hidden_a, grads_a = made_far[:2]

    row_all = (*row_own, *row_across, *row_beside, *row_far)
    up_all = (*up_own, *up_pair_across, *up_pair_beside, *up_pair_far)

    def home(total):
        return lax.psum_scatter(total, "outer", scatter_dimension=0, tiled=True)

    def slots(local):
        return local.reshape(inner_count, shard, local.shape[1])

    total_a = expert_grad(row_all, grads_a, width, 3 * ff, 0, 1)
    total_a = expert_grad(up_all, hidden_a, width, 3 * ff, 2, 1, (total_a,))
    home_a = home(total_a)
    far_parts = after(made_far[2:], total_a)

    made_far = experts(1, 3, row_far, up_pair_far, (), far_parts)
    far_got, far_out_got = core_swap(made_far[5]), core_swap(made_far[3])
    made_across = experts(1, 1, row_across, up_pair_across, made_far[:2], made_across[2:])
    across_got, across_out_got = core_swap(made_across[5]), core_swap(made_across[3])
    far_got, far_out_got, held = lax.optimization_barrier((far_got, far_out_got, made_across[:2]))
    far_sum, far_out, held = lax.optimization_barrier(
        (low_plus(made_far[4], far_got), low_plus(made_far[2], far_out_got), held)
    )
    back_low, back_top = side_swap(far_sum[half:]), seq_swap(far_sum[:half])
    made_beside = experts(1, 2, row_beside, up_pair_beside, held, made_beside[2:], 15)
    beside_got, beside_out_got = core_swap(made_beside[5]), core_swap(made_beside[3])
    across_got, across_out_got, back_low, back_top, held = lax.optimization_barrier(
        (across_got, across_out_got, back_low, back_top, made_beside[:2])
    )
    across_sum, out_across, held = lax.optimization_barrier(
        (lower(low_plus(made_across[4], across_got), back_low), low_plus(made_across[2], across_out_got), held)
    )
    across_in = seq_swap(across_sum)
    made_own = experts(1, 0, row_own, up_own, held, made_own[2:], 15)
    hidden_b, grads_b = made_own[:2]
    own_got = core_swap(made_own[5])
    beside_got, beside_out_got, grads_b = lax.optimization_barrier((beside_got, beside_out_got, grads_b))
    beside_sum, out_beside, grads_b = lax.optimization_barrier(
        (
            upper(low_plus(made_beside[4], beside_got), back_top),
            low_plus(made_beside[2], beside_out_got),
            grads_b,
        )
    )
    beside_in = side_swap(beside_sum)
    out_low, out_top = side_swap(far_out[half:]), seq_swap(far_out[:half])

    total_b = expert_grad(row_all, grads_b, width, 3 * ff, 0, 1)
    total_b = expert_grad(up_all, hidden_b, width, 3 * ff, 2, 1, (total_b,))
    home_b = home(total_b)
    across_in, beside_in, own_got, _ = lax.optimization_barrier((across_in, beside_in, own_got, total_b))

    middle_grad, branch_grad, mixed_grad, second_gain_grad = middle_back(
        made_own[4], own_got, across_in, beside_in, middle, upstream_low, gains, project_out, query_width
    )
    second_gain_grad = second_gain_grad[0]
    chain = Chain(mixed_grad)
    own_out_got = core_swap(chain.enter(made_own[3]))
    out_top, out_low = chain.enter((out_top, out_low))
    out_across, out_beside = lower(out_across, out_low), upper(out_beside, out_top)
    out_across, out_beside = chain.leave(lax.optimization_barrier((out_across, out_beside)))
    out_across_in, out_beside_in = seq_swap(out_across), side_swap(out_beside)
    def back(pair, past, stats, first):
        return attend_back(
            chain.enter(place), query, pair, past, mixed, mixed_grad, stats, first, stats.shape[0], 24
        )

    query_a, key_a, value_a, key_past_a, value_past_a = chain.leave(back(pair_a, past_a, stats_a, 0))
    late_a = lax.ppermute(jnp.concatenate([key_past_a, value_past_a], axis=1), "seq", [(1, 0)])
    out_home = HomeSum(chain.leave(dot_tn(chain.enter(mixed), branch_grad).astype(BF)))
    out_across_in, out_beside_in, own_out_got = chain.enter((out_across_in, out_beside_in, own_out_got))
    combined = (
        made_own[2].astype(F32) + own_out_got.astype(F32) + out_across_in.astype(F32) + out_beside_in.astype(F32)
    )
    block_output = chain.leave((middle + combined[:, :width]).astype(BF))[None]
    dots = combined[:, width : width + EXPERTS] + combined[:, width + EXPERTS : width + 2 * EXPERTS]
    grad_gates = chain.leave(jnp.sum(jnp.where(chosen, chain.enter(dots)[:, None, :], 0.0), axis=-1))[None]
    out_home.got = chain.enter(out_home.got)
    chain.leave(out_home.beside())
    a_slots = slots(home_a)
    a_mine = chain.leave(exchange_end(a_slots, chain.enter(exchange_start(a_slots))))
    late_a = chain.leave(chain.enter(late_a))
    a_other = seq_swap(a_mine)
    query_b, key_b, value_b, key_past_b, value_past_b = chain.leave(
        back(pair_b, past_b, stats_b, stats_a.shape[0])
    )
    late_b = lax.ppermute(jnp.concatenate([key_past_b, value_past_b], axis=1), "seq", [(1, 0)])
    a_other = chain.enter(a_other)
    out_home.got = chain.enter(out_home.got)
    chain.leave((out_home.across(), a_other))
    query_grad = jnp.concatenate([query_a, query_b], axis=1)
    query_home = HomeSum(chain.leave(dot_tn(chain.enter(lowered_one), query_grad).astype(BF)))
    query_home.got = chain.enter(query_home.got)
    chain.leave(query_home.beside())
    late_b = chain.enter(late_b)
    pair_grad, pair_weight = chain.leave(
        pair_back(chain.enter(lowered_one), key_a, key_b, value_a, value_b, late_a, late_b)
    )
    pair_part = lax.psum_scatter(pair_weight, ROWS, scatter_dimension=0, tiled=True)
    query_home.got = chain.enter(query_home.got)
    chain.leave(query_home.across())
    b_slots = slots(chain.enter(home_b))
    b_got = exchange_start(b_slots)
    projected_grad = jnp.concatenate([query_grad, pair_grad], axis=1)
    normed_grad_one = chain.leave(dot_nt(chain.enter(projected_grad), project_in[:, :qkv]))
    query_home.got = chain.enter(query_home.got)
    chain.leave(query_home.along())
    b_mine = chain.leave(exchange_end(b_slots, chain.enter(b_got)))
    normed_one, inverse_one, _ = norm_rows(inputs, gains[0])
    input_norm_grad, first_gain_grad = norm_back(chain.enter(normed_grad_one), normed_one, inverse_one, gains[0])
    grad_tokens = chain.leave(middle_grad + input_norm_grad)[None]
    b_other = seq_swap(b_mine)

    gain_grads = jnp.stack([first_gain_grad, second_gain_grad])
    gain_grads = gain_grads + core_swap(gain_grads)
    out_home.got = chain.enter(out_home.got)
    chain.leave(out_home.along())
    gain_grads = chain.leave(chain.enter(gain_grads))
    gain_grads = gain_grads + side_swap(gain_grads)
    query_home.got = chain.enter(query_home.got)
    chain.leave(query_home.final())
    gain_grads = chain.leave(chain.enter(gain_grads)).reshape(2, outer_count, inner_count * shard)
    gain_sum = pick(gain_grads, outer_at, 1)
    for step in range(1, outer_count):
        piece = pick(gain_grads, lax.rem(outer_at + step, outer_count), 1)
        gain_sum = gain_sum + lax.ppermute(
            piece, "outer", [(i, (i + step) % outer_count) for i in range(outer_count)]
        )
    out_home.got = chain.enter(out_home.got)
    chain.leave(out_home.final())
    gain_sum = chain.leave(pick(chain.enter(gain_sum).reshape(2, inner_count, shard), lax.axis_index("inner"), 1))
    gain_sum = gain_sum + seq_swap(gain_sum)
    parts = chain.enter((a_mine, a_other, b_mine, b_other))
    grads = [unpack_experts(seq_place, parts, kind, ff) for kind in range(3)]
    grad_gate, grad_lift, grad_down = chain.leave(lax.optimization_barrier(tuple(grads)))
    out_home.other, query_home.other = chain.enter((out_home.other, query_home.other))
    grad_out = chain.leave(out_home.result())
    pair_part = chain.enter(pair_part)
    pair_sum = pair_part.astype(F32) + seq_swap(pair_part).astype(F32)
    grad_in = jnp.concatenate([query_home.result(), pair_sum], axis=1)
    return (
        block_output,
        grad_tokens,
        grad_gates,
        gain_sum[0],
        grad_in,
        grad_out,
        gain_sum[1],
        grad_gate,
        grad_lift,
        grad_down,
    )


def solution(mesh):
    seq_count, fsdp_count = mesh.devices.shape
    inner_count = EXPERTS // (2 * seq_count)
    fine = jax.sharding.Mesh(
        mesh.devices.reshape(seq_count, fsdp_count // inner_count, inner_count), ("seq", "outer", "inner")
    )
    return jax.shard_map(
        body,
        mesh=fine,
        in_specs=(
            P(ROWS, "seq", None),
            P(ROWS),
            P(ROWS, "seq", None),
            P(ROWS, "seq", None),
            P(ROWS, "seq", None),
            P(ROWS),
            P(ROWS, None),
            P(ROWS, None),
            P(ROWS),
            P(ROWS, None, None),
            P(ROWS, None, None),
            P(ROWS, None, None),
        ),
        out_specs=(
            P(ROWS, "seq", None),
            P(ROWS, "seq", None),
            P(ROWS, "seq", None),
            P(ROWS),
            P(ROWS, None),
            P(ROWS, None),
            P(ROWS),
            P(ROWS, None, None),
            P(ROWS, None, None),
            P(ROWS, None, None),
        ),
        check_vma=False,
    )
```

```python
import functools

import jax
import jax.numpy as jnp
from jax import lax
from jax.experimental import pallas as pl
from jax.experimental.pallas import tpu as pltpu
from jax.sharding import PartitionSpec as P

HEADS = 24
KV_HEADS = 8
HEAD_DIM = 64
EXPERTS = 16
GROUP = HEADS // KV_HEADS
EPS = 1e-06
BF = jnp.bfloat16
F32 = jnp.float32
ROWS = ("outer", "inner")
VMEM_LIMIT = 60 * 1024 * 1024


def cost(microseconds):
    return pl.CostEstimate(flops=int(microseconds * 0.6e9), bytes_accessed=1000, transcendentals=0)


def norm_rows(values, gain_vector):
    inverse = lax.rsqrt(jnp.mean(values * values, axis=-1, keepdims=True) + EPS)
    normed = values * inverse
    return (normed, inverse, (normed * gain_vector).astype(BF))


def norm_back(upstream, normed, inverse, gain_vector):
    scaled = upstream * gain_vector
    spread = jnp.mean(scaled * normed, axis=-1, keepdims=True)
    return (inverse * (scaled - normed * spread), jnp.sum(upstream * normed, axis=0))


def swap(x, axis, bit):
    return lax.ppermute(x, axis, [(i, i ^ bit) for i in range(lax.axis_size(axis))])


def core_swap(x):
    return swap(x, "inner", 1)


def side_swap(x):
    return swap(x, "inner", 2)


def seq_swap(x):
    return swap(x, "seq", 1)


def after(x, *others):
    return lax.optimization_barrier((x, others))[0]


def low_plus(a, b):
    return (a.astype(F32) + b.astype(F32)).astype(BF)


def exchange_start(pieces):
    at = lax.axis_index("inner")
    bits = range(1, lax.axis_size("inner"))
    return [swap(lax.dynamic_index_in_dim(pieces, at ^ bit, 0, keepdims=False), "inner", bit) for bit in bits]


def exchange_end(pieces, got):
    at = lax.axis_index("inner")
    for bit, piece in enumerate(got, 1):
        pieces = lax.dynamic_update_index_in_dim(pieces, piece, at ^ bit, 0)
    return pieces


def pick(x, at, axis):
    return lax.dynamic_index_in_dim(x, at, axis, keepdims=False)


class HomeSum:
    def __init__(self, *totals):
        rows, columns = totals[0].shape[0], sum(total.shape[1] for total in totals)
        self.n = lax.axis_size("outer")
        self.seq_at = lax.axis_index("seq")
        self.outer_at = lax.axis_index("outer")
        inner_at = lax.axis_index("inner")
        sides = lax.axis_size("inner") // 2
        self.side_at, core_at = inner_at // 2, inner_at % 2
        self.half = columns // 2
        self.split = False
        part = rows // (self.n * sides * 2)

        def half_of(at):
            return jnp.concatenate(
                [pick(total.reshape(self.n, sides, 2, part, total.shape[1]), at, 2) for total in totals], axis=-1
            )

        self.held = half_of(core_at)
        self.got = core_swap(half_of(1 - core_at))

    def beside(self):
        held = low_plus(self.held, self.got)
        self.got = side_swap(pick(held, 1 - self.side_at, 1))
        self.held = pick(held, self.side_at, 1)
        return held

    def across(self):
        held = low_plus(self.held, self.got)
        self.got = seq_swap(lax.dynamic_slice_in_dim(held, (1 - self.seq_at) * self.half, self.half, 2))
        self.held = lax.dynamic_slice_in_dim(held, self.seq_at * self.half, self.half, 2)
        self.split = True
        return held

    def along(self):
        held = low_plus(self.held, self.got)
        self.held = pick(held, self.outer_at, 0)
        self.got = []
        for step in range(1, self.n):
            piece = pick(held, lax.rem(self.outer_at + step, self.n), 0)
            self.got.append(lax.ppermute(piece, "outer", [(i, (i + step) % self.n) for i in range(self.n)]))
        return held

    def final(self):
        result = self.held.astype(F32)
        for got in self.got:
            result = result + got.astype(F32)
        self.low = result.astype(BF)
        self.other = seq_swap(self.low)
        return self.low

    def result(self):
        low, other = self.low.astype(F32), self.other.astype(F32)
        if not self.split:
            return low + other
        first = self.seq_at == 0
        return jnp.concatenate([jnp.where(first, low, other), jnp.where(first, other, low)], axis=1)


class Chain:
    def __init__(self, last):
        self.last = last

    def enter(self, x):
        return after(x, self.last)

    def leave(self, y):
        self.last = y
        return y


def dot_nt(a, b):
    return lax.dot_general(a, b, (((1,), (1,)), ((), ())), preferred_element_type=F32)


def dot_nn(a, b):
    return lax.dot_general(a, b, (((1,), (0,)), ((), ())), preferred_element_type=F32)


def dot_tn(a, b):
    return lax.dot_general(a, b, (((0,), (0,)), ((), ())), preferred_element_type=F32)


def project_in_kernel(token_ref, weight_ref, tail_ref, query_ref, paira_ref, pairb_ref, low_ref, gain_ref):
    step = pl.program_id(0)
    queries = HEADS * HEAD_DIM // weight_ref.shape[1]

    @pl.when(step == 0)
    def _():
        row = lax.broadcasted_iota(jnp.int32, (8, 128), 0)
        lane = lax.broadcasted_iota(jnp.int32, (8, 128), 1)
        gain_ref[...] = dot_nt((row == lane).astype(BF), tail_ref[...])
        x = token_ref[...].astype(F32)
        inverse = lax.rsqrt(jnp.mean(x * x, axis=-1, keepdims=True) + EPS)
        low_ref[...] = (x * inverse * gain_ref[0:1, :]).astype(BF)

    result = dot_nn(low_ref[...], weight_ref[...]).astype(BF)

    @pl.when(step < queries)
    def _():
        query_ref[...] = result

    half = result.shape[1] // 2
    for part in range(2):

        @pl.when(step == queries + part)
        def _():
            cols = slice(part * half, (part + 1) * half)
            paira_ref[:, cols] = result[:, :half]
            pairb_ref[:, cols] = result[:, half:]


def project_rows(tokens, weight, qkv, before):
    count, width = tokens.shape
    tile = 512
    query_width = HEADS * HEAD_DIM
    queries = query_width // tile
    return pl.pallas_call(
        project_in_kernel,
        grid=(qkv // tile,),
        in_specs=[
            pl.BlockSpec((count, width), lambda j: (0, 0)),
            pl.BlockSpec((width, tile), lambda j: (0, before // tile + j)),
            pl.BlockSpec((width, 128), lambda j: (0, (before + qkv) // 128)),
        ],
        out_specs=[
            pl.BlockSpec((count, tile), lambda j: (0, jnp.minimum(j, queries - 1))),
            pl.BlockSpec((count, tile), lambda j: (0, 0)),
            pl.BlockSpec((count, tile), lambda j: (0, 0)),
            pl.BlockSpec((count, width), lambda j: (0, 0)),
            pl.BlockSpec((8, width), lambda j: (0, 0)),
        ],
        out_shape=[
            jax.ShapeDtypeStruct((count, query_width), BF),
            jax.ShapeDtypeStruct((count, tile), BF),
            jax.ShapeDtypeStruct((count, tile), BF),
            jax.ShapeDtypeStruct((count, width), BF),
            jax.ShapeDtypeStruct((8, width), F32),
        ],
        compiler_params=pltpu.CompilerParams(vmem_limit_bytes=VMEM_LIMIT),
        cost_estimate=cost(0),
        name="project_rows",
    )(tokens, weight, weight)


def merge_kernel(mixed_ref, weight_ref, token_ref, gain_ref, middle_ref, low_ref):
    product = dot_nn(mixed_ref[...], weight_ref[...])
    step = pl.program_id(0)

    @pl.when(step == 0)
    def _():
        middle_ref[...] = token_ref[...].astype(F32) + product

    @pl.when(step > 0)
    def _():
        middle_ref[...] += product

    @pl.when(step == pl.num_programs(0) - 1)
    def _():
        x = middle_ref[...]
        inverse = lax.rsqrt(jnp.mean(x * x, axis=-1, keepdims=True) + EPS)
        low_ref[...] = (x * inverse * gain_ref[1:2, :]).astype(BF)


def merge_rows(mixed, weight, tokens, gains):
    count, width = tokens.shape
    tile = 512
    whole = pl.BlockSpec((count, width), lambda j: (0, 0))
    return pl.pallas_call(
        merge_kernel,
        grid=(mixed.shape[1] // tile,),
        in_specs=[
            pl.BlockSpec((count, tile), lambda j: (0, j)),
            pl.BlockSpec((tile, width), lambda j: (j, 0)),
            whole,
            pl.BlockSpec((8, width), lambda j: (0, 0)),
        ],
        out_specs=[whole, whole],
        out_shape=[jax.ShapeDtypeStruct((count, width), F32), jax.ShapeDtypeStruct((count, width), BF)],
        compiler_params=pltpu.CompilerParams(vmem_limit_bytes=VMEM_LIMIT),
        cost_estimate=cost(0),
        name="merge_rows",
    )(mixed, weight, tokens, gains)


def middle_back_kernel(
    own_ref, got_ref, across_ref, beside_ref, middle_ref, up_ref, gain_ref, weight_ref,
    grad_ref, low_ref, mixed_ref, sum_ref,
):
    @pl.when(pl.program_id(0) == 0)
    def _():
        above = own_ref[...].astype(F32) + got_ref[...].astype(F32)
        above = above + across_ref[...].astype(F32) + beside_ref[...].astype(F32)
        x = middle_ref[...]
        inverse = lax.rsqrt(jnp.mean(x * x, axis=-1, keepdims=True) + EPS)
        normed = x * inverse
        scaled = above * gain_ref[1:2, :]
        spread = jnp.mean(scaled * normed, axis=-1, keepdims=True)
        grad = up_ref[...].astype(F32) + inverse * (scaled - normed * spread)
        grad_ref[...] = grad
        low_ref[...] = grad.astype(BF)
        sum_ref[...] = jnp.broadcast_to(jnp.sum(above * normed, axis=0, keepdims=True), sum_ref.shape)

    mixed_ref[...] = dot_nt(low_ref[...], weight_ref[...]).astype(BF)


def middle_back(own, got, across, beside, middle, up, gains, weight, columns):
    count, width = own.shape
    tile = 512
    whole = pl.BlockSpec((count, width), lambda j: (0, 0))
    row = pl.BlockSpec((8, width), lambda j: (0, 0))
    return pl.pallas_call(
        middle_back_kernel,
        grid=(columns // tile,),
        in_specs=[whole] * 6 + [row, pl.BlockSpec((tile, width), lambda j: (j, 0))],
        out_specs=[whole, whole, pl.BlockSpec((count, tile), lambda j: (0, j)), row],
        out_shape=[
            jax.ShapeDtypeStruct((count, width), F32),
            jax.ShapeDtypeStruct((count, width), BF),
            jax.ShapeDtypeStruct((count, columns), BF),
            jax.ShapeDtypeStruct((8, width), F32),
        ],
        compiler_params=pltpu.CompilerParams(vmem_limit_bytes=VMEM_LIMIT),
        cost_estimate=cost(1),
        name="middle_back",
    )(own, got, across, beside, middle, up, gains, weight)


def attend_kernel(place_ref, q_ref, k_ref, v_ref, kr_ref, vr_ref, *refs):
    mixed_ref, stat_ref, bias_ref, col_ref = refs[-4:]
    count = q_ref.shape[0]
    half = count // 2
    seq_at = place_ref[0]
    live = place_ref[1]

    @pl.when(pl.program_id(0) == 0)
    def _():
        row = lax.broadcasted_iota(jnp.int32, (count, count), 0)
        col = lax.broadcasted_iota(jnp.int32, (count, count), 1)
        bias_ref[...] = jnp.where((col <= row) & (col < live), 0.0, -jnp.inf)
        col_ref[...] = jnp.zeros_like(col_ref)

    def run(with_past):
        for g in range(2):
            lanes = slice(g * HEAD_DIM, (g + 1) * HEAD_DIM)
            key = k_ref[:, lanes]
            value = v_ref[:, lanes]
            if with_past:
                key_past = kr_ref[:, lanes]
                value_past = vr_ref[:, lanes]
            for r in range(GROUP):
                h = g * GROUP + r
                for part in range(2):
                    rows = slice(part * half, (part + 1) * half)
                    span = (part + 1) * half
                    query = q_ref[rows, h * HEAD_DIM : (h + 1) * HEAD_DIM] * BF(HEAD_DIM**-0.5)
                    scores = dot_nt(query, key[:span]) + bias_ref[rows, :span]
                    peak = jnp.max(scores, axis=-1, keepdims=True)
                    if with_past:
                        past = dot_nt(query, key_past)
                        peak = jnp.maximum(peak, jnp.max(past, axis=-1, keepdims=True))
                    lifted = jnp.exp(scores - peak)
                    total = jnp.sum(lifted, axis=-1, keepdims=True)
                    mixed = dot_nn(lifted.astype(BF), value[:span])
                    if with_past:
                        lifted_past = jnp.exp(past - peak)
                        total = total + jnp.sum(lifted_past, axis=-1, keepdims=True)
                        mixed = mixed + dot_nn(lifted_past.astype(BF), value_past)
                    mixed_ref[rows, h * HEAD_DIM : (h + 1) * HEAD_DIM] = (mixed / total).astype(BF)
                    col_ref[rows, h : h + 1] = peak + jnp.log(total)

    @pl.when(seq_at == 0)
    def _():
        run(False)

    @pl.when(seq_at != 0)
    def _():
        run(True)

    stat_ref[...] = col_ref[...].T[:8, :]


def attend(place, query, pair, past, first, held=()):
    count = query.shape[0]
    steps = pair.shape[1] // 256
    wide = 2 * GROUP * HEAD_DIM
    return pl.pallas_call(
        attend_kernel,
        grid_spec=pltpu.PrefetchScalarGridSpec(
            num_scalar_prefetch=1,
            grid=(steps,),
            in_specs=[
                pl.BlockSpec((count, wide), lambda j, place: (0, first + j)),
                pl.BlockSpec((count, 128), lambda j, place: (0, j)),
                pl.BlockSpec((count, 128), lambda j, place: (0, steps + j)),
                pl.BlockSpec((count, 128), lambda j, place: (0, j)),
                pl.BlockSpec((count, 128), lambda j, place: (0, steps + j)),
            ]
            + [pl.BlockSpec(memory_space=pl.ANY)] * len(held),
            out_specs=[
                pl.BlockSpec((count, wide), lambda j, place: (0, first + j)),
                pl.BlockSpec((None, 8, count), lambda j, place: (j, 0, 0)),
            ],
            scratch_shapes=[pltpu.VMEM((count, count), F32), pltpu.VMEM((count, 128), F32)],
        ),
        out_shape=[
            jax.ShapeDtypeStruct((count, HEADS * HEAD_DIM), BF),
            jax.ShapeDtypeStruct((steps, 8, count), F32),
        ],
        input_output_aliases={6: 0} if held else {},
        compiler_params=pltpu.CompilerParams(vmem_limit_bytes=VMEM_LIMIT),
        cost_estimate=cost(0),
        name="attend",
    )(place, query, pair, pair, past, past, *held)


def attend_back_kernel(
    place_ref, q_ref, k_ref, v_ref, kr_ref, vr_ref, mixed_ref, grad_ref, stat_ref,
    dq_ref, dk_ref, dv_ref, dkr_ref, dvr_ref, bias_ref,
):
    count = q_ref.shape[0]
    half = count // 2
    seq_at = place_ref[0]
    live = place_ref[1]
    scale = HEAD_DIM**-0.5

    @pl.when(pl.program_id(0) == 0)
    def _():
        key_at = lax.broadcasted_iota(jnp.int32, (count, count), 0)
        query_at = lax.broadcasted_iota(jnp.int32, (count, count), 1)
        bias_ref[...] = jnp.where((key_at <= query_at) & (key_at < live), 0.0, -jnp.inf)

    def run(with_past):
        for g in range(2):
            lanes = slice(g * HEAD_DIM, (g + 1) * HEAD_DIM)
            key = k_ref[:, lanes]
            value = v_ref[:, lanes]
            sums = [[jnp.zeros((half, HEAD_DIM), F32) for _ in range(2)] for _ in range(2)]
            if with_past:
                key_past = kr_ref[:, lanes]
                value_past = vr_ref[:, lanes]
                past_sums = [jnp.zeros((count, HEAD_DIM), F32) for _ in range(2)]
            for r in range(GROUP):
                h = g * GROUP + r
                cols = slice(h * HEAD_DIM, (h + 1) * HEAD_DIM)
                query = q_ref[:, cols] * BF(scale)
                grad = grad_ref[:, cols]
                product = grad.astype(F32) * mixed_ref[:, cols].astype(F32)
                delta = lax.dot_general(
                    jnp.ones((8, HEAD_DIM), F32), product, (((1,), (1,)), ((), ())),
                    precision=lax.Precision.HIGHEST, preferred_element_type=F32,
                )[:1]
                stat = stat_ref[h : h + 1, :]

                def piece(keys, values, queries, grads, stats, deltas, bias):
                    scores = dot_nt(keys, queries)
                    if bias is not None:
                        scores = scores + bias
                    chances = jnp.exp(scores - stats)
                    chance_grad = dot_nt(values, grads)
                    score_grad = (chances * (chance_grad - deltas)).astype(BF)
                    return chances.astype(BF), score_grad

                p0, s0 = piece(key[:half], value[:half], query, grad, stat, delta, bias_ref[:half, :])
                p1, s1 = piece(
                    key[half:], value[half:], query[half:], grad[half:], stat[:, half:], delta[:, half:],
                    bias_ref[half:, half:],
                )
                dq = dot_tn(s0, key[:half])
                dq_late = dot_tn(s1, key[half:])
                sums[0][0] += dot_nn(s0, query)
                sums[0][1] += dot_nn(s1, query[half:])
                sums[1][0] += dot_nn(p0, grad)
                sums[1][1] += dot_nn(p1, grad[half:])
                if with_past:
                    pp, sp = piece(key_past, value_past, query, grad, stat, delta, None)
                    dq = dq + dot_tn(sp, key_past)
                    past_sums[0] += dot_nn(sp, query)
                    past_sums[1] += dot_nn(pp, grad)
                dq_ref[:half, cols] = (dq[:half] * scale).astype(BF)
                dq_ref[half:, cols] = ((dq[half:] + dq_late) * scale).astype(BF)
            for where, out in ((0, dk_ref), (1, dv_ref)):
                out[:half, lanes] = sums[where][0].astype(BF)
                out[half:, lanes] = sums[where][1].astype(BF)
            if with_past:
                dkr_ref[:, lanes] = past_sums[0].astype(BF)
                dvr_ref[:, lanes] = past_sums[1].astype(BF)

    @pl.when(seq_at == 0)
    def _():
        run(False)
        dkr_ref[...] = jnp.zeros_like(dkr_ref)
        dvr_ref[...] = jnp.zeros_like(dvr_ref)

    @pl.when(seq_at != 0)
    def _():
        run(True)


def attend_back(place, query, pair, past, mixed, mixed_grad, stats, first, steps, us):
    count = query.shape[0]
    wide = 2 * GROUP * HEAD_DIM
    narrow = jax.ShapeDtypeStruct((count, steps * 128), BF)
    head_spec = pl.BlockSpec((count, wide), lambda j, place: (0, first + j))
    pair_spec = pl.BlockSpec((count, 128), lambda j, place: (0, j))
    return pl.pallas_call(
        attend_back_kernel,
        grid_spec=pltpu.PrefetchScalarGridSpec(
            num_scalar_prefetch=1,
            grid=(steps,),
            in_specs=[
                head_spec,
                pl.BlockSpec((count, 128), lambda j, place: (0, j)),
                pl.BlockSpec((count, 128), lambda j, place: (0, steps + j)),
                pl.BlockSpec((count, 128), lambda j, place: (0, j)),
                pl.BlockSpec((count, 128), lambda j, place: (0, steps + j)),
                head_spec,
                head_spec,
                pl.BlockSpec((None, 8, count), lambda j, place: (j, 0, 0)),
            ],
            out_specs=[pl.BlockSpec((count, wide), lambda j, place: (0, j))] + [pair_spec] * 4,
            scratch_shapes=[pltpu.VMEM((count, count), F32)],
        ),
        out_shape=[jax.ShapeDtypeStruct((count, steps * wide), BF), narrow, narrow, narrow, narrow],
        compiler_params=pltpu.CompilerParams(vmem_limit_bytes=VMEM_LIMIT),
        cost_estimate=cost(us),
        name="attend_back",
    )(place, query, pair, pair, past, past, mixed, mixed_grad, stats)


def pair_kernel(low_ref, keya_ref, keyb_ref, valuea_ref, valueb_ref, latea_ref, lateb_ref, pair_ref, grad_ref):
    half = keya_ref.shape[1]
    for part, (a_ref, b_ref) in enumerate(((keya_ref, keyb_ref), (valuea_ref, valueb_ref))):

        @pl.when(pl.program_id(0) == part)
        def _():
            cols = slice(part * half, (part + 1) * half)
            pair_ref[:, :half] = (a_ref[...].astype(F32) + latea_ref[:, cols].astype(F32)).astype(BF)
            pair_ref[:, half:] = (b_ref[...].astype(F32) + lateb_ref[:, cols].astype(F32)).astype(BF)

    grad_ref[...] = dot_tn(low_ref[...], pair_ref[...]).astype(BF)


def pair_back(low, key_a, key_b, value_a, value_b, late_a, late_b):
    count, width = low.shape
    half = key_a.shape[1]

    def whole(x):
        return pl.BlockSpec(x.shape, lambda j: (0, 0))

    args = (low, key_a, key_b, value_a, value_b, late_a, late_b)
    return pl.pallas_call(
        pair_kernel,
        grid=(2,),
        in_specs=[whole(x) for x in args],
        out_specs=[
            pl.BlockSpec((count, 2 * half), lambda j: (0, j)),
            pl.BlockSpec((width, 2 * half), lambda j: (0, j)),
        ],
        out_shape=[
            jax.ShapeDtypeStruct((count, 4 * half), BF),
            jax.ShapeDtypeStruct((width, 4 * half), BF),
        ],
        compiler_params=pltpu.CompilerParams(vmem_limit_bytes=VMEM_LIMIT),
        cost_estimate=cost(0),
        name="pair_back",
    )(*args)


def pack_kernel(seq_ref, gate_ref, lift_ref, down_ref, *out_refs):
    owners, _, columns = out_refs[0].shape
    ff = columns // 3
    for seq in range(2):

        @pl.when(seq_ref[0] == seq)
        def _():
            for kind, ref in enumerate((gate_ref, lift_ref, down_ref)):
                for owner in range(owners):
                    for e in range(2):
                        out_refs[e][owner, :, kind * ff : (kind + 1) * ff] = ref[:, (seq * owners + owner) * 2 + e, :]


def pack_experts(seq, gate, lift, down, owners):
    rows, experts, ff = gate.shape
    tile = 32 if rows % 32 == 0 else rows
    in_spec = pl.BlockSpec((tile, experts, ff), lambda i, seq: (i, 0, 0))
    out_spec = pl.BlockSpec((owners, tile, 3 * ff), lambda i, seq: (0, i, 0))
    out = jax.ShapeDtypeStruct((owners, rows, 3 * ff), BF)
    return pl.pallas_call(
        pack_kernel,
        grid_spec=pltpu.PrefetchScalarGridSpec(
            num_scalar_prefetch=1, grid=(rows // tile,), in_specs=[in_spec] * 3, out_specs=[out_spec] * 2
        ),
        out_shape=[out, out],
        compiler_params=pltpu.CompilerParams(vmem_limit_bytes=VMEM_LIMIT),
        cost_estimate=cost(6),
        name="pack_experts",
    )(seq, gate, lift, down)


def unpack_kernel(seq_ref, *refs):
    out_ref = refs[-1]
    owners = refs[0].shape[0]
    for seq in range(2):

        @pl.when(seq_ref[0] == seq)
        def _():
            for e in range(2):
                for at, ref in ((seq, refs[2 * e]), (1 - seq, refs[2 * e + 1])):
                    for owner in range(owners):
                        out_ref[:, (at * owners + owner) * 2 + e, :] = ref[owner].astype(F32)


def unpack_experts(seq, parts, column, ff):
    owners, rows, _ = parts[0].shape
    in_spec = pl.BlockSpec((owners, rows, ff), lambda i, seq: (0, 0, column))
    return pl.pallas_call(
        unpack_kernel,
        grid_spec=pltpu.PrefetchScalarGridSpec(
            num_scalar_prefetch=1,
            grid=(1,),
            in_specs=[in_spec] * 4,
            out_specs=pl.BlockSpec((rows, EXPERTS, ff), lambda i, seq: (0, 0, 0)),
        ),
        out_shape=jax.ShapeDtypeStruct((rows, EXPERTS, ff), F32),
        compiler_params=pltpu.CompilerParams(vmem_limit_bytes=VMEM_LIMIT),
        cost_estimate=cost(4),
        name="unpack_experts",
    )(seq, *parts)


def expert_kernel(e, blocks, has_earlier, place_ref, *refs):
    rows_refs, up_refs = refs[:blocks], refs[blocks : 2 * blocks]
    if has_earlier:
        earlier_out, earlier_back, wt_ref = refs[2 * blocks : 2 * blocks + 3]
        (ch_ref, gl_ref, outa_ref, outb_ref, backa_ref, backb_ref) = refs[-12:-6]
        n_buf, c_buf, sems, out_buf, back_buf, out_sems = refs[-6:]
    else:
        wt_ref = refs[2 * blocks]
        ch_ref, gl_ref, out_ref, back_ref, n_buf, c_buf, sems = refs[-7:]
    tile, width = n_buf.shape[1:]
    tiles = 2 * blocks
    ff = wt_ref.shape[1] // 3
    step = pl.program_id(0)
    slot = lax.rem(step, 2)
    mine = 2 * place_ref[0] + e
    if has_earlier:
        out_ref, back_ref = out_buf.at[step], back_buf.at[step]

    def fetch(t):
        part = pl.ds((t % 2) * tile, tile)
        return (
            pltpu.make_async_copy(rows_refs[t // 2].at[part], n_buf.at[t % 2], sems.at[0, t % 2]),
            pltpu.make_async_copy(up_refs[t // 2].at[part], c_buf.at[t % 2], sems.at[1, t % 2]),
        )

    @pl.when(step == 0)
    def _():
        for copy in fetch(0):
            copy.start()

    for t in range(tiles):

        @pl.when(step == t)
        def _():
            if t + 1 < tiles:
                for copy in fetch(t + 1):
                    copy.start()
            for copy in fetch(t):
                copy.wait()

    n_ref, c_ref = n_buf.at[slot], c_buf.at[slot]
    packed = c_ref[:, width:].astype(F32)
    lane = lax.broadcasted_iota(jnp.int32, packed.shape, 1)
    g = dot_nn(n_ref[...], wt_ref[:, :ff])
    l = dot_nn(n_ref[...], wt_ref[:, ff : 2 * ff])
    u = dot_nn(c_ref[:, :width], wt_ref[:, 2 * ff :])
    own_lane = (lane == mine) | (lane == EXPERTS + mine)
    weight = jnp.sum(jnp.where(own_lane, packed, 0.0), axis=-1, keepdims=True)
    sig = 1.0 / (1.0 + jnp.exp(-g))
    silu = g * sig
    hidden = silu * l
    dot = jnp.sum(hidden * u, axis=-1, keepdims=True)
    dot_high = dot.astype(BF).astype(F32)
    dots = jnp.where(lane == mine, dot_high, 0.0)
    dots = jnp.where(lane == EXPERTS + mine, dot - dot_high, dots)
    grad = u * weight
    ch_ref[...] = (hidden * weight).astype(BF)
    gl_ref[:, :ff] = (grad * l * (sig + silu * (1.0 - sig))).astype(BF)
    gl_ref[:, ff:] = (grad * silu).astype(BF)
    back = dot_nt(gl_ref[...], wt_ref[:, : 2 * ff])
    out = dot_nt(ch_ref[...], wt_ref[:, 2 * ff :])
    if has_earlier:
        out = out + earlier_out[:, :width].astype(F32)
        dots = dots + earlier_out[:, width:].astype(F32)
        back = back + earlier_back[...].astype(F32)
    back_ref[...] = back.astype(BF)
    out_ref[:, :width] = out.astype(BF)
    out_ref[:, width:] = dots.astype(BF)
    if has_earlier:

        def send(t):
            part = pl.ds((t % 2) * tile, tile)
            to_out, to_back = (outa_ref, backa_ref) if t < 2 else (outb_ref, backb_ref)
            return (
                pltpu.make_async_copy(out_buf.at[t], to_out.at[part], out_sems.at[0, t]),
                pltpu.make_async_copy(back_buf.at[t], to_back.at[part], out_sems.at[1, t]),
            )

        for t in range(tiles):

            @pl.when(step == t)
            def _():
                for copy in send(t):
                    copy.start()

        @pl.when(step == tiles - 1)
        def _():
            for t in range(tiles):
                for copy in send(t):
                    copy.wait()


def expert_rows(place, e, rows, up, packed, chunk, total, held, earlier, us):
    count, width = rows[0].shape
    blocks = len(rows)
    ff = packed.shape[1] // 3
    tile = count // 2
    more = width + 128

    def at_rows(i, place):
        return (4 * chunk + i, 0)

    any_spec = pl.BlockSpec(memory_space=pl.ANY)
    sum_specs = [pl.BlockSpec((tile, more), at_rows), pl.BlockSpec((tile, width), at_rows)]
    packed_spec = pl.BlockSpec((width, 3 * ff), lambda i, place: (0, 0), pipeline_mode=pl.Buffered(1))
    one = jax.ShapeDtypeStruct((count, width), BF)
    one_more = jax.ShapeDtypeStruct((count, more), BF)
    scratch = [pltpu.VMEM((2, tile, width), BF), pltpu.VMEM((2, tile, more), BF), pltpu.SemaphoreType.DMA((2, 2))]
    held, earlier = list(held), list(earlier)
    begin = 2 + 2 * blocks + len(earlier)
    if earlier:
        sums = [one_more] * 2 + [one] * 2
        out_sums = [any_spec] * 4
        scratch += [
            pltpu.VMEM((2 * blocks, tile, more), BF),
            pltpu.VMEM((2 * blocks, tile, width), BF),
            pltpu.SemaphoreType.DMA((2, 2 * blocks)),
        ]
    else:
        sums = [jax.ShapeDtypeStruct((total, more), BF), jax.ShapeDtypeStruct((total, width), BF)]
        out_sums = sum_specs
    return pl.pallas_call(
        functools.partial(expert_kernel, e, blocks, len(earlier) > 0),
        grid_spec=pltpu.PrefetchScalarGridSpec(
            num_scalar_prefetch=1,
            grid=(2 * blocks,),
            in_specs=[any_spec] * (2 * blocks)
            + (sum_specs if earlier else [])
            + [packed_spec]
            + [any_spec] * len(held),
            out_specs=[pl.BlockSpec((tile, ff), at_rows), pl.BlockSpec((tile, 2 * ff), at_rows)] + out_sums,
            scratch_shapes=scratch,
        ),
        out_shape=[jax.ShapeDtypeStruct((total, ff), BF), jax.ShapeDtypeStruct((total, 2 * ff), BF)] + sums,
        input_output_aliases={begin + at: at for at in range(len(held))},
        compiler_params=pltpu.CompilerParams(vmem_limit_bytes=VMEM_LIMIT),
        cost_estimate=cost(us),
        name="expert_rows",
    )(place, *rows, *up, *earlier, packed, *held)


def expert_grad_kernel(*refs):
    out_ref, sum_ref, held_ref, sems = refs[-4:]
    sources, right_ref = refs[:8], refs[8]
    width = held_ref.shape[2]
    step = pl.program_id(0)

    def fetch(at):
        return pltpu.make_async_copy(sources[at].at[:, :width], held_ref.at[at % 2], sems.at[at % 2])

    @pl.when(step == 0)
    def _():
        fetch(0).start()

    for at in range(len(sources)):

        @pl.when(step == at)
        def _():
            if at + 1 < len(sources):
                fetch(at + 1).start()
            fetch(at).wait()
            product = dot_tn(held_ref[at % 2], right_ref[...])
            if at == 0:
                sum_ref[...] = product
            elif at + 1 < len(sources):
                sum_ref[...] += product
            else:
                out_ref[...] = (sum_ref[...] + product).astype(BF)


def expert_grad(lefts, right, width, total, column, us, held=()):
    count = lefts[0].shape[0]
    columns = right.shape[1]
    any_spec = pl.BlockSpec(memory_space=pl.ANY)
    return pl.pallas_call(
        expert_grad_kernel,
        grid=(len(lefts),),
        in_specs=[any_spec] * len(lefts)
        + [pl.BlockSpec((count, columns), lambda i: (i, 0))]
        + [any_spec] * len(held),
        out_specs=pl.BlockSpec((width, columns), lambda i: (0, column)),
        out_shape=jax.ShapeDtypeStruct((width, total), BF),
        scratch_shapes=[
            pltpu.VMEM((width, columns), F32),
            pltpu.VMEM((2, count, width), BF),
            pltpu.SemaphoreType.DMA((2,)),
        ],
        input_output_aliases={len(lefts) + 1: 0} if held else {},
        compiler_params=pltpu.CompilerParams(vmem_limit_bytes=VMEM_LIMIT),
        cost_estimate=cost(us),
        name="expert_grad",
    )(*lefts, right, *held)


def body(
    tokens,
    lengths,
    routes,
    route_gates,
    cotangent,
    norm_first,
    attention_in,
    attention_out,
    norm_second,
    expert_gate,
    expert_lift,
    expert_down,
):
    count = tokens.shape[1]
    width = tokens.shape[2]
    choose = routes.shape[2]
    seq_count = lax.axis_size("seq")
    inner_count = lax.axis_size("inner")
    owners = seq_count * inner_count
    per_owner = EXPERTS // owners
    ff = expert_gate.shape[2]
    query_width = HEADS * HEAD_DIM
    seq_at = lax.axis_index("seq")
    layer_at = seq_at * inner_count + lax.axis_index("inner")
    length = lengths[0]
    place = jnp.stack([seq_at.astype(jnp.int32), length - seq_at.astype(jnp.int32) * count])
    live_rows = seq_at * count + jnp.arange(count, dtype=jnp.int32) < length
    inputs = tokens[0].astype(F32)
    upstream_low = cotangent[0]
    upstream = upstream_low.astype(F32)

    outer_count = lax.axis_size("outer")
    outer_at = lax.axis_index("outer")
    shard = width // (outer_count * inner_count)
    qkv = attention_in.shape[1]
    gains = jnp.concatenate([norm_first[:, None], norm_second[:, None], jnp.zeros((shard, 126), BF)], axis=1)
    project_in = lax.all_gather(jnp.concatenate([attention_in, gains], axis=1), ROWS, axis=0, tiled=True)
    project_out = lax.all_gather(attention_out, ROWS, axis=0, tiled=True)

    seq_place = seq_at.astype(jnp.int32)[None]
    expert_place = jnp.stack([layer_at.astype(jnp.int32), outer_at.astype(jnp.int32)])
    packed = pack_experts(seq_place, expert_gate, expert_lift, expert_down, inner_count)
    got = [exchange_start(part) for part in packed]
    packed = [exchange_end(*pair).reshape(inner_count * shard, 3 * ff) for pair in zip(packed, got)]
    gathered = [lax.all_gather(packed[0], "outer", axis=0, tiled=True)]
    gathered.append(lax.all_gather(after(packed[1], gathered[0][:8, :128]), "outer", axis=0, tiled=True))

    chosen = (
        routes[0][:, :, None] == jnp.arange(EXPERTS, dtype=jnp.int32)[None, None, :]
    ) & live_rows[:, None, None]
    combine = jnp.sum(jnp.where(chosen, route_gates[0][:, :, None], 0.0), axis=1)
    combine_high = combine.astype(BF)
    combine_low = (combine - combine_high.astype(F32)).astype(BF)
    up_block = jnp.concatenate(
        [upstream_low, combine_high, combine_low, jnp.zeros((count, 128 - 2 * EXPERTS), BF)], axis=1
    )
    half = count // 2
    up_block = after(up_block, packed)
    up_across, up_beside, up_sibling = seq_swap(up_block), side_swap(up_block), core_swap(up_block)

    query, pair_a, pair_b, lowered_one, gains = project_rows(tokens[0], project_in, qkv, 0)
    past_a = lax.ppermute(pair_a, "seq", [(0, 1)])
    late_pair, past_a = lax.optimization_barrier((pair_b, past_a))
    past_b = lax.ppermute(late_pair, "seq", [(0, 1)])
    mixed, stats_a = attend(place, query, pair_a, past_a, 0)
    mixed, stats_b = attend(place, query, pair_b, past_b, stats_a.shape[0], (mixed,))
    up_across, up_beside, stats_a = lax.optimization_barrier((up_across, up_beside, stats_a))
    up_far_top, up_far_low = seq_swap(up_beside[:half]), side_swap(up_across[half:])
    up_across_other, up_beside_other = core_swap(up_across), core_swap(up_beside)
    mixed, up_far_top, up_far_low, up_sibling, up_across_other, up_beside_other = lax.optimization_barrier(
        (mixed, up_far_top, up_far_low, up_sibling, up_across_other, up_beside_other)
    )
    up_pair_across, up_pair_beside = (up_across, up_across_other), (up_beside, up_beside_other)
    up_far = jnp.concatenate([up_far_top, up_far_low], axis=0)
    up_pair_far = (up_far, core_swap(up_far))
    middle, lowered_two = merge_rows(mixed, project_out, tokens[0], gains)

    chips = 4
    across, beside, sibling = seq_swap(lowered_two), side_swap(lowered_two), core_swap(lowered_two)

    def experts(e, at, rows, up, held, earlier=(), us=1):
        return expert_rows(expert_place, e, rows, up, gathered[e], at, 2 * chips * count, held, earlier, us)

    def upper(block, more):
        return jnp.concatenate([low_plus(block[:half], more), block[half:]])

    def lower(block, more):
        return jnp.concatenate([block[:half], low_plus(block[half:], more)])

    lowered_two, across, beside, sibling = lax.optimization_barrier((lowered_two, across, beside, sibling))
    row_own, up_own = (lowered_two, sibling), (up_block, up_sibling)
    far_top, far_low = seq_swap(beside[:half]), side_swap(across[half:])
    row_across = (across, core_swap(across))
    row_beside = (beside, core_swap(beside))
    far = jnp.concatenate([far_top, far_low], axis=0)
    row_far = (far, core_swap(far))
    row_all = (*row_own, *row_across, *row_beside, *row_far)
    up_all = (*up_own, *up_pair_across, *up_pair_beside, *up_pair_far)
    hidden_a, grads_a, *sums_a = experts(0, 0, row_all, up_all, ())

    def home(total):
        return lax.psum_scatter(total, "outer", scatter_dimension=0, tiled=True)

    def slots(local):
        return local.reshape(inner_count, shard, local.shape[1])

    total_a = expert_grad(row_all, grads_a, width, 3 * ff, 0, 1)
    total_a = expert_grad(up_all, hidden_a, width, 3 * ff, 2, 1, (total_a,))
    home_a = home(total_a)
    sums_a = after(sums_a, total_a)

    made_far = experts(1, 3, row_far, up_pair_far, (), sums_a)
    far_got, far_out_got = core_swap(made_far[5]), core_swap(made_far[3])
    made_across = experts(1, 1, row_across, up_pair_across, made_far[:2], sums_a)
    across_got, across_out_got = core_swap(made_across[5]), core_swap(made_across[3])
    far_got, far_out_got, held = lax.optimization_barrier((far_got, far_out_got, made_across[:2]))
    far_sum, far_out, held = lax.optimization_barrier(
        (low_plus(made_far[4], far_got), low_plus(made_far[2], far_out_got), held)
    )
    back_low, back_top = side_swap(far_sum[half:]), seq_swap(far_sum[:half])
    made_beside = experts(1, 2, row_beside, up_pair_beside, held, sums_a, 15)
    beside_got, beside_out_got = core_swap(made_beside[5]), core_swap(made_beside[3])
    across_got, across_out_got, back_low, back_top, held = lax.optimization_barrier(
        (across_got, across_out_got, back_low, back_top, made_beside[:2])
    )
    across_sum, out_across, held = lax.optimization_barrier(
        (lower(low_plus(made_across[4], across_got), back_low), low_plus(made_across[2], across_out_got), held)
    )
    across_in = seq_swap(across_sum)
    made_own = experts(1, 0, row_own, up_own, held, sums_a, 15)
    hidden_b, grads_b = made_own[:2]
    own_got = core_swap(made_own[5])
    beside_got, beside_out_got, grads_b = lax.optimization_barrier((beside_got, beside_out_got, grads_b))
    beside_sum, out_beside, grads_b = lax.optimization_barrier(
        (
            upper(low_plus(made_beside[4], beside_got), back_top),
            low_plus(made_beside[2], beside_out_got),
            grads_b,
        )
    )
    beside_in = side_swap(beside_sum)
    out_low, out_top = side_swap(far_out[half:]), seq_swap(far_out[:half])

    total_b = expert_grad(row_all, grads_b, width, 3 * ff, 0, 1)
    total_b = expert_grad(up_all, hidden_b, width, 3 * ff, 2, 1, (total_b,))
    home_b = home(total_b)
    across_in, beside_in, own_got, _ = lax.optimization_barrier((across_in, beside_in, own_got, total_b))

    middle_grad, branch_grad, mixed_grad, second_gain_grad = middle_back(
        made_own[4], own_got, across_in, beside_in, middle, upstream_low, gains, project_out, query_width
    )
    second_gain_grad = second_gain_grad[0]
    chain = Chain(mixed_grad)
    own_out_got = core_swap(chain.enter(made_own[3]))
    out_top, out_low = chain.enter((out_top, out_low))
    out_across, out_beside = lower(out_across, out_low), upper(out_beside, out_top)
    out_across, out_beside = chain.leave(lax.optimization_barrier((out_across, out_beside)))
    out_across_in, out_beside_in = seq_swap(out_across), side_swap(out_beside)
    def back(pair, past, stats, first):
        return attend_back(
            chain.enter(place), query, pair, past, mixed, mixed_grad, stats, first, stats.shape[0], 24
        )

    query_a, key_a, value_a, key_past_a, value_past_a = chain.leave(back(pair_a, past_a, stats_a, 0))
    late_a = lax.ppermute(jnp.concatenate([key_past_a, value_past_a], axis=1), "seq", [(1, 0)])
    out_home = HomeSum(chain.leave(dot_tn(chain.enter(mixed), branch_grad).astype(BF)))
    out_across_in, out_beside_in, own_out_got = chain.enter((out_across_in, out_beside_in, own_out_got))
    combined = (
        made_own[2].astype(F32) + own_out_got.astype(F32) + out_across_in.astype(F32) + out_beside_in.astype(F32)
    )
    block_output = chain.leave((middle + combined[:, :width]).astype(BF))[None]
    dots = combined[:, width : width + EXPERTS] + combined[:, width + EXPERTS : width + 2 * EXPERTS]
    grad_gates = chain.leave(jnp.sum(jnp.where(chosen, chain.enter(dots)[:, None, :], 0.0), axis=-1))[None]
    out_home.got = chain.enter(out_home.got)
    chain.leave(out_home.beside())
    a_slots = slots(home_a)
    a_mine = chain.leave(exchange_end(a_slots, chain.enter(exchange_start(a_slots))))
    late_a = chain.leave(chain.enter(late_a))
    a_other = seq_swap(a_mine)
    query_b, key_b, value_b, key_past_b, value_past_b = chain.leave(
        back(pair_b, past_b, stats_b, stats_a.shape[0])
    )
    late_b = lax.ppermute(jnp.concatenate([key_past_b, value_past_b], axis=1), "seq", [(1, 0)])
    a_other = chain.enter(a_other)
    out_home.got = chain.enter(out_home.got)
    chain.leave((out_home.across(), a_other))
    query_grad = jnp.concatenate([query_a, query_b], axis=1)
    query_home = HomeSum(chain.leave(dot_tn(chain.enter(lowered_one), query_grad).astype(BF)))
    query_home.got = chain.enter(query_home.got)
    chain.leave(query_home.beside())
    late_b = chain.enter(late_b)
    pair_grad, pair_weight = chain.leave(
        pair_back(chain.enter(lowered_one), key_a, key_b, value_a, value_b, late_a, late_b)
    )
    pair_part = lax.psum_scatter(pair_weight, ROWS, scatter_dimension=0, tiled=True)
    query_home.got = chain.enter(query_home.got)
    chain.leave(query_home.across())
    b_slots = slots(chain.enter(home_b))
    b_got = exchange_start(b_slots)
    projected_grad = jnp.concatenate([query_grad, pair_grad], axis=1)
    normed_grad_one = chain.leave(dot_nt(chain.enter(projected_grad), project_in[:, :qkv]))
    query_home.got = chain.enter(query_home.got)
    chain.leave(query_home.along())
    b_mine = chain.leave(exchange_end(b_slots, chain.enter(b_got)))
    normed_one, inverse_one, _ = norm_rows(inputs, gains[0])
    input_norm_grad, first_gain_grad = norm_back(chain.enter(normed_grad_one), normed_one, inverse_one, gains[0])
    grad_tokens = chain.leave(middle_grad + input_norm_grad)[None]
    b_other = seq_swap(b_mine)

    gain_grads = jnp.stack([first_gain_grad, second_gain_grad])
    gain_grads = gain_grads + core_swap(gain_grads)
    out_home.got = chain.enter(out_home.got)
    chain.leave(out_home.along())
    gain_grads = chain.leave(chain.enter(gain_grads))
    gain_grads = gain_grads + side_swap(gain_grads)
    query_home.got = chain.enter(query_home.got)
    chain.leave(query_home.final())
    gain_grads = chain.leave(chain.enter(gain_grads)).reshape(2, outer_count, inner_count * shard)
    gain_sum = pick(gain_grads, outer_at, 1)
    for step in range(1, outer_count):
        piece = pick(gain_grads, lax.rem(outer_at + step, outer_count), 1)
        gain_sum = gain_sum + lax.ppermute(
            piece, "outer", [(i, (i + step) % outer_count) for i in range(outer_count)]
        )
    out_home.got = chain.enter(out_home.got)
    chain.leave(out_home.final())
    gain_sum = chain.leave(pick(chain.enter(gain_sum).reshape(2, inner_count, shard), lax.axis_index("inner"), 1))
    gain_sum = gain_sum + seq_swap(gain_sum)
    parts = chain.enter((a_mine, a_other, b_mine, b_other))
    grads = [unpack_experts(seq_place, parts, kind, ff) for kind in range(3)]
    grad_gate, grad_lift, grad_down = chain.leave(lax.optimization_barrier(tuple(grads)))
    out_home.other, query_home.other = chain.enter((out_home.other, query_home.other))
    grad_out = chain.leave(out_home.result())
    pair_part = chain.enter(pair_part)
    pair_sum = pair_part.astype(F32) + seq_swap(pair_part).astype(F32)
    grad_in = jnp.concatenate([query_home.result(), pair_sum], axis=1)
    return (
        block_output,
        grad_tokens,
        grad_gates,
        gain_sum[0],
        grad_in,
        grad_out,
        gain_sum[1],
        grad_gate,
        grad_lift,
        grad_down,
    )


def solution(mesh):
    seq_count, fsdp_count = mesh.devices.shape
    inner_count = EXPERTS // (2 * seq_count)
    fine = jax.sharding.Mesh(
        mesh.devices.reshape(seq_count, fsdp_count // inner_count, inner_count), ("seq", "outer", "inner")
    )
    return jax.shard_map(
        body,
        mesh=fine,
        in_specs=(
            P(ROWS, "seq", None),
            P(ROWS),
            P(ROWS, "seq", None),
            P(ROWS, "seq", None),
            P(ROWS, "seq", None),
            P(ROWS),
            P(ROWS, None),
            P(ROWS, None),
            P(ROWS),
            P(ROWS, None, None),
            P(ROWS, None, None),
            P(ROWS, None, None),
        ),
        out_specs=(
            P(ROWS, "seq", None),
            P(ROWS, "seq", None),
            P(ROWS, "seq", None),
            P(ROWS),
            P(ROWS, None),
            P(ROWS, None),
            P(ROWS),
            P(ROWS, None, None),
            P(ROWS, None, None),
            P(ROWS, None, None),
        ),
        check_vma=False,
    )
```

```python
import functools

import jax
import jax.numpy as jnp
from jax import lax
from jax.experimental import pallas as pl
from jax.experimental.pallas import tpu as pltpu
from jax.sharding import PartitionSpec as P

HEADS = 24
KV_HEADS = 8
HEAD_DIM = 64
EXPERTS = 16
GROUP = HEADS // KV_HEADS
EPS = 1e-06
BF = jnp.bfloat16
F32 = jnp.float32
ROWS = ("outer", "inner")
VMEM_LIMIT = 60 * 1024 * 1024


def cost(microseconds):
    return pl.CostEstimate(flops=int(microseconds * 0.6e9), bytes_accessed=1000, transcendentals=0)


def norm_rows(values, gain_vector):
    inverse = lax.rsqrt(jnp.mean(values * values, axis=-1, keepdims=True) + EPS)
    normed = values * inverse
    return (normed, inverse, (normed * gain_vector).astype(BF))


def norm_back(upstream, normed, inverse, gain_vector):
    scaled = upstream * gain_vector
    spread = jnp.mean(scaled * normed, axis=-1, keepdims=True)
    return (inverse * (scaled - normed * spread), jnp.sum(upstream * normed, axis=0))


def swap(x, axis, bit):
    return lax.ppermute(x, axis, [(i, i ^ bit) for i in range(lax.axis_size(axis))])


def core_swap(x):
    return swap(x, "inner", 1)


def side_swap(x):
    return swap(x, "inner", 2)


def seq_swap(x):
    return swap(x, "seq", 1)


def after(x, *others):
    return lax.optimization_barrier((x, others))[0]


def low_plus(a, b):
    return (a.astype(F32) + b.astype(F32)).astype(BF)


def exchange_start(pieces):
    at = lax.axis_index("inner")
    bits = range(1, lax.axis_size("inner"))
    return [swap(lax.dynamic_index_in_dim(pieces, at ^ bit, 0, keepdims=False), "inner", bit) for bit in bits]


def exchange_end(pieces, got):
    at = lax.axis_index("inner")
    for bit, piece in enumerate(got, 1):
        pieces = lax.dynamic_update_index_in_dim(pieces, piece, at ^ bit, 0)
    return pieces


def pick(x, at, axis):
    return lax.dynamic_index_in_dim(x, at, axis, keepdims=False)


class HomeSum:
    def __init__(self, *totals):
        rows, columns = totals[0].shape[0], sum(total.shape[1] for total in totals)
        self.n = lax.axis_size("outer")
        self.seq_at = lax.axis_index("seq")
        self.outer_at = lax.axis_index("outer")
        inner_at = lax.axis_index("inner")
        sides = lax.axis_size("inner") // 2
        self.side_at, core_at = inner_at // 2, inner_at % 2
        self.half = columns // 2
        self.split = False
        part = rows // (self.n * sides * 2)

        def half_of(at):
            return jnp.concatenate(
                [pick(total.reshape(self.n, sides, 2, part, total.shape[1]), at, 2) for total in totals], axis=-1
            )

        self.held = half_of(core_at)
        self.got = core_swap(half_of(1 - core_at))

    def beside(self):
        held = low_plus(self.held, self.got)
        self.got = side_swap(pick(held, 1 - self.side_at, 1))
        self.held = pick(held, self.side_at, 1)
        return held

    def across(self):
        held = low_plus(self.held, self.got)
        self.got = seq_swap(lax.dynamic_slice_in_dim(held, (1 - self.seq_at) * self.half, self.half, 2))
        self.held = lax.dynamic_slice_in_dim(held, self.seq_at * self.half, self.half, 2)
        self.split = True
        return held

    def along(self):
        held = low_plus(self.held, self.got)
        self.held = pick(held, self.outer_at, 0)
        self.got = []
        for step in range(1, self.n):
            piece = pick(held, lax.rem(self.outer_at + step, self.n), 0)
            self.got.append(lax.ppermute(piece, "outer", [(i, (i + step) % self.n) for i in range(self.n)]))
        return held

    def final(self):
        result = self.held.astype(F32)
        for got in self.got:
            result = result + got.astype(F32)
        self.low = result.astype(BF)
        self.other = seq_swap(self.low)
        return self.low

    def result(self):
        low, other = self.low.astype(F32), self.other.astype(F32)
        if not self.split:
            return low + other
        first = self.seq_at == 0
        return jnp.concatenate([jnp.where(first, low, other), jnp.where(first, other, low)], axis=1)


class Chain:
    def __init__(self, last):
        self.last = last

    def enter(self, x):
        return after(x, self.last)

    def leave(self, y):
        self.last = y
        return y


def dot_nt(a, b):
    return lax.dot_general(a, b, (((1,), (1,)), ((), ())), preferred_element_type=F32)


def dot_nn(a, b):
    return lax.dot_general(a, b, (((1,), (0,)), ((), ())), preferred_element_type=F32)


def dot_tn(a, b):
    return lax.dot_general(a, b, (((0,), (0,)), ((), ())), preferred_element_type=F32)


def project_in_kernel(token_ref, weight_ref, tail_ref, query_ref, paira_ref, pairb_ref, low_ref, gain_ref):
    step = pl.program_id(0)
    queries = HEADS * HEAD_DIM // weight_ref.shape[1]

    @pl.when(step == 0)
    def _():
        row = lax.broadcasted_iota(jnp.int32, (8, 128), 0)
        lane = lax.broadcasted_iota(jnp.int32, (8, 128), 1)
        gain_ref[...] = dot_nt((row == lane).astype(BF), tail_ref[...])
        x = token_ref[...].astype(F32)
        inverse = lax.rsqrt(jnp.mean(x * x, axis=-1, keepdims=True) + EPS)
        low_ref[...] = (x * inverse * gain_ref[0:1, :]).astype(BF)

    result = dot_nn(low_ref[...], weight_ref[...]).astype(BF)

    @pl.when(step < queries)
    def _():
        query_ref[...] = result

    half = result.shape[1] // 2
    for part in range(2):

        @pl.when(step == queries + part)
        def _():
            cols = slice(part * half, (part + 1) * half)
            paira_ref[:, cols] = result[:, :half]
            pairb_ref[:, cols] = result[:, half:]


def project_rows(tokens, weight, qkv, before):
    count, width = tokens.shape
    tile = 512
    query_width = HEADS * HEAD_DIM
    queries = query_width // tile
    return pl.pallas_call(
        project_in_kernel,
        grid=(qkv // tile,),
        in_specs=[
            pl.BlockSpec((count, width), lambda j: (0, 0)),
            pl.BlockSpec((width, tile), lambda j: (0, before // tile + j)),
            pl.BlockSpec((width, 128), lambda j: (0, (before + qkv) // 128)),
        ],
        out_specs=[
            pl.BlockSpec((count, tile), lambda j: (0, jnp.minimum(j, queries - 1))),
            pl.BlockSpec((count, tile), lambda j: (0, 0)),
            pl.BlockSpec((count, tile), lambda j: (0, 0)),
            pl.BlockSpec((count, width), lambda j: (0, 0)),
            pl.BlockSpec((8, width), lambda j: (0, 0)),
        ],
        out_shape=[
            jax.ShapeDtypeStruct((count, query_width), BF),
            jax.ShapeDtypeStruct((count, tile), BF),
            jax.ShapeDtypeStruct((count, tile), BF),
            jax.ShapeDtypeStruct((count, width), BF),
            jax.ShapeDtypeStruct((8, width), F32),
        ],
        compiler_params=pltpu.CompilerParams(vmem_limit_bytes=VMEM_LIMIT),
        cost_estimate=cost(0),
        name="project_rows",
    )(tokens, weight, weight)


def merge_kernel(mixed_ref, weight_ref, token_ref, gain_ref, middle_ref, low_ref):
    product = dot_nn(mixed_ref[...], weight_ref[...])
    step = pl.program_id(0)

    @pl.when(step == 0)
    def _():
        middle_ref[...] = token_ref[...].astype(F32) + product

    @pl.when(step > 0)
    def _():
        middle_ref[...] += product

    @pl.when(step == pl.num_programs(0) - 1)
    def _():
        x = middle_ref[...]
        inverse = lax.rsqrt(jnp.mean(x * x, axis=-1, keepdims=True) + EPS)
        low_ref[...] = (x * inverse * gain_ref[1:2, :]).astype(BF)


def merge_rows(mixed, weight, tokens, gains):
    count, width = tokens.shape
    tile = 512
    whole = pl.BlockSpec((count, width), lambda j: (0, 0))
    return pl.pallas_call(
        merge_kernel,
        grid=(mixed.shape[1] // tile,),
        in_specs=[
            pl.BlockSpec((count, tile), lambda j: (0, j)),
            pl.BlockSpec((tile, width), lambda j: (j, 0)),
            whole,
            pl.BlockSpec((8, width), lambda j: (0, 0)),
        ],
        out_specs=[whole, whole],
        out_shape=[jax.ShapeDtypeStruct((count, width), F32), jax.ShapeDtypeStruct((count, width), BF)],
        compiler_params=pltpu.CompilerParams(vmem_limit_bytes=VMEM_LIMIT),
        cost_estimate=cost(0),
        name="merge_rows",
    )(mixed, weight, tokens, gains)


def middle_back_kernel(
    own_ref, got_ref, across_ref, beside_ref, middle_ref, up_ref, gain_ref, weight_ref,
    grad_ref, low_ref, mixed_ref, sum_ref,
):
    @pl.when(pl.program_id(0) == 0)
    def _():
        above = own_ref[...].astype(F32) + got_ref[...].astype(F32)
        above = above + across_ref[...].astype(F32) + beside_ref[...].astype(F32)
        x = middle_ref[...]
        inverse = lax.rsqrt(jnp.mean(x * x, axis=-1, keepdims=True) + EPS)
        normed = x * inverse
        scaled = above * gain_ref[1:2, :]
        spread = jnp.mean(scaled * normed, axis=-1, keepdims=True)
        grad = up_ref[...].astype(F32) + inverse * (scaled - normed * spread)
        grad_ref[...] = grad
        low_ref[...] = grad.astype(BF)
        sum_ref[...] = jnp.broadcast_to(jnp.sum(above * normed, axis=0, keepdims=True), sum_ref.shape)

    mixed_ref[...] = dot_nt(low_ref[...], weight_ref[...]).astype(BF)


def middle_back(own, got, across, beside, middle, up, gains, weight, columns):
    count, width = own.shape
    tile = 512
    whole = pl.BlockSpec((count, width), lambda j: (0, 0))
    row = pl.BlockSpec((8, width), lambda j: (0, 0))
    return pl.pallas_call(
        middle_back_kernel,
        grid=(columns // tile,),
        in_specs=[whole] * 6 + [row, pl.BlockSpec((tile, width), lambda j: (j, 0))],
        out_specs=[whole, whole, pl.BlockSpec((count, tile), lambda j: (0, j)), row],
        out_shape=[
            jax.ShapeDtypeStruct((count, width), F32),
            jax.ShapeDtypeStruct((count, width), BF),
            jax.ShapeDtypeStruct((count, columns), BF),
            jax.ShapeDtypeStruct((8, width), F32),
        ],
        compiler_params=pltpu.CompilerParams(vmem_limit_bytes=VMEM_LIMIT),
        cost_estimate=cost(1),
        name="middle_back",
    )(own, got, across, beside, middle, up, gains, weight)


def attend_kernel(place_ref, q_ref, k_ref, v_ref, kr_ref, vr_ref, *refs):
    mixed_ref, stat_ref, bias_ref, col_ref = refs[-4:]
    count = q_ref.shape[0]
    half = count // 2
    seq_at = place_ref[0]
    live = place_ref[1]

    @pl.when(pl.program_id(0) == 0)
    def _():
        row = lax.broadcasted_iota(jnp.int32, (count, count), 0)
        col = lax.broadcasted_iota(jnp.int32, (count, count), 1)
        bias_ref[...] = jnp.where((col <= row) & (col < live), 0.0, -jnp.inf)
        col_ref[...] = jnp.zeros_like(col_ref)

    def run(with_past):
        for g in range(2):
            lanes = slice(g * HEAD_DIM, (g + 1) * HEAD_DIM)
            key = k_ref[:, lanes]
            value = v_ref[:, lanes]
            if with_past:
                key_past = kr_ref[:, lanes]
                value_past = vr_ref[:, lanes]
            for r in range(GROUP):
                h = g * GROUP + r
                for part in range(2):
                    rows = slice(part * half, (part + 1) * half)
                    span = (part + 1) * half
                    query = q_ref[rows, h * HEAD_DIM : (h + 1) * HEAD_DIM] * BF(HEAD_DIM**-0.5)
                    scores = dot_nt(query, key[:span]) + bias_ref[rows, :span]
                    peak = jnp.max(scores, axis=-1, keepdims=True)
                    if with_past:
                        past = dot_nt(query, key_past)
                        peak = jnp.maximum(peak, jnp.max(past, axis=-1, keepdims=True))
                    lifted = jnp.exp(scores - peak)
                    total = jnp.sum(lifted, axis=-1, keepdims=True)
                    mixed = dot_nn(lifted.astype(BF), value[:span])
                    if with_past:
                        lifted_past = jnp.exp(past - peak)
                        total = total + jnp.sum(lifted_past, axis=-1, keepdims=True)
                        mixed = mixed + dot_nn(lifted_past.astype(BF), value_past)
                    mixed_ref[rows, h * HEAD_DIM : (h + 1) * HEAD_DIM] = (mixed / total).astype(BF)
                    col_ref[rows, h : h + 1] = peak + jnp.log(total)

    @pl.when(seq_at == 0)
    def _():
        run(False)

    @pl.when(seq_at != 0)
    def _():
        run(True)

    stat_ref[...] = col_ref[...].T[:8, :]


def attend(place, query, pair, past, first, held=()):
    count = query.shape[0]
    steps = pair.shape[1] // 256
    wide = 2 * GROUP * HEAD_DIM
    return pl.pallas_call(
        attend_kernel,
        grid_spec=pltpu.PrefetchScalarGridSpec(
            num_scalar_prefetch=1,
            grid=(steps,),
            in_specs=[
                pl.BlockSpec((count, wide), lambda j, place: (0, first + j)),
                pl.BlockSpec((count, 128), lambda j, place: (0, j)),
                pl.BlockSpec((count, 128), lambda j, place: (0, steps + j)),
                pl.BlockSpec((count, 128), lambda j, place: (0, j)),
                pl.BlockSpec((count, 128), lambda j, place: (0, steps + j)),
            ]
            + [pl.BlockSpec(memory_space=pl.ANY)] * len(held),
            out_specs=[
                pl.BlockSpec((count, wide), lambda j, place: (0, first + j)),
                pl.BlockSpec((None, 8, count), lambda j, place: (j, 0, 0)),
            ],
            scratch_shapes=[pltpu.VMEM((count, count), F32), pltpu.VMEM((count, 128), F32)],
        ),
        out_shape=[
            jax.ShapeDtypeStruct((count, HEADS * HEAD_DIM), BF),
            jax.ShapeDtypeStruct((steps, 8, count), F32),
        ],
        input_output_aliases={6: 0} if held else {},
        compiler_params=pltpu.CompilerParams(vmem_limit_bytes=VMEM_LIMIT),
        cost_estimate=cost(0),
        name="attend",
    )(place, query, pair, pair, past, past, *held)


def attend_back_kernel(
    place_ref, q_ref, k_ref, v_ref, kr_ref, vr_ref, mixed_ref, grad_ref, stat_ref,
    dq_ref, dk_ref, dv_ref, dkr_ref, dvr_ref, bias_ref,
):
    count = q_ref.shape[0]
    half = count // 2
    seq_at = place_ref[0]
    live = place_ref[1]
    scale = HEAD_DIM**-0.5

    @pl.when(pl.program_id(0) == 0)
    def _():
        key_at = lax.broadcasted_iota(jnp.int32, (count, count), 0)
        query_at = lax.broadcasted_iota(jnp.int32, (count, count), 1)
        bias_ref[...] = jnp.where((key_at <= query_at) & (key_at < live), 0.0, -jnp.inf)

    def run(with_past):
        for g in range(2):
            lanes = slice(g * HEAD_DIM, (g + 1) * HEAD_DIM)
            key = k_ref[:, lanes]
            value = v_ref[:, lanes]
            sums = [[jnp.zeros((half, HEAD_DIM), F32) for _ in range(2)] for _ in range(2)]
            if with_past:
                key_past = kr_ref[:, lanes]
                value_past = vr_ref[:, lanes]
                past_sums = [jnp.zeros((count, HEAD_DIM), F32) for _ in range(2)]
            for r in range(GROUP):
                h = g * GROUP + r
                cols = slice(h * HEAD_DIM, (h + 1) * HEAD_DIM)
                query = q_ref[:, cols] * BF(scale)
                grad = grad_ref[:, cols]
                product = grad.astype(F32) * mixed_ref[:, cols].astype(F32)
                delta = lax.dot_general(
                    jnp.ones((8, HEAD_DIM), F32), product, (((1,), (1,)), ((), ())),
                    precision=lax.Precision.HIGHEST, preferred_element_type=F32,
                )[:1]
                stat = stat_ref[h : h + 1, :]

                def piece(keys, values, queries, grads, stats, deltas, bias):
                    scores = dot_nt(keys, queries)
                    if bias is not None:
                        scores = scores + bias
                    chances = jnp.exp(scores - stats)
                    chance_grad = dot_nt(values, grads)
                    score_grad = (chances * (chance_grad - deltas)).astype(BF)
                    return chances.astype(BF), score_grad

                p0, s0 = piece(key[:half], value[:half], query, grad, stat, delta, bias_ref[:half, :])
                p1, s1 = piece(
                    key[half:], value[half:], query[half:], grad[half:], stat[:, half:], delta[:, half:],
                    bias_ref[half:, half:],
                )
                dq = dot_tn(s0, key[:half])
                dq_late = dot_tn(s1, key[half:])
                sums[0][0] += dot_nn(s0, query)
                sums[0][1] += dot_nn(s1, query[half:])
                sums[1][0] += dot_nn(p0, grad)
                sums[1][1] += dot_nn(p1, grad[half:])
                if with_past:
                    pp, sp = piece(key_past, value_past, query, grad, stat, delta, None)
                    dq = dq + dot_tn(sp, key_past)
                    past_sums[0] += dot_nn(sp, query)
                    past_sums[1] += dot_nn(pp, grad)
                dq_ref[:half, cols] = (dq[:half] * scale).astype(BF)
                dq_ref[half:, cols] = ((dq[half:] + dq_late) * scale).astype(BF)
            for where, out in ((0, dk_ref), (1, dv_ref)):
                out[:half, lanes] = sums[where][0].astype(BF)
                out[half:, lanes] = sums[where][1].astype(BF)
            if with_past:
                dkr_ref[:, lanes] = past_sums[0].astype(BF)
                dvr_ref[:, lanes] = past_sums[1].astype(BF)

    @pl.when(seq_at == 0)
    def _():
        run(False)
        dkr_ref[...] = jnp.zeros_like(dkr_ref)
        dvr_ref[...] = jnp.zeros_like(dvr_ref)

    @pl.when(seq_at != 0)
    def _():
        run(True)


def attend_back(place, query, pair, past, mixed, mixed_grad, stats, first, steps, us):
    count = query.shape[0]
    wide = 2 * GROUP * HEAD_DIM
    narrow = jax.ShapeDtypeStruct((count, steps * 128), BF)
    head_spec = pl.BlockSpec((count, wide), lambda j, place: (0, first + j))
    pair_spec = pl.BlockSpec((count, 128), lambda j, place: (0, j))
    return pl.pallas_call(
        attend_back_kernel,
        grid_spec=pltpu.PrefetchScalarGridSpec(
            num_scalar_prefetch=1,
            grid=(steps,),
            in_specs=[
                head_spec,
                pl.BlockSpec((count, 128), lambda j, place: (0, j)),
                pl.BlockSpec((count, 128), lambda j, place: (0, steps + j)),
                pl.BlockSpec((count, 128), lambda j, place: (0, j)),
                pl.BlockSpec((count, 128), lambda j, place: (0, steps + j)),
                head_spec,
                head_spec,
                pl.BlockSpec((None, 8, count), lambda j, place: (j, 0, 0)),
            ],
            out_specs=[pl.BlockSpec((count, wide), lambda j, place: (0, j))] + [pair_spec] * 4,
            scratch_shapes=[pltpu.VMEM((count, count), F32)],
        ),
        out_shape=[jax.ShapeDtypeStruct((count, steps * wide), BF), narrow, narrow, narrow, narrow],
        compiler_params=pltpu.CompilerParams(vmem_limit_bytes=VMEM_LIMIT),
        cost_estimate=cost(us),
        name="attend_back",
    )(place, query, pair, pair, past, past, mixed, mixed_grad, stats)


def pair_kernel(low_ref, keya_ref, keyb_ref, valuea_ref, valueb_ref, latea_ref, lateb_ref, pair_ref, grad_ref):
    half = keya_ref.shape[1]
    for part, (a_ref, b_ref) in enumerate(((keya_ref, keyb_ref), (valuea_ref, valueb_ref))):

        @pl.when(pl.program_id(0) == part)
        def _():
            cols = slice(part * half, (part + 1) * half)
            pair_ref[:, :half] = (a_ref[...].astype(F32) + latea_ref[:, cols].astype(F32)).astype(BF)
            pair_ref[:, half:] = (b_ref[...].astype(F32) + lateb_ref[:, cols].astype(F32)).astype(BF)

    grad_ref[...] = dot_tn(low_ref[...], pair_ref[...]).astype(BF)


def pair_back(low, key_a, key_b, value_a, value_b, late_a, late_b):
    count, width = low.shape
    half = key_a.shape[1]

    def whole(x):
        return pl.BlockSpec(x.shape, lambda j: (0, 0))

    args = (low, key_a, key_b, value_a, value_b, late_a, late_b)
    return pl.pallas_call(
        pair_kernel,
        grid=(2,),
        in_specs=[whole(x) for x in args],
        out_specs=[
            pl.BlockSpec((count, 2 * half), lambda j: (0, j)),
            pl.BlockSpec((width, 2 * half), lambda j: (0, j)),
        ],
        out_shape=[
            jax.ShapeDtypeStruct((count, 4 * half), BF),
            jax.ShapeDtypeStruct((width, 4 * half), BF),
        ],
        compiler_params=pltpu.CompilerParams(vmem_limit_bytes=VMEM_LIMIT),
        cost_estimate=cost(0),
        name="pair_back",
    )(*args)


def pack_kernel(seq_ref, gate_ref, lift_ref, down_ref, *out_refs):
    owners, _, columns = out_refs[0].shape
    ff = columns // 3
    for seq in range(2):

        @pl.when(seq_ref[0] == seq)
        def _():
            for kind, ref in enumerate((gate_ref, lift_ref, down_ref)):
                for owner in range(owners):
                    for e in range(2):
                        out_refs[e][owner, :, kind * ff : (kind + 1) * ff] = ref[:, (seq * owners + owner) * 2 + e, :]


def pack_experts(seq, gate, lift, down, owners):
    rows, experts, ff = gate.shape
    tile = 32 if rows % 32 == 0 else rows
    in_spec = pl.BlockSpec((tile, experts, ff), lambda i, seq: (i, 0, 0))
    out_spec = pl.BlockSpec((owners, tile, 3 * ff), lambda i, seq: (0, i, 0))
    out = jax.ShapeDtypeStruct((owners, rows, 3 * ff), BF)
    return pl.pallas_call(
        pack_kernel,
        grid_spec=pltpu.PrefetchScalarGridSpec(
            num_scalar_prefetch=1, grid=(rows // tile,), in_specs=[in_spec] * 3, out_specs=[out_spec] * 2
        ),
        out_shape=[out, out],
        compiler_params=pltpu.CompilerParams(vmem_limit_bytes=VMEM_LIMIT),
        cost_estimate=cost(6),
        name="pack_experts",
    )(seq, gate, lift, down)


def unpack_kernel(seq_ref, *refs):
    out_ref = refs[-1]
    owners = refs[0].shape[0]
    for seq in range(2):

        @pl.when(seq_ref[0] == seq)
        def _():
            for e in range(2):
                for at, ref in ((seq, refs[2 * e]), (1 - seq, refs[2 * e + 1])):
                    for owner in range(owners):
                        out_ref[:, (at * owners + owner) * 2 + e, :] = ref[owner].astype(F32)


def unpack_experts(seq, parts, column, ff):
    owners, rows, _ = parts[0].shape
    in_spec = pl.BlockSpec((owners, rows, ff), lambda i, seq: (0, 0, column))
    return pl.pallas_call(
        unpack_kernel,
        grid_spec=pltpu.PrefetchScalarGridSpec(
            num_scalar_prefetch=1,
            grid=(1,),
            in_specs=[in_spec] * 4,
            out_specs=pl.BlockSpec((rows, EXPERTS, ff), lambda i, seq: (0, 0, 0)),
        ),
        out_shape=jax.ShapeDtypeStruct((rows, EXPERTS, ff), F32),
        compiler_params=pltpu.CompilerParams(vmem_limit_bytes=VMEM_LIMIT),
        cost_estimate=cost(4),
        name="unpack_experts",
    )(seq, *parts)


def expert_kernel(e, blocks, has_earlier, place_ref, *refs):
    rows_refs, up_refs = refs[:blocks], refs[blocks : 2 * blocks]
    if has_earlier:
        earlier_out, earlier_back, wt_ref = refs[2 * blocks : 2 * blocks + 3]
        (ch_ref, gl_ref, outa_ref, outb_ref, backa_ref, backb_ref) = refs[-12:-6]
        n_buf, c_buf, sems, out_buf, back_buf, out_sems = refs[-6:]
    else:
        wt_ref = refs[2 * blocks]
        ch_ref, gl_ref, out_ref, back_ref, n_buf, c_buf, sems = refs[-7:]
    tile, width = n_buf.shape[1:]
    tiles = 2 * blocks
    ff = wt_ref.shape[1] // 3
    step = pl.program_id(0)
    slot = lax.rem(step, 2)
    mine = 2 * place_ref[0] + e
    if has_earlier:
        out_ref, back_ref = out_buf.at[step], back_buf.at[step]

    def fetch(t):
        part = pl.ds((t % 2) * tile, tile)
        return (
            pltpu.make_async_copy(rows_refs[t // 2].at[part], n_buf.at[t % 2], sems.at[0, t % 2]),
            pltpu.make_async_copy(up_refs[t // 2].at[part], c_buf.at[t % 2], sems.at[1, t % 2]),
        )

    @pl.when(step == 0)
    def _():
        for copy in fetch(0):
            copy.start()

    for t in range(tiles):

        @pl.when(step == t)
        def _():
            if t + 1 < tiles:
                for copy in fetch(t + 1):
                    copy.start()
            for copy in fetch(t):
                copy.wait()

    n_ref, c_ref = n_buf.at[slot], c_buf.at[slot]
    packed = c_ref[:, width:].astype(F32)
    lane = lax.broadcasted_iota(jnp.int32, packed.shape, 1)
    g = dot_nn(n_ref[...], wt_ref[:, :ff])
    l = dot_nn(n_ref[...], wt_ref[:, ff : 2 * ff])
    u = dot_nn(c_ref[:, :width], wt_ref[:, 2 * ff :])
    own_lane = (lane == mine) | (lane == EXPERTS + mine)
    weight = jnp.sum(jnp.where(own_lane, packed, 0.0), axis=-1, keepdims=True)
    sig = 1.0 / (1.0 + jnp.exp(-g))
    silu = g * sig
    hidden = silu * l
    dot = jnp.sum(hidden * u, axis=-1, keepdims=True)
    dot_high = dot.astype(BF).astype(F32)
    dots = jnp.where(lane == mine, dot_high, 0.0)
    dots = jnp.where(lane == EXPERTS + mine, dot - dot_high, dots)
    grad = u * weight
    ch_ref[...] = (hidden * weight).astype(BF)
    gl_ref[:, :ff] = (grad * l * (sig + silu * (1.0 - sig))).astype(BF)
    gl_ref[:, ff:] = (grad * silu).astype(BF)
    back = dot_nt(gl_ref[...], wt_ref[:, : 2 * ff])
    out = dot_nt(ch_ref[...], wt_ref[:, 2 * ff :])
    if has_earlier:
        out = out + earlier_out[:, :width].astype(F32)
        dots = dots + earlier_out[:, width:].astype(F32)
        back = back + earlier_back[...].astype(F32)
    back_ref[...] = back.astype(BF)
    out_ref[:, :width] = out.astype(BF)
    out_ref[:, width:] = dots.astype(BF)
    if has_earlier:

        def send(t):
            part = pl.ds((t % 2) * tile, tile)
            to_out, to_back = (outa_ref, backa_ref) if t < 2 else (outb_ref, backb_ref)
            return (
                pltpu.make_async_copy(out_buf.at[t], to_out.at[part], out_sems.at[0, t]),
                pltpu.make_async_copy(back_buf.at[t], to_back.at[part], out_sems.at[1, t]),
            )

        for t in range(tiles):

            @pl.when(step == t)
            def _():
                for copy in send(t):
                    copy.start()

        @pl.when(step == tiles - 1)
        def _():
            for t in range(tiles):
                for copy in send(t):
                    copy.wait()


def expert_rows(place, e, rows, up, packed, chunk, total, held, earlier, us):
    count, width = rows[0].shape
    blocks = len(rows)
    ff = packed.shape[1] // 3
    tile = count // 2
    more = width + 128

    def at_rows(i, place):
        return (4 * chunk + i, 0)

    any_spec = pl.BlockSpec(memory_space=pl.ANY)
    sum_specs = [pl.BlockSpec((tile, more), at_rows), pl.BlockSpec((tile, width), at_rows)]
    packed_spec = pl.BlockSpec((width, 3 * ff), lambda i, place: (0, 0), pipeline_mode=pl.Buffered(1))
    one = jax.ShapeDtypeStruct((count, width), BF)
    one_more = jax.ShapeDtypeStruct((count, more), BF)
    scratch = [pltpu.VMEM((2, tile, width), BF), pltpu.VMEM((2, tile, more), BF), pltpu.SemaphoreType.DMA((2, 2))]
    held, earlier = list(held), list(earlier)
    begin = 2 + 2 * blocks + len(earlier)
    if earlier:
        sums = [one_more] * 2 + [one] * 2
        out_sums = [any_spec] * 4
        scratch += [
            pltpu.VMEM((2 * blocks, tile, more), BF),
            pltpu.VMEM((2 * blocks, tile, width), BF),
            pltpu.SemaphoreType.DMA((2, 2 * blocks)),
        ]
    else:
        sums = [jax.ShapeDtypeStruct((total, more), BF), jax.ShapeDtypeStruct((total, width), BF)]
        out_sums = sum_specs
    return pl.pallas_call(
        functools.partial(expert_kernel, e, blocks, len(earlier) > 0),
        grid_spec=pltpu.PrefetchScalarGridSpec(
            num_scalar_prefetch=1,
            grid=(2 * blocks,),
            in_specs=[any_spec] * (2 * blocks)
            + (sum_specs if earlier else [])
            + [packed_spec]
            + [any_spec] * len(held),
            out_specs=[pl.BlockSpec((tile, ff), at_rows), pl.BlockSpec((tile, 2 * ff), at_rows)] + out_sums,
            scratch_shapes=scratch,
        ),
        out_shape=[jax.ShapeDtypeStruct((total, ff), BF), jax.ShapeDtypeStruct((total, 2 * ff), BF)] + sums,
        input_output_aliases={begin + at: at for at in range(len(held))},
        compiler_params=pltpu.CompilerParams(vmem_limit_bytes=VMEM_LIMIT),
        cost_estimate=cost(us),
        name="expert_rows",
    )(place, *rows, *up, *earlier, packed, *held)


def expert_grad_kernel(*refs):
    out_ref, sum_ref, held_ref, sems = refs[-4:]
    sources, right_ref = refs[:8], refs[8]
    width = held_ref.shape[2]
    step = pl.program_id(0)

    def fetch(at):
        return pltpu.make_async_copy(sources[at].at[:, :width], held_ref.at[at % 2], sems.at[at % 2])

    @pl.when(step == 0)
    def _():
        fetch(0).start()

    for at in range(len(sources)):

        @pl.when(step == at)
        def _():
            if at + 1 < len(sources):
                fetch(at + 1).start()
            fetch(at).wait()
            product = dot_tn(held_ref[at % 2], right_ref[...])
            if at == 0:
                sum_ref[...] = product
            elif at + 1 < len(sources):
                sum_ref[...] += product
            else:
                out_ref[...] = (sum_ref[...] + product).astype(BF)


def expert_grad(lefts, right, width, total, column, us, held=()):
    count = lefts[0].shape[0]
    columns = right.shape[1]
    any_spec = pl.BlockSpec(memory_space=pl.ANY)
    return pl.pallas_call(
        expert_grad_kernel,
        grid=(len(lefts),),
        in_specs=[any_spec] * len(lefts)
        + [pl.BlockSpec((count, columns), lambda i: (i, 0))]
        + [any_spec] * len(held),
        out_specs=pl.BlockSpec((width, columns), lambda i: (0, column)),
        out_shape=jax.ShapeDtypeStruct((width, total), BF),
        scratch_shapes=[
            pltpu.VMEM((width, columns), F32),
            pltpu.VMEM((2, count, width), BF),
            pltpu.SemaphoreType.DMA((2,)),
        ],
        input_output_aliases={len(lefts) + 1: 0} if held else {},
        compiler_params=pltpu.CompilerParams(vmem_limit_bytes=VMEM_LIMIT),
        cost_estimate=cost(us),
        name="expert_grad",
    )(*lefts, right, *held)


def body(
    tokens,
    lengths,
    routes,
    route_gates,
    cotangent,
    norm_first,
    attention_in,
    attention_out,
    norm_second,
    expert_gate,
    expert_lift,
    expert_down,
):
    count = tokens.shape[1]
    width = tokens.shape[2]
    choose = routes.shape[2]
    seq_count = lax.axis_size("seq")
    inner_count = lax.axis_size("inner")
    owners = seq_count * inner_count
    per_owner = EXPERTS // owners
    ff = expert_gate.shape[2]
    query_width = HEADS * HEAD_DIM
    seq_at = lax.axis_index("seq")
    layer_at = seq_at * inner_count + lax.axis_index("inner")
    length = lengths[0]
    place = jnp.stack([seq_at.astype(jnp.int32), length - seq_at.astype(jnp.int32) * count])
    live_rows = seq_at * count + jnp.arange(count, dtype=jnp.int32) < length
    inputs = tokens[0].astype(F32)
    upstream_low = cotangent[0]
    upstream = upstream_low.astype(F32)

    outer_count = lax.axis_size("outer")
    outer_at = lax.axis_index("outer")
    shard = width // (outer_count * inner_count)
    qkv = attention_in.shape[1]
    gains = jnp.concatenate([norm_first[:, None], norm_second[:, None], jnp.zeros((shard, 126), BF)], axis=1)
    project_in = lax.all_gather(jnp.concatenate([attention_in, gains], axis=1), ROWS, axis=0, tiled=True)
    project_out = lax.all_gather(attention_out, ROWS, axis=0, tiled=True)

    seq_place = seq_at.astype(jnp.int32)[None]
    expert_place = jnp.stack([layer_at.astype(jnp.int32), outer_at.astype(jnp.int32)])
    packed = pack_experts(seq_place, expert_gate, expert_lift, expert_down, inner_count)
    got = [exchange_start(part) for part in packed]
    packed = [exchange_end(*pair).reshape(inner_count * shard, 3 * ff) for pair in zip(packed, got)]
    gathered = [lax.all_gather(packed[0], "outer", axis=0, tiled=True)]
    gathered.append(lax.all_gather(after(packed[1], gathered[0][:8, :128]), "outer", axis=0, tiled=True))

    chosen = (
        routes[0][:, :, None] == jnp.arange(EXPERTS, dtype=jnp.int32)[None, None, :]
    ) & live_rows[:, None, None]
    combine = jnp.sum(jnp.where(chosen, route_gates[0][:, :, None], 0.0), axis=1)
    combine_high = combine.astype(BF)
    combine_low = (combine - combine_high.astype(F32)).astype(BF)
    up_block = jnp.concatenate(
        [upstream_low, combine_high, combine_low, jnp.zeros((count, 128 - 2 * EXPERTS), BF)], axis=1
    )
    half = count // 2
    up_block = after(up_block, packed)
    up_across, up_beside, up_sibling = seq_swap(up_block), side_swap(up_block), core_swap(up_block)

    query, pair_a, pair_b, lowered_one, gains = project_rows(tokens[0], project_in, qkv, 0)
    past_a = lax.ppermute(pair_a, "seq", [(0, 1)])
    late_pair, past_a = lax.optimization_barrier((pair_b, past_a))
    past_b = lax.ppermute(late_pair, "seq", [(0, 1)])
    mixed, stats_a = attend(place, query, pair_a, past_a, 0)
    mixed, stats_b = attend(place, query, pair_b, past_b, stats_a.shape[0], (mixed,))
    up_across, up_beside, stats_a = lax.optimization_barrier((up_across, up_beside, stats_a))
    up_far_top, up_far_low = seq_swap(up_beside[:half]), side_swap(up_across[half:])
    up_across_other, up_beside_other = core_swap(up_across), core_swap(up_beside)
    mixed, up_far_top, up_far_low, up_sibling, up_across_other, up_beside_other = lax.optimization_barrier(
        (mixed, up_far_top, up_far_low, up_sibling, up_across_other, up_beside_other)
    )
    up_pair_across, up_pair_beside = (up_across, up_across_other), (up_beside, up_beside_other)
    up_far = jnp.concatenate([up_far_top, up_far_low], axis=0)
    up_pair_far = (up_far, core_swap(up_far))
    middle, lowered_two = merge_rows(mixed, project_out, tokens[0], gains)

    chips = 4
    across, beside, sibling = seq_swap(lowered_two), side_swap(lowered_two), core_swap(lowered_two)

    def experts(e, at, rows, up, held, earlier=(), us=1):
        return expert_rows(expert_place, e, rows, up, gathered[e], at, 2 * chips * count, held, earlier, us)

    def upper(block, more):
        return jnp.concatenate([low_plus(block[:half], more), block[half:]])

    def lower(block, more):
        return jnp.concatenate([block[:half], low_plus(block[half:], more)])

    lowered_two, across, beside, sibling = lax.optimization_barrier((lowered_two, across, beside, sibling))
    row_own, up_own = (lowered_two, sibling), (up_block, up_sibling)
    far_top, far_low = seq_swap(beside[:half]), side_swap(across[half:])
    row_across = (across, core_swap(across))
    row_beside = (beside, core_swap(beside))
    far = jnp.concatenate([far_top, far_low], axis=0)
    row_far = (far, core_swap(far))
    row_all = (*row_own, *row_across, *row_beside, *row_far)
    up_all = (*up_own, *up_pair_across, *up_pair_beside, *up_pair_far)
    hidden_a, grads_a, *sums_a = experts(0, 0, row_all, up_all, ())

    def home(total):
        return lax.psum_scatter(total, "outer", scatter_dimension=0, tiled=True)

    def slots(local):
        return local.reshape(inner_count, shard, local.shape[1])

    total_a = expert_grad(row_all, grads_a, width, 3 * ff, 0, 1)
    total_a = expert_grad(up_all, hidden_a, width, 3 * ff, 2, 1, (total_a,))
    home_a = home(total_a)
    sums_a = after(sums_a, total_a)

    made_far = experts(1, 3, row_far, up_pair_far, (), sums_a)
    far_got, far_out_got = core_swap(made_far[5]), core_swap(made_far[3])
    made_across = experts(1, 1, row_across, up_pair_across, made_far[:2], sums_a)
    across_got, across_out_got = core_swap(made_across[5]), core_swap(made_across[3])
    far_got, far_out_got, held = lax.optimization_barrier((far_got, far_out_got, made_across[:2]))
    far_sum, far_out, held = lax.optimization_barrier(
        (low_plus(made_far[4], far_got), low_plus(made_far[2], far_out_got), held)
    )
    back_low, back_top = side_swap(far_sum[half:]), seq_swap(far_sum[:half])
    made_beside = experts(1, 2, row_beside, up_pair_beside, held, sums_a, 15)
    beside_got, beside_out_got = core_swap(made_beside[5]), core_swap(made_beside[3])
    across_got, across_out_got, back_low, back_top, held = lax.optimization_barrier(
        (across_got, across_out_got, back_low, back_top, made_beside[:2])
    )
    across_sum, out_across, held = lax.optimization_barrier(
        (lower(low_plus(made_across[4], across_got), back_low), low_plus(made_across[2], across_out_got), held)
    )
    across_in = seq_swap(across_sum)
    made_own = experts(1, 0, row_own, up_own, held, sums_a, 15)
    hidden_b, grads_b = made_own[:2]
    own_got = core_swap(made_own[5])
    beside_got, beside_out_got, grads_b = lax.optimization_barrier((beside_got, beside_out_got, grads_b))
    beside_sum, out_beside, grads_b = lax.optimization_barrier(
        (
            upper(low_plus(made_beside[4], beside_got), back_top),
            low_plus(made_beside[2], beside_out_got),
            grads_b,
        )
    )
    beside_in = side_swap(beside_sum)
    out_low, out_top = side_swap(far_out[half:]), seq_swap(far_out[:half])

    total_b = expert_grad(row_all, grads_b, width, 3 * ff, 0, 1)
    total_b = expert_grad(up_all, hidden_b, width, 3 * ff, 2, 1, (total_b,))
    home_b = home(total_b)
    across_in, beside_in, own_got, _ = lax.optimization_barrier((across_in, beside_in, own_got, total_b))

    middle_grad, branch_grad, mixed_grad, second_gain_grad = middle_back(
        made_own[4], own_got, across_in, beside_in, middle, upstream_low, gains, project_out, query_width
    )
    second_gain_grad = second_gain_grad[0]
    chain = Chain(mixed_grad)
    own_out_got = core_swap(chain.enter(made_own[3]))
    out_top, out_low = chain.enter((out_top, out_low))
    out_across, out_beside = lower(out_across, out_low), upper(out_beside, out_top)
    out_across, out_beside = chain.leave(lax.optimization_barrier((out_across, out_beside)))
    out_across_in, out_beside_in = seq_swap(out_across), side_swap(out_beside)
    def back(pair, past, stats, first):
        return attend_back(
            chain.enter(place), query, pair, past, mixed, mixed_grad, stats, first, stats.shape[0], 24
        )

    query_a, key_a, value_a, key_past_a, value_past_a = chain.leave(back(pair_a, past_a, stats_a, 0))
    late_a = lax.ppermute(jnp.concatenate([key_past_a, value_past_a], axis=1), "seq", [(1, 0)])
    out_home = HomeSum(chain.leave(dot_tn(chain.enter(mixed), branch_grad).astype(BF)))
    out_across_in, out_beside_in, own_out_got = chain.enter((out_across_in, out_beside_in, own_out_got))
    combined = (
        made_own[2].astype(F32) + own_out_got.astype(F32) + out_across_in.astype(F32) + out_beside_in.astype(F32)
    )
    block_output = chain.leave((middle + combined[:, :width]).astype(BF))[None]
    dots = combined[:, width : width + EXPERTS] + combined[:, width + EXPERTS : width + 2 * EXPERTS]
    grad_gates = chain.leave(jnp.sum(jnp.where(chosen, chain.enter(dots)[:, None, :], 0.0), axis=-1))[None]
    out_home.got = chain.enter(out_home.got)
    chain.leave(out_home.beside())
    a_slots = slots(home_a)
    a_mine = chain.leave(exchange_end(a_slots, chain.enter(exchange_start(a_slots))))
    late_a = chain.leave(chain.enter(late_a))
    a_other = seq_swap(a_mine)
    query_b, key_b, value_b, key_past_b, value_past_b = chain.leave(
        back(pair_b, past_b, stats_b, stats_a.shape[0])
    )
    late_b = lax.ppermute(jnp.concatenate([key_past_b, value_past_b], axis=1), "seq", [(1, 0)])
    a_other = chain.enter(a_other)
    out_home.got = chain.enter(out_home.got)
    chain.leave((out_home.across(), a_other))
    query_grad = jnp.concatenate([query_a, query_b], axis=1)
    query_home = HomeSum(chain.leave(dot_tn(chain.enter(lowered_one), query_grad).astype(BF)))
    query_home.got = chain.enter(query_home.got)
    chain.leave(query_home.beside())
    late_b = chain.enter(late_b)
    pair_grad, pair_weight = chain.leave(
        pair_back(chain.enter(lowered_one), key_a, key_b, value_a, value_b, late_a, late_b)
    )
    pair_part = lax.psum_scatter(pair_weight, ROWS, scatter_dimension=0, tiled=True)
    query_home.got = chain.enter(query_home.got)
    chain.leave(query_home.across())
    b_slots = slots(chain.enter(home_b))
    b_got = exchange_start(b_slots)
    projected_grad = jnp.concatenate([query_grad, pair_grad], axis=1)
    normed_grad_one = chain.leave(dot_nt(chain.enter(projected_grad), project_in[:, :qkv]))
    query_home.got = chain.enter(query_home.got)
    chain.leave(query_home.along())
    b_mine = chain.leave(exchange_end(b_slots, chain.enter(b_got)))
    normed_one, inverse_one, _ = norm_rows(inputs, gains[0])
    input_norm_grad, first_gain_grad = norm_back(chain.enter(normed_grad_one), normed_one, inverse_one, gains[0])
    grad_tokens = chain.leave(middle_grad + input_norm_grad)[None]
    b_other = seq_swap(b_mine)

    gain_grads = jnp.stack([first_gain_grad, second_gain_grad])
    gain_grads = gain_grads + core_swap(gain_grads)
    out_home.got = chain.enter(out_home.got)
    chain.leave(out_home.along())
    gain_grads = chain.leave(chain.enter(gain_grads))
    gain_grads = gain_grads + side_swap(gain_grads)
    query_home.got = chain.enter(query_home.got)
    chain.leave(query_home.final())
    gain_grads = chain.leave(chain.enter(gain_grads)).reshape(2, outer_count, inner_count * shard)
    gain_sum = pick(gain_grads, outer_at, 1)
    for step in range(1, outer_count):
        piece = pick(gain_grads, lax.rem(outer_at + step, outer_count), 1)
        gain_sum = gain_sum + lax.ppermute(
            piece, "outer", [(i, (i + step) % outer_count) for i in range(outer_count)]
        )
    out_home.got = chain.enter(out_home.got)
    chain.leave(out_home.final())
    gain_sum = chain.leave(pick(chain.enter(gain_sum).reshape(2, inner_count, shard), lax.axis_index("inner"), 1))
    gain_sum = gain_sum + seq_swap(gain_sum)
    pair_other = seq_swap(chain.enter(pair_part))
    parts = chain.enter((a_mine, a_other, b_mine, b_other))
    grads = [unpack_experts(seq_place, parts, kind, ff) for kind in range(3)]
    grad_gate, grad_lift, grad_down = chain.leave(lax.optimization_barrier(tuple(grads)))
    out_home.other, query_home.other = chain.enter((out_home.other, query_home.other))
    grad_out = chain.leave(out_home.result())
    pair_sum = pair_part.astype(F32) + chain.enter(pair_other).astype(F32)
    grad_in = jnp.concatenate([query_home.result(), pair_sum], axis=1)
    return (
        block_output,
        grad_tokens,
        grad_gates,
        gain_sum[0],
        grad_in,
        grad_out,
        gain_sum[1],
        grad_gate,
        grad_lift,
        grad_down,
    )


def solution(mesh):
    seq_count, fsdp_count = mesh.devices.shape
    inner_count = EXPERTS // (2 * seq_count)
    fine = jax.sharding.Mesh(
        mesh.devices.reshape(seq_count, fsdp_count // inner_count, inner_count), ("seq", "outer", "inner")
    )
    return jax.shard_map(
        body,
        mesh=fine,
        in_specs=(
            P(ROWS, "seq", None),
            P(ROWS),
            P(ROWS, "seq", None),
            P(ROWS, "seq", None),
            P(ROWS, "seq", None),
            P(ROWS),
            P(ROWS, None),
            P(ROWS, None),
            P(ROWS),
            P(ROWS, None, None),
            P(ROWS, None, None),
            P(ROWS, None, None),
        ),
        out_specs=(
            P(ROWS, "seq", None),
            P(ROWS, "seq", None),
            P(ROWS, "seq", None),
            P(ROWS),
            P(ROWS, None),
            P(ROWS, None),
            P(ROWS),
            P(ROWS, None, None),
            P(ROWS, None, None),
            P(ROWS, None, None),
        ),
        check_vma=False,
    )
```
